128 devices in a mesh: ty: 8 (over x_lo, y), tx: 16 (over z, x_hi, core).
Axes of the slice: x: 4 (x_hi: 2, x_lo: 2; x = x_hi * 2 + x_lo), y: 4, z: 4, core: 2. Of those that a mesh axis runs over, the one named last changes fastest.
Arguments:
- fields: float32 [8, 2, 2048, 4096], P(None, None, 'ty', 'tx'), may hold values from -6 to 6
- ocean_mask: int32 [2048, 4096], P('ty', 'tx'), may hold values 0 or 1
- diffusivity: float32 [8], replicated, may hold values from 0.02 to 0.2
- patch_slot_assignment: int32 [8, 16, 32], P('ty', 'tx'), may hold values from 0 to 31, each once within a row
- conv_in: bfloat16 [3, 3, 8, 128], replicated, may hold values from -0.75 to 0.75
- conv_mid: bfloat16 [3, 3, 128, 128], replicated, may hold values from -0.1875 to 0.1875
- conv_out: bfloat16 [3, 3, 128, 2], replicated, may hold values from -0.1875 to 0.1875
Outputs:
- new_fields: float32 [8, 2, 2048, 4096], P(None, None, 'ty', 'tx')
- member_loss: float32 [8, 16], P('ty', 'tx')
- step_in: float32 [3, 3, 8, 128], replicated
- step_mid: float32 [3, 3, 128, 128], replicated
- step_out: float32 [3, 3, 128, 2], replicated
The draws below stay inside these ranges and needn't reach their ends.
Inputs may be any that keep to these rules, and one draw needn't show every extreme that they name: `patch_slot_assignment`: each row of 32 numbers names every patch slot once.
All inputs are finite; a program needn't handle non-finite values. No bound on the sum of `ocean_mask` on one device may be relied on, other than what follows from the above.
Results may differ from the reference program's by a relative error of at most 0.0022.
Values may be sent and summed in bfloat16 or wider, within the bound.
A program may use at most 192 MiB of HBM per device.

```python
import math
import jax
import jax.numpy as jnp
from jax import lax

FIELDS = 8
CH = 128
PS = 16
NSTEP = 3
LEV = 2
NPATCH = 32
NY = 2048
NX = 4096
N_TY = 8
N_TX = 16


def place_ends(entries, own_key, least, high):
    index_at = [jax.random.randint(jax.random.fold_in(own_key, axis), (), 0, length) for axis, length in enumerate(entries.shape)]
    longest = entries.shape.index(max(entries.shape))
    neighbour = index_at[:longest] + [(index_at[longest] + 1) % entries.shape[longest]] + index_at[longest + 1:]
    return entries.at[tuple(index_at)].set(least).at[tuple(neighbour)].set(high)


def block_levels(rng, dims, cuts, least, largest):
    def one(dim, shards_of):
        steps = jax.random.uniform(jax.random.fold_in(jax.random.fold_in(rng, 6), dim), (shards_of,), jnp.float32, least / len(cuts), largest / len(cuts))
        return jnp.repeat(jnp.exp(steps), dims[dim] // shards_of).reshape((-1,) + (1,) * (len(dims) - dim - 1))

    gain = one(*cuts[0])
    for cut in cuts[1:]:
        gain = gain * one(*cut)
    return gain


def noise(stream_key, shape, scale, most, pieces=(), held_as=jnp.bfloat16):
    loudness = block_levels(stream_key, shape, pieces, -0.22, 0.18) if pieces else 1.0
    result = jax.random.normal(stream_key, shape, jnp.float32) * scale * loudness
    return jnp.minimum(jnp.maximum(result, -most), most).astype(held_as)


def setup_inputs(seed: int = 0) -> dict:
    seeds = jax.random.split(jax.random.key(seed), 8)
    return {
        "fields": noise(seeds[0], (FIELDS, LEV, NY, NX), 1.0, 6.0, ((2, 8), (3, 16)), jnp.float32),
        "ocean_mask": place_ends((jax.random.randint(seeds[1], (NY, NX), 0, 5) < 4).astype(jnp.int32), jax.random.fold_in(seeds[1], 1), 0, 1),
        "diffusivity": jnp.clip(jnp.exp(jax.random.uniform(seeds[2], (FIELDS,), jnp.float32, math.log(0.02), math.log(0.2))), 0.02, 0.2),
        "patch_slot_assignment": jax.vmap(lambda own: jax.random.permutation(own, NPATCH))(jax.random.split(seeds[3], N_TY * N_TX)).reshape((N_TY, N_TX, NPATCH)).astype(jnp.int32),
        "conv_in": noise(seeds[4], (3, 3, FIELDS, CH), (9 * FIELDS) ** -0.5, 0.75),
        "conv_mid": noise(seeds[5], (3, 3, CH, CH), (9 * CH) ** -0.5, 0.1875),
        "conv_out": noise(seeds[6], (3, 3, CH, 2), (9 * CH) ** -0.5, 0.1875),
    }


advect_rate = 0.1
norm_eps = 1e-06

def advance(padded, wet_cells, diffusivity):
    centre = padded[:, :, 1:-1, 1:-1]
    row_above = padded[:, :, :-2, 1:-1]
    row_below = padded[:, :, 2:, 1:-1]
    col_left = padded[:, :, 1:-1, :-2]
    col_right = padded[:, :, 1:-1, 2:]
    laplacian = row_above + row_below + col_left + col_right - 4.0 * centre
    advection = centre[0] * (col_right - col_left) * 0.5 + centre[1] * (row_below - row_above) * 0.5
    return wet_cells * (centre + diffusivity[:, None, None, None] * laplacian - advect_rate * advection)

def coarse(values):
    shape = values.shape[:-2] + (values.shape[-2] // 4, 4, values.shape[-1] // 4, 4)
    return values.reshape(shape).mean(axis=(-3, -1))

def coarse_parts(current, wet_cells):
    means = coarse(current)
    flux_east = coarse(current[0] * current[2]) - means[0] * means[2]
    flux_north = coarse(current[1] * current[3]) - means[1] * means[3]
    ocean_cell_fraction = coarse(jnp.broadcast_to(wet_cells, current[0].shape))
    labels = jnp.stack([flux_east, flux_north, ocean_cell_fraction]).astype(jnp.bfloat16)
    return (means.astype(jnp.bfloat16), labels)

def patchify(values, tile_rows, tile_cols):
    depth, levels = (values.shape[0], values.shape[1])
    rows_in = values.shape[2] // (tile_rows * PS)
    cols_in = values.shape[3] // (tile_cols * PS)
    split = values.reshape(depth, levels, tile_rows, rows_in, PS, tile_cols, cols_in, PS)
    split = split.transpose(2, 5, 1, 3, 6, 0, 4, 7)
    return split.reshape(tile_rows, tile_cols, levels * rows_in * cols_in, depth, PS * PS)

def apply_stencil(inputs, kernel):
    height, width = (inputs.shape[1], inputs.shape[2])
    padded = jnp.pad(inputs, ((0, 0), (1, 1), (1, 1), (0, 0)))
    summed = jnp.zeros(inputs.shape[:3] + (kernel.shape[3],), jnp.float32)
    for i in range(3):
        for j in range(3):
            summed = summed + jnp.einsum('phwc,cd->phwd', padded[:, i:i + height, j:j + width, :], kernel[i, j], preferred_element_type=jnp.float32)
    return summed

def learner_misfit(params, features, labels):
    first, middle, final_layer_output = params
    patches_here = features.shape[0]
    inputs = features.reshape(patches_here, features.shape[1], PS, PS).transpose(0, 2, 3, 1)
    hidden_one = jax.nn.silu(apply_stencil(inputs, first)).astype(jnp.bfloat16)
    second_hidden_layer = jax.nn.silu(apply_stencil(hidden_one, middle)).astype(jnp.bfloat16)
    predicted_tendency = apply_stencil(second_hidden_layer, final_layer_output)
    target_tendency = labels[:, :2].reshape(patches_here, 2, PS, PS).transpose(0, 2, 3, 1).astype(jnp.float32)
    ocean_cell_fraction = labels[:, 2].reshape(patches_here, PS, PS, 1).astype(jnp.float32)
    return jnp.sum(ocean_cell_fraction * (predicted_tendency - target_tendency) ** 2)

def learner_grads(first, middle, final_layer_output, features, labels):

    def objective(params):
        return learner_misfit(params, features, labels)
    misfit, backward = jax.vjp(objective, (first, middle, final_layer_output))
    gradients = backward(jnp.ones((), jnp.float32))[0]
    return (gradients, misfit)

def normalized(gradient):
    return gradient * lax.rsqrt(jnp.mean(gradient * gradient) + norm_eps)

def reference(fields, ocean_mask, diffusivity, patch_slot_assignment, conv_in, conv_mid, conv_out):
    wet_cells = ocean_mask.astype(jnp.float32)
    current = fields
    for sweep in range(NSTEP):
        padded = jnp.pad(current, ((0, 0), (0, 0), (1, 1), (1, 1)))
        current = advance(padded, wet_cells, diffusivity)
    means, labels = coarse_parts(current, wet_cells)
    own_means = patchify(means, N_TY, N_TX)
    own_labels = patchify(labels, N_TY, N_TX)
    slots = patch_slot_assignment.astype(jnp.int32)[:, :, :, None, None]
    own_means = jnp.take_along_axis(own_means, slots, axis=2)
    own_labels = jnp.take_along_axis(own_labels, slots, axis=2)
    group = NPATCH // N_TY

    def regroup(values):
        depth = values.shape[3]
        values = values.reshape(N_TY, N_TX, N_TY, group, depth, PS * PS)
        values = values.transpose(2, 1, 0, 3, 4, 5)
        return values.reshape(N_TY * N_TX, NPATCH, depth, PS * PS)

    def single_learner_update(pair):
        return learner_grads(conv_in, conv_mid, conv_out, pair[0], pair[1])
    gradients, misfits = lax.map(single_learner_update, (regroup(own_means), regroup(own_labels)))
    grad_in = lax.optimization_barrier(jnp.sum(gradients[0].astype(jnp.float32), axis=0))
    grad_mid = lax.optimization_barrier(jnp.sum(gradients[1].astype(jnp.float32), axis=0))
    grad_out = lax.optimization_barrier(jnp.sum(gradients[2].astype(jnp.float32), axis=0))
    member_loss = misfits.reshape(N_TY, N_TX) / (NPATCH * PS * PS)
    return (current, member_loss, normalized(grad_in), normalized(grad_mid), normalized(grad_out))
```

```python
import functools

import jax
import jax.numpy as jnp
import ml_dtypes
import numpy as np
from jax import lax
from jax.experimental import pallas as pl
from jax.experimental.pallas import tpu as pltpu
from jax.sharding import PartitionSpec as P

F32 = jnp.float32
BF16 = jnp.bfloat16
MESH = pl.DeviceIdType.MESH
NTY, NTX = 8, 16
ROWS = 1280
CHUNK = ROWS // NTY
PIECE = 16
OWNERS = CHUNK // PIECE
GROUP = 4
TAPS = [(i - 1, j - 1) for i in range(3) for j in range(3)]
NORM_EPS = 1e-6
ANY = pl.BlockSpec(memory_space=pl.ANY)
VMEM = pl.BlockSpec(memory_space=pltpu.VMEM)
SMEM = pl.BlockSpec(memory_space=pltpu.SMEM)


def lanes(shape):
    return lax.broadcasted_iota(jnp.int32, shape, len(shape) - 1)


def pack_edges(field, lane):
    packed = None
    for i in range(16):
        first, last = field(i)
        edge = pltpu.roll(jnp.where(lane >= 124, last, first), (8 * i + 4) % 128, 1)
        packed = edge if packed is None else jnp.where(lane >= 8 * i, edge, packed)
    return packed


def halo_kernel(fields, mask, top, bot, mtop, mbot, left, right, tile, packed, in_sem, send, recv):
    my, mx = lax.axis_index("ty"), lax.axis_index("tx")
    has = {-1: my > 0, 1: my < NTY - 1}
    has_x = {-1: mx > 0, 1: mx < NTX - 1}
    loads = []
    for i in range(4):
        cut = pl.ds(4 * i, 4)
        loads.append(pltpu.make_async_copy(fields.at[cut], tile.at[cut], in_sem.at[i]))
        loads[-1].start()

    def both(a, b):
        return jnp.logical_and(a, b)

    barrier = pltpu.get_barrier_semaphore()
    steps = [(a, b) for a in (-1, 0, 1) for b in (-1, 0, 1) if (a, b) != (0, 0)]

    def present(a, b):
        if a == 0:
            return has_x[b]
        if b == 0:
            return has[a]
        return both(has[a], has_x[b])

    count = jnp.int32(0)
    for a, b in steps:
        here = present(a, b)
        count = count + here.astype(jnp.int32)

        @pl.when(here)
        def _(a=a, b=b):
            pl.semaphore_signal(
                barrier, inc=1, device_id={"ty": my + a, "tx": mx + b}, device_id_type=MESH
            )

    @pl.when(my == 0)
    def _():
        top[...] = jnp.zeros_like(top)
        mtop[...] = jnp.zeros_like(mtop)
        left[0:8, :] = jnp.zeros((8, 128), F32)
        right[0:8, :] = jnp.zeros((8, 128), F32)

    @pl.when(my == NTY - 1)
    def _():
        bot[...] = jnp.zeros_like(bot)
        mbot[...] = jnp.zeros_like(mbot)
        left[264:272, :] = jnp.zeros((8, 128), F32)
        right[264:272, :] = jnp.zeros((8, 128), F32)

    @pl.when(mx == 0)
    def _():
        left[...] = jnp.zeros_like(left)

    @pl.when(mx == NTX - 1)
    def _():
        right[...] = jnp.zeros_like(right)

    pl.semaphore_wait(barrier, count)

    def copy(src, dst, index, a, b):
        return pltpu.make_async_remote_copy(
            src_ref=src,
            dst_ref=dst,
            send_sem=send.at[index],
            recv_sem=recv.at[index],
            device_id={"ty": my + a, "tx": mx + b},
            device_id_type=MESH,
        )

    row_copies = [
        (fields.at[:, pl.ds(248, 8), :], top, 1, 0),
        (mask.at[pl.ds(248, 8), :], mtop, 1, 0),
        (fields.at[:, pl.ds(0, 8), :], bot, -1, 0),
        (mask.at[pl.ds(0, 8), :], mbot, -1, 0),
    ]
    side_copies = [
        (packed, left.at[pl.ds(8, 256), :], 0, 1),
        (packed, right.at[pl.ds(8, 256), :], 0, -1),
        (packed.at[pl.ds(248, 8), :], left.at[pl.ds(0, 8), :], 1, 1),
        (packed.at[pl.ds(0, 8), :], left.at[pl.ds(264, 8), :], -1, 1),
        (packed.at[pl.ds(248, 8), :], right.at[pl.ds(0, 8), :], 1, -1),
        (packed.at[pl.ds(0, 8), :], right.at[pl.ds(264, 8), :], -1, -1),
    ]
    every = row_copies + side_copies

    for index, (src, dst, a, b) in enumerate(row_copies):

        @pl.when(present(a, b))
        def _(index=index, src=src, dst=dst, a=a, b=b):
            copy(src, dst, index, a, b).start()

    for load in loads:
        load.wait()

    def pack(block, _):
        row = pl.multiple_of(block * 16, 16)
        at = pl.ds(row, 16)
        lane = lanes((16, 128))
        edges = pack_edges(lambda i: (tile[i, at, 0:128], tile[i, at, 128:256]), lane)
        wet0 = mask[at, 0:128].astype(F32)
        wet1 = mask[at, 128:256].astype(F32)
        edges = jnp.where(lane == 0, pltpu.roll(wet1, 2, 1), edges)
        edges = jnp.where(lane == 8, pltpu.roll(wet1, 9, 1), edges)
        edges = jnp.where(lane == 7, pltpu.roll(wet0, 7, 1), edges)
        edges = jnp.where(lane == 15, pltpu.roll(wet0, 14, 1), edges)
        packed[at, :] = edges
        return 0

    lax.fori_loop(0, 16, pack, 0)

    for index, (src, dst, a, b) in enumerate(side_copies):

        @pl.when(present(a, b))
        def _(index=index + 4, src=src, dst=dst, a=a, b=b):
            copy(src, dst, index, a, b).start()

    for index, (src, dst, a, b) in enumerate(every):

        @pl.when(present(-a, -b))
        def _(index=index, src=src, dst=dst, a=a, b=b):
            copy(src, dst, index, a, b).wait_recv()

    for index, (src, dst, a, b) in enumerate(every):

        @pl.when(present(a, b))
        def _(index=index, src=src, dst=dst, a=a, b=b):
            copy(src, dst, index, a, b).wait_send()


def exchange_halo(fields, mask):
    return pl.pallas_call(
        halo_kernel,
        out_shape=(
            jax.ShapeDtypeStruct((16, 8, 256), F32),
            jax.ShapeDtypeStruct((16, 8, 256), F32),
            jax.ShapeDtypeStruct((8, 256), jnp.int32),
            jax.ShapeDtypeStruct((8, 256), jnp.int32),
            jax.ShapeDtypeStruct((272, 128), F32),
            jax.ShapeDtypeStruct((272, 128), F32),
        ),
        in_specs=[ANY, VMEM],
        out_specs=(VMEM,) * 6,
        scratch_shapes=[
            pltpu.VMEM((16, 256, 256), F32),
            pltpu.VMEM((256, 128), F32),
            pltpu.SemaphoreType.DMA((4,)),
            pltpu.SemaphoreType.DMA((10,)),
            pltpu.SemaphoreType.DMA((10,)),
        ],
        compiler_params=pltpu.CompilerParams(
            collective_id=0, has_side_effects=True, vmem_limit_bytes=24 << 20
        ),
        name="halo",
    )(fields, mask)


def coarse_matrix():
    matrix = np.zeros((8, 128, 2, 8, 16), np.float32)
    for row in range(8):
        for column in range(128):
            matrix[row, column, column // 64, row, (column % 64) // 4] = 1 / 16
    return matrix.reshape(1024, 256).astype(ml_dtypes.bfloat16)


def ocean_kernel(
    rate, slot, fields, mask, top, bot, mtop, mbot, left, right, gather,
    out, chosen,
    now, later, final, wet, sl0, sl1, sr0, sr1, wl, wr, sums, wide, patches, in_sem, out_sem,
):
    loads = []
    for half in range(2):
        side = pl.ds(128 * half, 128)
        for j, (src, start, rows) in enumerate(((fields, 16, 256), (top, 8, 8), (bot, 272, 8))):
            dst = now.at[half, :, pl.ds(start, rows), :]
            loads.append(pltpu.make_async_copy(src.at[:, :, side], dst, in_sem.at[3 * half + j]))
    for load in loads:
        load.start()
    for half in range(2):
        side = pl.ds(128 * half, 128)
        wet[half, 8:16, :] = mtop[:, side].astype(F32)
        wet[half, 16:272, :] = mask[:, side].astype(F32)
        wet[half, 272:280, :] = mbot[:, side].astype(F32)
    for buf in (sl0, sr0, sl1, sr1):
        buf[0:8, :] = jnp.zeros((8, 128), F32)
        buf[280:288, :] = jnp.zeros((8, 128), F32)
    for buf in (now, later):
        buf[:, :, 0:8, :] = jnp.zeros((2, 16, 8, 128), F32)
        buf[:, :, 280:288, :] = jnp.zeros((2, 16, 8, 128), F32)
    for load in loads:
        load.wait()

    def strips(block, _):
        row = pl.multiple_of(block * 16 + 8, 8)
        at = pl.ds(row, 16)
        got = pl.ds(pl.multiple_of(block * 16, 16), 16)
        lane = lanes((16, 128))
        own = pack_edges(lambda i: (now[0, i, at, :], now[1, i, at, :]), lane)
        west, east = left[got, :], right[got, :]
        inner = (lane & 7) < 4
        sl0[at, :] = jnp.where(inner, west, own)
        sr0[at, :] = jnp.where(inner, own, east)
        wet0, wet1 = wet[0, at, :], wet[1, at, :]
        low = jnp.where((lane >= 4) & (lane < 8), pltpu.roll(wet0, 4, 1), 0.0)
        low = jnp.where(lane == 2, pltpu.roll(west, 2, 1), low)
        low = jnp.where(lane == 3, pltpu.roll(west, 123, 1), low)
        high = jnp.where(lane < 4, pltpu.roll(wet1, 4, 1), 0.0)
        high = jnp.where(lane == 4, pltpu.roll(east, 125, 1), high)
        high = jnp.where(lane == 5, pltpu.roll(east, 118, 1), high)
        for shift in (8, 16, 32, 64):
            low = low + pltpu.roll(low, shift, 1)
            high = high + pltpu.roll(high, shift, 1)
        wl[at, :] = low
        wr[at, :] = high
        return 0

    lax.fori_loop(0, 17, strips, 0)

    def advance_strip(src, dst, cells):
        def body(block, _):
            row = pl.multiple_of(block * 16 + 8, 8)
            at = pl.ds(row, 16)
            lane = lanes((16, 128))
            level = jnp.zeros((16, 128), F32)
            for k in range(8):
                level = jnp.where(lane >> 4 == k, rate[k], level)
            c = src[at, :]
            big = src[pl.ds(row - 8, 32), :]
            n, s = big[7:23], big[9:25]
            e, w = pltpu.roll(c, 127, 1), pltpu.roll(c, 1, 1)
            u = jnp.where(lane < 16, c, 0.0)
            v = jnp.where((lane >= 16) & (lane < 32), c, 0.0)
            for shift in (16, 32, 64):
                u = u + pltpu.roll(u, shift, 1)
                v = v + pltpu.roll(v, shift, 1)
            lap = (e + w) + (n + s) - 4.0 * c
            adv = u * (e - w) + v * (s - n)
            dst[at, :] = cells[at, :] * (c + level * lap - 0.05 * adv)
            return 0

        lax.fori_loop(0, 17, body, 0)

    def advance(src, dst, low, high, lead, blocks, shift):
        def body(k, _):
            diff = rate[k]
            for block in range(blocks):
                row = lead + 16 * block
                at = pl.ds(row, 16)
                lane = lanes((16, 128))
                strip_l, strip_r = low[at, :], high[at, :]
                for lev in range(2):
                    i = 2 * k + lev
                    x0, x1 = src[0, i, at, :], src[1, i, at, :]
                    into_l = pltpu.roll(strip_l, 125 - 8 * i, 1)
                    into_r = pltpu.roll(strip_r, 123 - 8 * i, 1)
                    r0, r1 = pltpu.roll(x0, 1, 1), pltpu.roll(x1, 1, 1)
                    l0, l1 = pltpu.roll(x0, 127, 1), pltpu.roll(x1, 127, 1)
                    w = (jnp.where(lane == 0, into_l, r0), jnp.where(lane == 0, r0, r1))
                    e = (jnp.where(lane == 127, l1, l0), jnp.where(lane == 127, into_r, l1))
                    for half in range(2):
                        c = (x0, x1)[half]
                        n = src[half, i, pl.ds(row - 1, 16), :]
                        s = src[half, i, pl.ds(row + 1, 16), :]
                        u, v = src[half, lev, at, :], src[half, 2 + lev, at, :]
                        lap = (e[half] + w[half]) + (n + s) - 4.0 * c
                        adv = u * (e[half] - w[half]) + v * (s - n)
                        new = wet[half, at, :] * (c + diff * lap - 0.05 * adv)
                        dst[half, i, pl.ds(row - shift, 16), :] = new
            return 0

        return body

    lax.fori_loop(0, 8, advance(now, later, sl0, sr0, 8, 17, 0), 0)
    advance_strip(sl0, sl1, wl)
    advance_strip(sr0, sr1, wr)
    lax.fori_loop(0, 8, advance(later, now, sl1, sr1, 8, 17, 0), 0)
    advance_strip(sl1, sl0, wl)
    advance_strip(sr1, sr0, wr)
    last = advance(now, final, sl0, sr0, 16, 16, 16)

    def every_fourth(half, i, j):
        return final[half, i, pl.ds(j, 64, stride=4), :]

    def send(k, half):
        cut = pl.ds(2 * k, 2)
        src, dst = final.at[half, cut], out.at[cut, :, pl.ds(128 * half, 128)]
        return pltpu.make_async_copy(src, dst, out_sem.at[k, half])

    def last_step(k, _):
        last(k, 0)
        for half in range(2):
            send(k, half).start()
        for lev in range(2):
            i = 2 * k + lev
            for half in range(2):
                total = every_fourth(half, i, 0)
                for j in range(1, 4):
                    total = total + every_fourth(half, i, j)
                for pr in range(4):
                    to = pl.multiple_of(((lev * 4 + pr) * 8 + k) * 16, 16)
                    sums[half, pl.ds(to, 16), :] = total[16 * pr : 16 * pr + 16]
        return 0

    sums[:, 1024:2048, :] = jnp.zeros((2, 1024, 128), F32)
    lax.fori_loop(0, 8, last_step, 0)

    for lev in range(2):
        for half in range(2):
            for which in range(3):
                total = None
                for j in range(4):
                    if which < 2:
                        term = every_fourth(half, 2 * which + lev, j)
                        term = term * every_fourth(half, 4 + 2 * which + lev, j)
                    else:
                        term = wet[half, pl.ds(16 + j, 64, stride=4), :]
                    total = term if total is None else total + term
                for pr in range(4):
                    to = 1024 + ((lev * 4 + pr) * 8 + which) * 16
                    sums[half, to : to + 16, :] = total[16 * pr : 16 * pr + 16]

    table = gather[...]
    for half in range(2):
        for rows in range(2):
            for y in range(8):
                x = sums[half, pl.ds(8 * rows + y, 128, stride=16), :]
                a = x.astype(BF16)
                x = x - a.astype(F32)
                b = x.astype(BF16)
                c = (x - b.astype(F32)).astype(BF16)
                side = pl.ds(128 * y, 128)
                wide[0:128, side] = a
                wide[128:256, side] = b
                wide[256:384, side] = c
            r = jnp.dot(wide[...], table, preferred_element_type=F32)
            r = r[0:128] + r[128:256] + r[256:384]
            means, products = r[0:64], r[64:128]
            for q in range(8):
                m = means[8 * q : 8 * q + 8]
                p = products[8 * q : 8 * q + 8]
                sub = lax.broadcasted_iota(jnp.int32, (8, 256), 0)
                p = p - jnp.where(sub < 2, m * pltpu.roll(m, 6, 0), 0.0)
                both = jnp.concatenate([m, p], axis=0).astype(BF16)
                for pc in range(2):
                    to = pl.ds(128 * rows, 128)
                    patches[4 * q + 2 * half + pc, :, to] = both[:, 128 * pc : 128 * pc + 128]

    for j in range(32):
        chosen[j] = patches[slot[j]]

    def finish(k, _):
        for half in range(2):
            send(k, half).wait()
        return 0

    lax.fori_loop(0, 8, finish, 0)


def run_ocean(rate, slot, fields, mask, halo, gather):
    return pl.pallas_call(
        ocean_kernel,
        out_shape=(
            jax.ShapeDtypeStruct((16, 256, 256), F32),
            jax.ShapeDtypeStruct((32, 16, 256), BF16),
        ),
        in_specs=[SMEM, SMEM, ANY, VMEM, ANY, ANY, VMEM, VMEM, VMEM, VMEM, VMEM],
        out_specs=(ANY, VMEM),
        scratch_shapes=[
            pltpu.VMEM((2, 16, 288, 128), F32),
            pltpu.VMEM((2, 16, 288, 128), F32),
            pltpu.VMEM((2, 16, 256, 128), F32),
            pltpu.VMEM((2, 288, 128), F32),
        ]
        + [pltpu.VMEM((288, 128), F32)] * 6
        + [
            pltpu.VMEM((2, 2048, 128), F32),
            pltpu.VMEM((384, 1024), BF16),
            pltpu.VMEM((32, 16, 256), BF16),
            pltpu.SemaphoreType.DMA((6,)),
            pltpu.SemaphoreType.DMA((8, 2)),
        ],
        compiler_params=pltpu.CompilerParams(vmem_limit_bytes=48 << 20),
        name="ocean",
    )(rate, slot, fields, mask, *halo, gather)


def swap_kernel(mine, got, own_sem, send, recv):
    my, mx = lax.axis_index("ty"), lax.axis_index("tx")
    barrier = pltpu.get_barrier_semaphore()
    for d in range(1, NTY):
        peer = lax.rem(my + d, NTY)
        pl.semaphore_signal(barrier, inc=1, device_id={"ty": peer, "tx": mx}, device_id_type=MESH)
    own = pltpu.make_async_copy(
        mine.at[pl.ds(4 * my, 4)], got.at[pl.ds(0, 4)], own_sem
    )
    own.start()
    pl.semaphore_wait(barrier, NTY - 1)
    copies = []
    for d in range(1, NTY):
        peer = lax.rem(my + d, NTY)
        copies.append(
            pltpu.make_async_remote_copy(
                src_ref=mine.at[pl.ds(4 * peer, 4)],
                dst_ref=got.at[pl.ds(4 * d, 4)],
                send_sem=send.at[d],
                recv_sem=recv.at[d],
                device_id={"ty": peer, "tx": mx},
                device_id_type=MESH,
            )
        )
        copies[-1].start()
    own.wait()
    for copy in copies:
        copy.wait()


def swap_patches(mine):
    return pl.pallas_call(
        swap_kernel,
        out_shape=jax.ShapeDtypeStruct((32, 16, 256), BF16),
        in_specs=[VMEM],
        out_specs=VMEM,
        scratch_shapes=[
            pltpu.SemaphoreType.DMA,
            pltpu.SemaphoreType.DMA((NTY,)),
            pltpu.SemaphoreType.DMA((NTY,)),
        ],
        compiler_params=pltpu.CompilerParams(
            collective_id=1, has_side_effects=True, vmem_limit_bytes=24 << 20
        ),
        name="swap",
    )(mine)


def contract(a, b, dim_a, dim_b):
    return lax.dot_general(
        a, b, (((dim_a,), (dim_b,)), ((), ())), preferred_element_type=F32
    )


def net_kernel(got, win, wmid, wout, grads, misfit, hs, ds, wback, amid, ain, aout, amis):
    step = pl.program_id(0)
    size = GROUP * 256

    @pl.when(step == 0)
    def _():
        for ref in (hs, ds, amid, ain, aout, amis):
            ref[...] = jnp.zeros_like(ref)
        for t in range(9):
            at = pl.ds(128 * t, 128)
            wback[at, :] = wmid[at, :].astype(F32).T.astype(BF16)

    lane = lanes((8, size))
    col, row = lane & 15, (lane >> 4) & 15

    def inside(dy, dx):
        ok = None
        for value, change in ((row, dy), (col, dx)):
            if change:
                one = value >= 1 if change < 0 else value <= 14
                ok = one if ok is None else ok & one
        return ok

    def moved(a, dy, dx):
        off = 16 * dy + dx
        if off == 0:
            return a
        return jnp.where(inside(dy, dx), pltpu.roll(a, (-off) % size, 1), 0.0)

    data = [got[p].astype(F32) for p in range(GROUP)]
    x = jnp.concatenate([d[0:8] for d in data], axis=1)
    lab = jnp.concatenate([d[8:16] for d in data], axis=1)
    xcat = jnp.concatenate([moved(x, dy, dx) for dy, dx in TAPS], axis=0).astype(BF16)

    side = lax.broadcasted_iota(jnp.int32, (size, 128), 0) & 15

    def spread(ref, a, sign):
        for j, dx in enumerate((-1, 0, 1)):
            go = sign * dx
            if go == 0:
                v = a
            elif go < 0:
                v = jnp.where(side == 0, 0.0, pltpu.roll(a, 1, 0))
            else:
                v = jnp.where(side == 15, 0.0, pltpu.roll(a, size - 1, 0))
            v = v.astype(BF16)
            for i, dy in enumerate((-1, 0, 1)):
                to = pl.ds(128 * (3 * i + j), 128)
                for p in range(GROUP):
                    b = 256 * p
                    if sign * dy == 0:
                        ref[b : b + 256, to] = v[b : b + 256]
                    elif sign * dy < 0:
                        ref[b + 16 : b + 256, to] = v[b : b + 240]
                    else:
                        ref[b : b + 240, to] = v[b + 16 : b + 256]

    def silu(z):
        s = 0.5 * jnp.tanh(0.5 * z) + 0.5
        h = z * s
        return h, s + h * (1.0 - s)

    z1 = contract(xcat, win[...], 0, 0)
    h1, slope1 = silu(z1)
    spread(hs, h1, 1)
    z2 = jnp.dot(hs[...], wmid[...], preferred_element_type=F32)
    h2, slope2 = silu(z2)
    h2 = h2.astype(BF16)
    parts = contract(wout[...], h2, 1, 1)
    y = jnp.zeros((8, size), F32)
    for t, (dy, dx) in enumerate(TAPS):
        y = y + moved(parts[8 * t : 8 * t + 8], dy, dx)
    sub = lax.broadcasted_iota(jnp.int32, (8, size), 0)
    diff = jnp.where(sub < 2, y - lab, 0.0)
    weighted = lab[2:3] * diff
    amis[...] += weighted * diff
    g = 2.0 * weighted
    gcat = jnp.concatenate([moved(g, -dy, -dx) for dy, dx in TAPS], axis=0).astype(BF16)
    aout[...] += jnp.dot(gcat, h2, preferred_element_type=F32)
    dh2 = contract(gcat, wout[...], 0, 0).astype(BF16).astype(F32)
    dz2 = dh2 * slope2
    spread(ds, dz2, -1)
    amid[...] += contract(h1.astype(BF16), ds[...], 0, 0)
    dh1 = jnp.dot(ds[...], wback[...], preferred_element_type=F32).astype(BF16).astype(F32)
    dz1 = (dh1 * slope1).astype(BF16)
    ain[...] += jnp.dot(xcat, dz1, preferred_element_type=F32)

    @pl.when(step == pl.num_programs(0) - 1)
    def _():
        for t in range(9):
            at = pl.ds(128 * t, 128)
            grads[at, :] = amid[:, at].astype(BF16)
        both = jnp.concatenate(
            [ain[...]] + [aout[8 * t : 8 * t + 2, :] for t in range(9)] + [jnp.zeros((38, 128), F32)],
            axis=0,
        )
        grads[1152:1280, :] = both.astype(BF16)
        misfit[...] = jnp.full((8, 128), jnp.sum(amis[...]), F32)


def run_net(got, win, wmid, wout):
    whole = lambda i: (0, 0)
    return pl.pallas_call(
        net_kernel,
        grid=(32 // GROUP,),
        out_shape=(
            jax.ShapeDtypeStruct((ROWS, 128), BF16),
            jax.ShapeDtypeStruct((8, 128), F32),
        ),
        in_specs=[
            pl.BlockSpec((GROUP, 16, 256), lambda i: (i, 0, 0)),
            pl.BlockSpec((72, 128), whole),
            pl.BlockSpec((1152, 128), whole),
            pl.BlockSpec((72, 128), whole),
        ],
        out_specs=(pl.BlockSpec((ROWS, 128), whole), pl.BlockSpec((8, 128), whole)),
        scratch_shapes=[
            pltpu.VMEM((GROUP * 256, 1152), BF16),
            pltpu.VMEM((GROUP * 256, 1152), BF16),
            pltpu.VMEM((1152, 128), BF16),
            pltpu.VMEM((128, 1152), F32),
            pltpu.VMEM((72, 128), F32),
            pltpu.VMEM((72, 128), F32),
            pltpu.VMEM((8, GROUP * 256), F32),
        ],
        compiler_params=pltpu.CompilerParams(vmem_limit_bytes=48 << 20),
        name="net",
    )(got, win, wmid, wout)


def total_kernel(
    grads, mid, first, last, got1, part, got2, whole, s1, r1, s2, r2, s3, r3, s4, r4
):
    my, mx = lax.axis_index("ty"), lax.axis_index("tx")
    barrier = pltpu.get_barrier_semaphore()
    for d in range(1, NTY):
        to = {"ty": lax.rem(my + d, NTY), "tx": mx}
        pl.semaphore_signal(barrier, inc=1, device_id=to, device_id_type=MESH)
    for d in range(1, NTX):
        to = {"ty": my, "tx": lax.rem(mx + d, NTX)}
        pl.semaphore_signal(barrier, inc=1, device_id=to, device_id_type=MESH)
    pl.semaphore_wait(barrier, NTY + NTX - 2)

    def copy(src, dst, send, recv, to):
        return pltpu.make_async_remote_copy(
            src_ref=src, dst_ref=dst, send_sem=send, recv_sem=recv, device_id=to, device_id_type=MESH
        )

    def one(d):
        peer = lax.rem(my + d, NTY)
        src = grads.at[pl.ds(pl.multiple_of(CHUNK * peer, 16), CHUNK), :]
        return copy(src, got1.at[d], s1.at[d], r1.at[d], {"ty": peer, "tx": mx})

    for d in range(1, NTY):
        one(d).start()
    part[...] = grads[pl.ds(pl.multiple_of(CHUNK * my, 16), CHUNK), :].astype(F32)
    for d in range(1, NTY):
        one(d).wait_recv()
        part[...] += got1[d].astype(F32)

    def two(d):
        peer = lax.rem(mx + d, NTX)
        src = part.at[pl.ds(pl.multiple_of(PIECE * peer, 8), PIECE), :]
        return copy(src, got2.at[d], s2.at[d], r2.at[d], {"ty": my, "tx": peer})

    def owns(device):
        return device < OWNERS

    for d in range(1, NTX):

        @pl.when(owns(lax.rem(mx + d, NTX)))
        def _(d=d):
            two(d).start()

    base = CHUNK * my

    def three(d, source, peer):
        place = whole.at[pl.ds(pl.multiple_of(base + PIECE * source, 8), PIECE), :]
        return copy(place, place, s3.at[d], r3.at[d], {"ty": my, "tx": peer})

    @pl.when(owns(mx))
    def _():
        at = pl.multiple_of(PIECE * mx, 8)
        total = part[pl.ds(at, PIECE), :]
        for d in range(1, NTX):
            peer = lax.rem(mx + d, NTX)
            copy(
                part.at[pl.ds(0, PIECE), :], got2.at[d], s2.at[d], r2.at[d], {"ty": my, "tx": peer}
            ).wait_recv()
            total = total + got2[d]
        whole[pl.ds(pl.multiple_of(base + PIECE * mx, 8), PIECE), :] = total
        for d in range(1, NTX):
            three(d, mx, lax.rem(mx + d, NTX)).start()

    for d in range(1, NTX):
        source = lax.rem(mx + NTX - d, NTX)

        @pl.when(owns(source))
        def _(d=d, source=source):
            three(d, source, source).wait_recv()

    def four(d, source, peer):
        place = whole.at[pl.ds(pl.multiple_of(CHUNK * source, 8), CHUNK), :]
        return copy(place, place, s4.at[d], r4.at[d], {"ty": peer, "tx": mx})

    for d in range(1, NTY):
        four(d, my, lax.rem(my + d, NTY)).start()
    for d in range(1, NTY):
        source = lax.rem(my + NTY - d, NTY)
        four(d, source, source).wait_recv()

    for ref, start, rows in ((mid, 0, 1152), (first, 1152, 72), (last, 1224, 18)):
        g = whole[start : start + rows, :]
        ref[...] = g * lax.rsqrt(jnp.sum(g * g) / F32(rows * 128) + NORM_EPS)

    for d in range(1, NTY):
        one(d).wait_send()
        four(d, my, lax.rem(my + d, NTY)).wait_send()
    for d in range(1, NTX):

        @pl.when(owns(lax.rem(mx + d, NTX)))
        def _(d=d):
            two(d).wait_send()

        @pl.when(owns(mx))
        def _(d=d):
            three(d, mx, lax.rem(mx + d, NTX)).wait_send()


def add_up(grads):
    dma = pltpu.SemaphoreType.DMA
    return pl.pallas_call(
        total_kernel,
        out_shape=(
            jax.ShapeDtypeStruct((1152, 128), F32),
            jax.ShapeDtypeStruct((72, 128), F32),
            jax.ShapeDtypeStruct((18, 128), F32),
        ),
        in_specs=[VMEM],
        out_specs=(VMEM,) * 3,
        scratch_shapes=[
            pltpu.VMEM((NTY, CHUNK, 128), BF16),
            pltpu.VMEM((CHUNK, 128), F32),
            pltpu.VMEM((NTX, PIECE, 128), F32),
            pltpu.VMEM((ROWS, 128), F32),
        ]
        + [dma((NTY,)), dma((NTY,)), dma((NTX,)), dma((NTX,)), dma((NTX,)), dma((NTX,)), dma((NTY,)), dma((NTY,))],
        compiler_params=pltpu.CompilerParams(
            collective_id=2, has_side_effects=True, vmem_limit_bytes=24 << 20
        ),
        name="total",
    )(grads)


def per_device(fields, ocean_mask, diffusivity, patch_slot_assignment, conv_in, conv_mid, conv_out):
    state = fields.reshape(16, 256, 256)
    halo = exchange_halo(state, ocean_mask)
    gather = jnp.asarray(coarse_matrix())
    current, mine = run_ocean(
        diffusivity, patch_slot_assignment.reshape(32), state, ocean_mask, halo, gather
    )
    got = swap_patches(mine)
    win = conv_in.reshape(72, 128)
    wmid = conv_mid.reshape(1152, 128)
    wout = jnp.pad(conv_out.reshape(9, 128, 2).transpose(0, 2, 1), ((0, 0), (0, 6), (0, 0)))
    grads, misfit = run_net(got, win, wmid, wout.reshape(72, 128))
    mid, first, last = add_up(grads)
    member_loss = misfit[0:1, 0:1] / 8192
    return (
        current.reshape(fields.shape),
        member_loss,
        first.reshape(conv_in.shape),
        mid.reshape(conv_mid.shape),
        last.reshape(9, 2, 128).transpose(0, 2, 1).reshape(conv_out.shape),
    )


def solution(mesh):
    placed = (P(None, None, "ty", "tx"), P("ty", "tx"), P(), P("ty", "tx", None), P(), P(), P())
    return jax.shard_map(
        per_device,
        mesh=mesh,
        in_specs=placed,
        out_specs=(P(None, None, "ty", "tx"), P("ty", "tx"), P(), P(), P()),
        check_vma=False,
    )
```

```python
import functools

import jax
import jax.numpy as jnp
import ml_dtypes
import numpy as np
from jax import lax
from jax.experimental import pallas as pl
from jax.experimental.pallas import tpu as pltpu
from jax.sharding import PartitionSpec as P

F32 = jnp.float32
BF16 = jnp.bfloat16
MESH = pl.DeviceIdType.MESH
NTY, NTX = 8, 16
ROWS = 1280
CHUNK = ROWS // NTY
PIECE = 16
OWNERS = CHUNK // PIECE
GROUP = 4
TEAMS = 2
TAPS = [(i - 1, j - 1) for i in range(3) for j in range(3)]
NORM_EPS = 1e-6
ANY = pl.BlockSpec(memory_space=pl.ANY)
VMEM = pl.BlockSpec(memory_space=pltpu.VMEM)
SMEM = pl.BlockSpec(memory_space=pltpu.SMEM)


def lanes(shape):
    return lax.broadcasted_iota(jnp.int32, shape, len(shape) - 1)


def pack_edges(field, lane):
    packed = None
    for i in range(16):
        first, last = field(i)
        edge = pltpu.roll(jnp.where(lane >= 124, last, first), (8 * i + 4) % 128, 1)
        packed = edge if packed is None else jnp.where(lane >= 8 * i, edge, packed)
    return packed


def halo_kernel(fields, mask, top, bot, mtop, mbot, left, right, tile, packed, in_sem, send, recv):
    my, mx = lax.axis_index("ty"), lax.axis_index("tx")
    has = {-1: my > 0, 1: my < NTY - 1}
    has_x = {-1: mx > 0, 1: mx < NTX - 1}
    loads = []
    for i in range(4):
        cut = pl.ds(4 * i, 4)
        loads.append(pltpu.make_async_copy(fields.at[cut], tile.at[cut], in_sem.at[i]))
        loads[-1].start()

    def both(a, b):
        return jnp.logical_and(a, b)

    barrier = pltpu.get_barrier_semaphore()
    steps = [(a, b) for a in (-1, 0, 1) for b in (-1, 0, 1) if (a, b) != (0, 0)]

    def present(a, b):
        if a == 0:
            return has_x[b]
        if b == 0:
            return has[a]
        return both(has[a], has_x[b])

    count = jnp.int32(0)
    for a, b in steps:
        here = present(a, b)
        count = count + here.astype(jnp.int32)

        @pl.when(here)
        def _(a=a, b=b):
            pl.semaphore_signal(
                barrier, inc=1, device_id={"ty": my + a, "tx": mx + b}, device_id_type=MESH
            )

    @pl.when(my == 0)
    def _():
        top[...] = jnp.zeros_like(top)
        mtop[...] = jnp.zeros_like(mtop)
        left[0:8, :] = jnp.zeros((8, 128), F32)
        right[0:8, :] = jnp.zeros((8, 128), F32)

    @pl.when(my == NTY - 1)
    def _():
        bot[...] = jnp.zeros_like(bot)
        mbot[...] = jnp.zeros_like(mbot)
        left[264:272, :] = jnp.zeros((8, 128), F32)
        right[264:272, :] = jnp.zeros((8, 128), F32)

    @pl.when(mx == 0)
    def _():
        left[...] = jnp.zeros_like(left)

    @pl.when(mx == NTX - 1)
    def _():
        right[...] = jnp.zeros_like(right)

    pl.semaphore_wait(barrier, count)

    def copy(src, dst, index, a, b):
        return pltpu.make_async_remote_copy(
            src_ref=src,
            dst_ref=dst,
            send_sem=send.at[index],
            recv_sem=recv.at[index],
            device_id={"ty": my + a, "tx": mx + b},
            device_id_type=MESH,
        )

    row_copies = [
        (fields.at[:, pl.ds(248, 8), :], top, 1, 0),
        (mask.at[pl.ds(248, 8), :], mtop, 1, 0),
        (fields.at[:, pl.ds(0, 8), :], bot, -1, 0),
        (mask.at[pl.ds(0, 8), :], mbot, -1, 0),
    ]
    side_copies = [
        (packed, left.at[pl.ds(8, 256), :], 0, 1),
        (packed, right.at[pl.ds(8, 256), :], 0, -1),
        (packed.at[pl.ds(248, 8), :], left.at[pl.ds(0, 8), :], 1, 1),
        (packed.at[pl.ds(0, 8), :], left.at[pl.ds(264, 8), :], -1, 1),
        (packed.at[pl.ds(248, 8), :], right.at[pl.ds(0, 8), :], 1, -1),
        (packed.at[pl.ds(0, 8), :], right.at[pl.ds(264, 8), :], -1, -1),
    ]
    every = row_copies + side_copies

    for index, (src, dst, a, b) in enumerate(row_copies):

        @pl.when(present(a, b))
        def _(index=index, src=src, dst=dst, a=a, b=b):
            copy(src, dst, index, a, b).start()

    for load in loads:
        load.wait()

    lane = lanes((128, 128))
    for block in range(2):
        at = pl.ds(128 * block, 128)
        edges = pack_edges(lambda i: (tile[i, at, 0:128], tile[i, at, 128:256]), lane)
        wet0 = mask[at, 0:128].astype(F32)
        wet1 = mask[at, 128:256].astype(F32)
        edges = jnp.where(lane == 0, pltpu.roll(wet1, 2, 1), edges)
        edges = jnp.where(lane == 8, pltpu.roll(wet1, 9, 1), edges)
        edges = jnp.where(lane == 7, pltpu.roll(wet0, 7, 1), edges)
        edges = jnp.where(lane == 15, pltpu.roll(wet0, 14, 1), edges)
        packed[at, :] = edges

    for index, (src, dst, a, b) in enumerate(side_copies):

        @pl.when(present(a, b))
        def _(index=index + 4, src=src, dst=dst, a=a, b=b):
            copy(src, dst, index, a, b).start()

    for index, (src, dst, a, b) in enumerate(every):

        @pl.when(present(-a, -b))
        def _(index=index, src=src, dst=dst, a=a, b=b):
            copy(src, dst, index, a, b).wait_recv()

    for index, (src, dst, a, b) in enumerate(every):

        @pl.when(present(a, b))
        def _(index=index, src=src, dst=dst, a=a, b=b):
            copy(src, dst, index, a, b).wait_send()


def exchange_halo(fields, mask):
    return pl.pallas_call(
        halo_kernel,
        out_shape=(
            jax.ShapeDtypeStruct((16, 8, 256), F32),
            jax.ShapeDtypeStruct((16, 8, 256), F32),
            jax.ShapeDtypeStruct((8, 256), jnp.int32),
            jax.ShapeDtypeStruct((8, 256), jnp.int32),
            jax.ShapeDtypeStruct((272, 128), F32),
            jax.ShapeDtypeStruct((272, 128), F32),
        ),
        in_specs=[ANY, VMEM],
        out_specs=(VMEM,) * 6,
        scratch_shapes=[
            pltpu.VMEM((16, 256, 256), F32),
            pltpu.VMEM((256, 128), F32),
            pltpu.SemaphoreType.DMA((4,)),
            pltpu.SemaphoreType.DMA((10,)),
            pltpu.SemaphoreType.DMA((10,)),
        ],
        compiler_params=pltpu.CompilerParams(
            collective_id=0, has_side_effects=True, vmem_limit_bytes=60 << 20
        ),
        name="halo",
    )(fields, mask)


def coarse_matrix():
    matrix = np.zeros((8, 128, 2, 8, 16), np.float32)
    for row in range(8):
        for column in range(128):
            matrix[row, column, column // 64, row, (column % 64) // 4] = 1 / 16
    return matrix.reshape(1024, 256).astype(ml_dtypes.bfloat16)


def ocean_kernel(
    rate, slot, fields, mask, top, bot, mtop, mbot, left, right, gather,
    out, chosen,
    now, later, final, wet, sl0, sl1, sr0, sr1, wl, wr, sums, wide, patches, in_sem, out_sem,
):
    loads = []
    for half in range(2):
        side = pl.ds(128 * half, 128)
        for j, (src, start, rows) in enumerate(((fields, 16, 256), (top, 8, 8), (bot, 272, 8))):
            dst = now.at[half, :, pl.ds(start, rows), :]
            loads.append(pltpu.make_async_copy(src.at[:, :, side], dst, in_sem.at[3 * half + j]))
    for load in loads:
        load.start()
    for half in range(2):
        side = pl.ds(128 * half, 128)
        wet[half, 8:16, :] = mtop[:, side].astype(F32)
        wet[half, 16:272, :] = mask[:, side].astype(F32)
        wet[half, 272:280, :] = mbot[:, side].astype(F32)
    for buf in (sl0, sr0, sl1, sr1):
        buf[0:8, :] = jnp.zeros((8, 128), F32)
        buf[280:288, :] = jnp.zeros((8, 128), F32)
    for buf in (now, later):
        buf[:, :, 0:8, :] = jnp.zeros((2, 16, 8, 128), F32)
        buf[:, :, 280:288, :] = jnp.zeros((2, 16, 8, 128), F32)
    for load in loads:
        load.wait()

    lane = lanes((136, 128))
    blocks = [(8 + 136 * b, pl.ds(8 + 136 * b, 136)) for b in range(2)]
    inner = (lane & 7) < 4
    for row, at in blocks:
        got = pl.ds(row - 8, 136)
        own = pack_edges(lambda i: (now[0, i, at, :], now[1, i, at, :]), lane)
        west, east = left[got, :], right[got, :]
        sl0[at, :] = jnp.where(inner, west, own)
        sr0[at, :] = jnp.where(inner, own, east)
        wet0, wet1 = wet[0, at, :], wet[1, at, :]
        low = jnp.where((lane >= 4) & (lane < 8), pltpu.roll(wet0, 4, 1), 0.0)
        low = jnp.where(lane == 2, pltpu.roll(west, 2, 1), low)
        low = jnp.where(lane == 3, pltpu.roll(west, 123, 1), low)
        high = jnp.where(lane < 4, pltpu.roll(wet1, 4, 1), 0.0)
        high = jnp.where(lane == 4, pltpu.roll(east, 125, 1), high)
        high = jnp.where(lane == 5, pltpu.roll(east, 118, 1), high)
        for shift in (8, 16, 32, 64):
            low = low + pltpu.roll(low, shift, 1)
            high = high + pltpu.roll(high, shift, 1)
        wl[at, :] = low
        wr[at, :] = high

    level = jnp.zeros((1, 128), F32)
    for k in range(8):
        level = jnp.where(lanes((1, 128)) >> 4 == k, rate[k], level)

    def advance_strips(*sides):
        for row, at in blocks:
            for src, dst, cells in sides:
                c = src[at, :]
                u = jnp.where(lane < 16, c, 0.0)
                v = jnp.where((lane >= 16) & (lane < 32), c, 0.0)
                for shift in (16, 32, 64):
                    u = u + pltpu.roll(u, shift, 1)
                    v = v + pltpu.roll(v, shift, 1)
                e, w = pltpu.roll(c, 127, 1), pltpu.roll(c, 1, 1)
                n, s = src[pl.ds(row - 1, 136), :], src[pl.ds(row + 1, 136), :]
                lap = (e + w) + (n + s) - 4.0 * c
                adv = u * (e - w) + v * (s - n)
                dst[at, :] = cells[at, :] * (c + level * lap - 0.05 * adv)

    def advance(src, dst, low, high, lead, blocks, shift):
        def body(k, _):
            diff = rate[k]
            for block in range(blocks):
                row = lead + 16 * block
                at = pl.ds(row, 16)
                lane = lanes((16, 128))
                strip_l, strip_r = low[at, :], high[at, :]
                for lev in range(2):
                    i = 2 * k + lev
                    x0, x1 = src[0, i, at, :], src[1, i, at, :]
                    into_l = pltpu.roll(strip_l, 125 - 8 * i, 1)
                    into_r = pltpu.roll(strip_r, 123 - 8 * i, 1)
                    r0, r1 = pltpu.roll(x0, 1, 1), pltpu.roll(x1, 1, 1)
                    l0, l1 = pltpu.roll(x0, 127, 1), pltpu.roll(x1, 127, 1)
                    w = (jnp.where(lane == 0, into_l, r0), jnp.where(lane == 0, r0, r1))
                    e = (jnp.where(lane == 127, l1, l0), jnp.where(lane == 127, into_r, l1))
                    for half in range(2):
                        c = (x0, x1)[half]
                        n = src[half, i, pl.ds(row - 1, 16), :]
                        s = src[half, i, pl.ds(row + 1, 16), :]
                        u, v = src[half, lev, at, :], src[half, 2 + lev, at, :]
                        lap = (e[half] + w[half]) + (n + s) - 4.0 * c
                        adv = u * (e[half] - w[half]) + v * (s - n)
                        new = wet[half, at, :] * (c + diff * lap - 0.05 * adv)
                        dst[half, i, pl.ds(row - shift, 16), :] = new
            return 0

        return body

    lax.fori_loop(0, 8, advance(now, later, sl0, sr0, 8, 17, 0), 0)
    advance_strips((sl0, sl1, wl), (sr0, sr1, wr))
    lax.fori_loop(0, 8, advance(later, now, sl1, sr1, 8, 17, 0), 0)
    advance_strips((sl1, sl0, wl), (sr1, sr0, wr))
    last = advance(now, final, sl0, sr0, 16, 16, 16)

    def every_fourth(half, i, j):
        return final[half, i, pl.ds(j, 64, stride=4), :]

    def send(k, half):
        cut = pl.ds(2 * k, 2)
        src, dst = final.at[half, cut], out.at[cut, :, pl.ds(128 * half, 128)]
        return pltpu.make_async_copy(src, dst, out_sem.at[k, half])

    def last_step(k, _):
        last(k, 0)
        for half in range(2):
            send(k, half).start()
        for lev in range(2):
            i = 2 * k + lev
            for half in range(2):
                total = every_fourth(half, i, 0)
                for j in range(1, 4):
                    total = total + every_fourth(half, i, j)
                for pr in range(4):
                    to = pl.multiple_of(((lev * 4 + pr) * 8 + k) * 16, 16)
                    sums[half, pl.ds(to, 16), :] = total[16 * pr : 16 * pr + 16]
        return 0

    sums[:, 1024:2048, :] = jnp.zeros((2, 1024, 128), F32)
    lax.fori_loop(0, 8, last_step, 0)

    for lev in range(2):
        for half in range(2):
            for which in range(3):
                total = None
                for j in range(4):
                    if which < 2:
                        term = every_fourth(half, 2 * which + lev, j)
                        term = term * every_fourth(half, 4 + 2 * which + lev, j)
                    else:
                        term = wet[half, pl.ds(16 + j, 64, stride=4), :]
                    total = term if total is None else total + term
                for pr in range(4):
                    to = 1024 + ((lev * 4 + pr) * 8 + which) * 16
                    sums[half, to : to + 16, :] = total[16 * pr : 16 * pr + 16]

    table = gather[...]
    for half in range(2):
        for rows in range(2):
            for y in range(8):
                x = sums[half, pl.ds(8 * rows + y, 128, stride=16), :]
                a = x.astype(BF16)
                x = x - a.astype(F32)
                b = x.astype(BF16)
                c = (x - b.astype(F32)).astype(BF16)
                side = pl.ds(128 * y, 128)
                wide[0:128, side] = a
                wide[128:256, side] = b
                wide[256:384, side] = c
            r = jnp.dot(wide[...], table, preferred_element_type=F32)
            r = r[0:128] + r[128:256] + r[256:384]
            means, products = r[0:64], r[64:128]
            for q in range(8):
                m = means[8 * q : 8 * q + 8]
                p = products[8 * q : 8 * q + 8]
                sub = lax.broadcasted_iota(jnp.int32, (8, 256), 0)
                p = p - jnp.where(sub < 2, m * pltpu.roll(m, 6, 0), 0.0)
                both = jnp.concatenate([m, p], axis=0).astype(BF16)
                for pc in range(2):
                    to = pl.ds(128 * rows, 128)
                    patches[4 * q + 2 * half + pc, :, to] = both[:, 128 * pc : 128 * pc + 128]

    for j in range(32):
        chosen[j] = patches[slot[j]]

    def finish(k, _):
        for half in range(2):
            send(k, half).wait()
        return 0

    lax.fori_loop(0, 8, finish, 0)


def run_ocean(rate, slot, fields, mask, halo, gather):
    return pl.pallas_call(
        ocean_kernel,
        out_shape=(
            jax.ShapeDtypeStruct((16, 256, 256), F32),
            jax.ShapeDtypeStruct((32, 16, 256), BF16),
        ),
        in_specs=[SMEM, SMEM, ANY, VMEM, ANY, ANY, VMEM, VMEM, VMEM, VMEM, VMEM],
        out_specs=(ANY, VMEM),
        scratch_shapes=[
            pltpu.VMEM((2, 16, 288, 128), F32),
            pltpu.VMEM((2, 16, 288, 128), F32),
            pltpu.VMEM((2, 16, 256, 128), F32),
            pltpu.VMEM((2, 288, 128), F32),
        ]
        + [pltpu.VMEM((288, 128), F32)] * 6
        + [
            pltpu.VMEM((2, 2048, 128), F32),
            pltpu.VMEM((384, 1024), BF16),
            pltpu.VMEM((32, 16, 256), BF16),
            pltpu.SemaphoreType.DMA((6,)),
            pltpu.SemaphoreType.DMA((8, 2)),
        ],
        compiler_params=pltpu.CompilerParams(vmem_limit_bytes=60 << 20),
        name="ocean",
    )(rate, slot, fields, mask, *halo, gather)


def swap_kernel(mine, got, own_sem, send, recv):
    my, mx = lax.axis_index("ty"), lax.axis_index("tx")
    barrier = pltpu.get_barrier_semaphore()
    for d in range(1, NTY):
        peer = lax.rem(my + d, NTY)
        pl.semaphore_signal(barrier, inc=1, device_id={"ty": peer, "tx": mx}, device_id_type=MESH)
    own = pltpu.make_async_copy(
        mine.at[pl.ds(4 * my, 4)], got.at[pl.ds(0, 4)], own_sem
    )
    own.start()
    pl.semaphore_wait(barrier, NTY - 1)
    copies = []
    for d in range(1, NTY):
        peer = lax.rem(my + d, NTY)
        copies.append(
            pltpu.make_async_remote_copy(
                src_ref=mine.at[pl.ds(4 * peer, 4)],
                dst_ref=got.at[pl.ds(4 * d, 4)],
                send_sem=send.at[d],
                recv_sem=recv.at[d],
                device_id={"ty": peer, "tx": mx},
                device_id_type=MESH,
            )
        )
        copies[-1].start()
    own.wait()
    for copy in copies:
        copy.wait()


def swap_patches(mine):
    return pl.pallas_call(
        swap_kernel,
        out_shape=jax.ShapeDtypeStruct((32, 16, 256), BF16),
        in_specs=[VMEM],
        out_specs=VMEM,
        scratch_shapes=[
            pltpu.SemaphoreType.DMA,
            pltpu.SemaphoreType.DMA((NTY,)),
            pltpu.SemaphoreType.DMA((NTY,)),
        ],
        compiler_params=pltpu.CompilerParams(
            collective_id=1, has_side_effects=True, vmem_limit_bytes=24 << 20
        ),
        name="swap",
    )(mine)


def contract(a, b, dim_a, dim_b):
    return lax.dot_general(
        a, b, (((dim_a,), (dim_b,)), ((), ())), preferred_element_type=F32
    )


def net_kernel(got, win, wmid, wout, grads, misfit, hs, ds, wback, amid, ain, aout, amis):
    step = pl.program_id(0)
    size = GROUP * 256

    @pl.when(step == 0)
    def _():
        for ref in (hs, ds, amid, ain, aout, amis):
            ref[...] = jnp.zeros_like(ref)
        for t in range(9):
            at = pl.ds(128 * t, 128)
            wback[at, :] = wmid[at, :].astype(F32).T.astype(BF16)

    lane = lanes((8, size))
    col, row = lane & 15, (lane >> 4) & 15

    def inside(dy, dx):
        ok = None
        for value, change in ((row, dy), (col, dx)):
            if change:
                one = value >= 1 if change < 0 else value <= 14
                ok = one if ok is None else ok & one
        return ok

    def moved(a, dy, dx):
        off = 16 * dy + dx
        if off == 0:
            return a
        return jnp.where(inside(dy, dx), pltpu.roll(a, (-off) % size, 1), 0.0)

    side = lax.broadcasted_iota(jnp.int32, (size, 128), 0) & 15

    def spread(ref, a, sign):
        for j, dx in enumerate((-1, 0, 1)):
            go = sign * dx
            if go == 0:
                v = a
            elif go < 0:
                v = jnp.where(side == 0, 0.0, pltpu.roll(a, 1, 0))
            else:
                v = jnp.where(side == 15, 0.0, pltpu.roll(a, size - 1, 0))
            v = v.astype(BF16)
            for i, dy in enumerate((-1, 0, 1)):
                to = pl.ds(128 * (3 * i + j), 128)
                for p in range(GROUP):
                    b = 256 * p
                    if sign * dy == 0:
                        ref[b : b + 256, to] = v[b : b + 256]
                    elif sign * dy < 0:
                        ref[b + 16 : b + 256, to] = v[b : b + 240]
                    else:
                        ref[b : b + 240, to] = v[b + 16 : b + 256]

    def silu(z):
        s = 0.5 * jnp.tanh(0.5 * z) + 0.5
        h = z * s
        return h, s + h * (1.0 - s)

    def work(hs, ds, base):
        data = [got[base + p].astype(F32) for p in range(GROUP)]
        x = jnp.concatenate([d[0:8] for d in data], axis=1)
        lab = jnp.concatenate([d[8:16] for d in data], axis=1)
        xcat = jnp.concatenate([moved(x, dy, dx) for dy, dx in TAPS], axis=0).astype(BF16)
        z1 = contract(xcat, win[...], 0, 0)
        yield
        h1, slope1 = silu(z1)
        spread(hs, h1, 1)
        yield
        z2 = jnp.dot(hs[...], wmid[...], preferred_element_type=F32)
        yield
        h2, slope2 = silu(z2)
        h2 = h2.astype(BF16)
        parts = contract(wout[...], h2, 1, 1)
        yield
        y = jnp.zeros((8, size), F32)
        for t, (dy, dx) in enumerate(TAPS):
            y = y + moved(parts[8 * t : 8 * t + 8], dy, dx)
        sub = lax.broadcasted_iota(jnp.int32, (8, size), 0)
        diff = jnp.where(sub < 2, y - lab, 0.0)
        weighted = lab[2:3] * diff
        g = 2.0 * weighted
        gcat = jnp.concatenate([moved(g, -dy, -dx) for dy, dx in TAPS], axis=0).astype(BF16)
        dh2 = contract(gcat, wout[...], 0, 0).astype(BF16).astype(F32)
        yield
        dz2 = dh2 * slope2
        spread(ds, dz2, -1)
        yield
        dh1 = jnp.dot(ds[...], wback[...], preferred_element_type=F32).astype(BF16).astype(F32)
        yield
        dmid = contract(h1.astype(BF16), ds[...], 0, 0)
        yield
        dz1 = (dh1 * slope1).astype(BF16)
        dout = jnp.dot(gcat, h2, preferred_element_type=F32)
        din = jnp.dot(xcat, dz1, preferred_element_type=F32)
        yield weighted * diff, dmid, din, dout

    teams = [work(hs.at[i], ds.at[i], GROUP * i) for i in range(TEAMS)]
    results = []
    while len(results) < TEAMS:
        for team in teams:
            value = next(team)
            if value is not None:
                results.append(value)
    for ref, parts in zip((amis, amid, ain, aout), zip(*results)):
        ref[...] += functools.reduce(jnp.add, parts)

    @pl.when(step == pl.num_programs(0) - 1)
    def _():
        for t in range(9):
            at = pl.ds(128 * t, 128)
            grads[at, :] = amid[:, at].astype(BF16)
        both = jnp.concatenate(
            [ain[...]] + [aout[8 * t : 8 * t + 2, :] for t in range(9)] + [jnp.zeros((38, 128), F32)],
            axis=0,
        )
        grads[1152:1280, :] = both.astype(BF16)
        misfit[...] = jnp.full((8, 128), jnp.sum(amis[...]), F32)


def run_net(got, win, wmid, wout):
    whole = lambda i: (0, 0)
    return pl.pallas_call(
        net_kernel,
        grid=(32 // (GROUP * TEAMS),),
        out_shape=(
            jax.ShapeDtypeStruct((ROWS, 128), BF16),
            jax.ShapeDtypeStruct((8, 128), F32),
        ),
        in_specs=[
            pl.BlockSpec((GROUP * TEAMS, 16, 256), lambda i: (i, 0, 0)),
            pl.BlockSpec((72, 128), whole),
            pl.BlockSpec((1152, 128), whole),
            pl.BlockSpec((72, 128), whole),
        ],
        out_specs=(pl.BlockSpec((ROWS, 128), whole), pl.BlockSpec((8, 128), whole)),
        scratch_shapes=[
            pltpu.VMEM((TEAMS, GROUP * 256, 1152), BF16),
            pltpu.VMEM((TEAMS, GROUP * 256, 1152), BF16),
            pltpu.VMEM((1152, 128), BF16),
            pltpu.VMEM((128, 1152), F32),
            pltpu.VMEM((72, 128), F32),
            pltpu.VMEM((72, 128), F32),
            pltpu.VMEM((8, GROUP * 256), F32),
        ],
        compiler_params=pltpu.CompilerParams(vmem_limit_bytes=48 << 20),
        name="net",
    )(got, win, wmid, wout)


def total_kernel(
    grads, mid, first, last, got1, part, got2, whole, s1, r1, s2, r2, s3, r3, s4, r4
):
    my, mx = lax.axis_index("ty"), lax.axis_index("tx")
    barrier = pltpu.get_barrier_semaphore()
    for d in range(1, NTY):
        to = {"ty": lax.rem(my + d, NTY), "tx": mx}
        pl.semaphore_signal(barrier, inc=1, device_id=to, device_id_type=MESH)
    for d in range(1, NTX):
        to = {"ty": my, "tx": lax.rem(mx + d, NTX)}
        pl.semaphore_signal(barrier, inc=1, device_id=to, device_id_type=MESH)
    pl.semaphore_wait(barrier, NTY + NTX - 2)

    def copy(src, dst, send, recv, to):
        return pltpu.make_async_remote_copy(
            src_ref=src, dst_ref=dst, send_sem=send, recv_sem=recv, device_id=to, device_id_type=MESH
        )

    def one(d):
        peer = lax.rem(my + d, NTY)
        src = grads.at[pl.ds(pl.multiple_of(CHUNK * peer, 16), CHUNK), :]
        return copy(src, got1.at[d], s1.at[d], r1.at[d], {"ty": peer, "tx": mx})

    for d in range(1, NTY):
        one(d).start()
    part[...] = grads[pl.ds(pl.multiple_of(CHUNK * my, 16), CHUNK), :].astype(F32)
    for d in range(1, NTY):
        one(d).wait_recv()
        part[...] += got1[d].astype(F32)

    def two(d):
        peer = lax.rem(mx + d, NTX)
        src = part.at[pl.ds(pl.multiple_of(PIECE * peer, 8), PIECE), :]
        return copy(src, got2.at[d], s2.at[d], r2.at[d], {"ty": my, "tx": peer})

    def owns(device):
        return device < OWNERS

    for d in range(1, NTX):

        @pl.when(owns(lax.rem(mx + d, NTX)))
        def _(d=d):
            two(d).start()

    base = CHUNK * my

    def three(d, source, peer):
        place = whole.at[pl.ds(pl.multiple_of(base + PIECE * source, 8), PIECE), :]
        return copy(place, place, s3.at[d], r3.at[d], {"ty": my, "tx": peer})

    @pl.when(owns(mx))
    def _():
        at = pl.multiple_of(PIECE * mx, 8)
        total = part[pl.ds(at, PIECE), :]
        for d in range(1, NTX):
            peer = lax.rem(mx + d, NTX)
            copy(
                part.at[pl.ds(0, PIECE), :], got2.at[d], s2.at[d], r2.at[d], {"ty": my, "tx": peer}
            ).wait_recv()
            total = total + got2[d]
        whole[pl.ds(pl.multiple_of(base + PIECE * mx, 8), PIECE), :] = total
        for d in range(1, NTX):
            three(d, mx, lax.rem(mx + d, NTX)).start()

    for d in range(1, NTX):
        source = lax.rem(mx + NTX - d, NTX)

        @pl.when(owns(source))
        def _(d=d, source=source):
            three(d, source, source).wait_recv()

    def four(d, source, peer):
        place = whole.at[pl.ds(pl.multiple_of(CHUNK * source, 8), CHUNK), :]
        return copy(place, place, s4.at[d], r4.at[d], {"ty": peer, "tx": mx})

    for d in range(1, NTY):
        four(d, my, lax.rem(my + d, NTY)).start()
    for d in range(1, NTY):
        source = lax.rem(my + NTY - d, NTY)
        four(d, source, source).wait_recv()

    for ref, start, rows in ((mid, 0, 1152), (first, 1152, 72), (last, 1224, 18)):
        g = whole[start : start + rows, :]
        ref[...] = g * lax.rsqrt(jnp.sum(g * g) / F32(rows * 128) + NORM_EPS)

    for d in range(1, NTY):
        one(d).wait_send()
        four(d, my, lax.rem(my + d, NTY)).wait_send()
    for d in range(1, NTX):

        @pl.when(owns(lax.rem(mx + d, NTX)))
        def _(d=d):
            two(d).wait_send()

        @pl.when(owns(mx))
        def _(d=d):
            three(d, mx, lax.rem(mx + d, NTX)).wait_send()


def add_up(grads):
    dma = pltpu.SemaphoreType.DMA
    return pl.pallas_call(
        total_kernel,
        out_shape=(
            jax.ShapeDtypeStruct((1152, 128), F32),
            jax.ShapeDtypeStruct((72, 128), F32),
            jax.ShapeDtypeStruct((18, 128), F32),
        ),
        in_specs=[VMEM],
        out_specs=(VMEM,) * 3,
        scratch_shapes=[
            pltpu.VMEM((NTY, CHUNK, 128), BF16),
            pltpu.VMEM((CHUNK, 128), F32),
            pltpu.VMEM((NTX, PIECE, 128), F32),
            pltpu.VMEM((ROWS, 128), F32),
        ]
        + [dma((NTY,)), dma((NTY,)), dma((NTX,)), dma((NTX,)), dma((NTX,)), dma((NTX,)), dma((NTY,)), dma((NTY,))],
        compiler_params=pltpu.CompilerParams(
            collective_id=2, has_side_effects=True, vmem_limit_bytes=24 << 20
        ),
        name="total",
    )(grads)


def per_device(fields, ocean_mask, diffusivity, patch_slot_assignment, conv_in, conv_mid, conv_out):
    state = fields.reshape(16, 256, 256)
    halo = exchange_halo(state, ocean_mask)
    gather = jnp.asarray(coarse_matrix())
    current, mine = run_ocean(
        diffusivity, patch_slot_assignment.reshape(32), state, ocean_mask, halo, gather
    )
    got = swap_patches(mine)
    win = conv_in.reshape(72, 128)
    wmid = conv_mid.reshape(1152, 128)
    wout = jnp.pad(conv_out.reshape(9, 128, 2).transpose(0, 2, 1), ((0, 0), (0, 6), (0, 0)))
    grads, misfit = run_net(got, win, wmid, wout.reshape(72, 128))
    mid, first, last = add_up(grads)
    member_loss = misfit[0:1, 0:1] / 8192
    return (
        current.reshape(fields.shape),
        member_loss,
        first.reshape(conv_in.shape),
        mid.reshape(conv_mid.shape),
        last.reshape(9, 2, 128).transpose(0, 2, 1).reshape(conv_out.shape),
    )


def solution(mesh):
    placed = (P(None, None, "ty", "tx"), P("ty", "tx"), P(), P("ty", "tx", None), P(), P(), P())
    return jax.shard_map(
        per_device,
        mesh=mesh,
        in_specs=placed,
        out_specs=(P(None, None, "ty", "tx"), P("ty", "tx"), P(), P(), P()),
        check_vma=False,
    )
```

```python
import functools

import jax
import jax.numpy as jnp
import ml_dtypes
import numpy as np
from jax import lax
from jax.experimental import pallas as pl
from jax.experimental.pallas import tpu as pltpu
from jax.sharding import PartitionSpec as P

F32 = jnp.float32
BF16 = jnp.bfloat16
MESH = pl.DeviceIdType.MESH
NTY, NTX = 8, 16
ROWS = 1280
CHUNK = ROWS // NTY
PIECE = 16
HALF = CHUNK // 2
OWNERS = HALF // PIECE
GROUP = 4
TEAMS = 2
TAPS = [(i - 1, j - 1) for i in range(3) for j in range(3)]
NORM_EPS = 1e-6
ANY = pl.BlockSpec(memory_space=pl.ANY)
VMEM = pl.BlockSpec(memory_space=pltpu.VMEM)
SMEM = pl.BlockSpec(memory_space=pltpu.SMEM)


def lanes(shape):
    return lax.broadcasted_iota(jnp.int32, shape, len(shape) - 1)


def pack_edges(field, lane):
    packed = None
    for i in range(16):
        first, last = field(i)
        edge = pltpu.roll(jnp.where(lane >= 124, last, first), (8 * i + 4) % 128, 1)
        packed = edge if packed is None else jnp.where(lane >= 8 * i, edge, packed)
    return packed


def halo_kernel(fields, mask, top, bot, mtop, mbot, left, right, tile, packed, in_sem, send, recv):
    my, mx = lax.axis_index("ty"), lax.axis_index("tx")
    has = {-1: my > 0, 1: my < NTY - 1}
    has_x = {-1: mx > 0, 1: mx < NTX - 1}
    loads = []
    for i in range(4):
        cut = pl.ds(4 * i, 4)
        loads.append(pltpu.make_async_copy(fields.at[cut], tile.at[cut], in_sem.at[i]))
        loads[-1].start()

    def both(a, b):
        return jnp.logical_and(a, b)

    barrier = pltpu.get_barrier_semaphore()
    steps = [(a, b) for a in (-1, 0, 1) for b in (-1, 0, 1) if (a, b) != (0, 0)]

    def present(a, b):
        if a == 0:
            return has_x[b]
        if b == 0:
            return has[a]
        return both(has[a], has_x[b])

    count = jnp.int32(0)
    for a, b in steps:
        here = present(a, b)
        count = count + here.astype(jnp.int32)

        @pl.when(here)
        def _(a=a, b=b):
            pl.semaphore_signal(
                barrier, inc=1, device_id={"ty": my + a, "tx": mx + b}, device_id_type=MESH
            )

    @pl.when(my == 0)
    def _():
        top[...] = jnp.zeros_like(top)
        mtop[...] = jnp.zeros_like(mtop)
        left[0:8, :] = jnp.zeros((8, 128), F32)
        right[0:8, :] = jnp.zeros((8, 128), F32)

    @pl.when(my == NTY - 1)
    def _():
        bot[...] = jnp.zeros_like(bot)
        mbot[...] = jnp.zeros_like(mbot)
        left[264:272, :] = jnp.zeros((8, 128), F32)
        right[264:272, :] = jnp.zeros((8, 128), F32)

    @pl.when(mx == 0)
    def _():
        left[...] = jnp.zeros_like(left)

    @pl.when(mx == NTX - 1)
    def _():
        right[...] = jnp.zeros_like(right)

    pl.semaphore_wait(barrier, count)

    def copy(src, dst, index, a, b):
        return pltpu.make_async_remote_copy(
            src_ref=src,
            dst_ref=dst,
            send_sem=send.at[index],
            recv_sem=recv.at[index],
            device_id={"ty": my + a, "tx": mx + b},
            device_id_type=MESH,
        )

    row_copies = [
        (fields.at[:, pl.ds(248, 8), :], top, 1, 0),
        (mask.at[pl.ds(248, 8), :], mtop, 1, 0),
        (fields.at[:, pl.ds(0, 8), :], bot, -1, 0),
        (mask.at[pl.ds(0, 8), :], mbot, -1, 0),
    ]
    side_copies = [
        (packed, left.at[pl.ds(8, 256), :], 0, 1),
        (packed, right.at[pl.ds(8, 256), :], 0, -1),
        (packed.at[pl.ds(248, 8), :], left.at[pl.ds(0, 8), :], 1, 1),
        (packed.at[pl.ds(0, 8), :], left.at[pl.ds(264, 8), :], -1, 1),
        (packed.at[pl.ds(248, 8), :], right.at[pl.ds(0, 8), :], 1, -1),
        (packed.at[pl.ds(0, 8), :], right.at[pl.ds(264, 8), :], -1, -1),
    ]
    every = row_copies + side_copies

    for index, (src, dst, a, b) in enumerate(row_copies):

        @pl.when(present(a, b))
        def _(index=index, src=src, dst=dst, a=a, b=b):
            copy(src, dst, index, a, b).start()

    for load in loads:
        load.wait()

    lane = lanes((128, 128))
    for block in range(2):
        at = pl.ds(128 * block, 128)
        edges = pack_edges(lambda i: (tile[i, at, 0:128], tile[i, at, 128:256]), lane)
        wet0 = mask[at, 0:128].astype(F32)
        wet1 = mask[at, 128:256].astype(F32)
        edges = jnp.where(lane == 0, pltpu.roll(wet1, 2, 1), edges)
        edges = jnp.where(lane == 8, pltpu.roll(wet1, 9, 1), edges)
        edges = jnp.where(lane == 7, pltpu.roll(wet0, 7, 1), edges)
        edges = jnp.where(lane == 15, pltpu.roll(wet0, 14, 1), edges)
        packed[at, :] = edges

    for index, (src, dst, a, b) in enumerate(side_copies):

        @pl.when(present(a, b))
        def _(index=index + 4, src=src, dst=dst, a=a, b=b):
            copy(src, dst, index, a, b).start()

    for index, (src, dst, a, b) in enumerate(every):

        @pl.when(present(-a, -b))
        def _(index=index, src=src, dst=dst, a=a, b=b):
            copy(src, dst, index, a, b).wait_recv()

    for index, (src, dst, a, b) in enumerate(every):

        @pl.when(present(a, b))
        def _(index=index, src=src, dst=dst, a=a, b=b):
            copy(src, dst, index, a, b).wait_send()


def exchange_halo(fields, mask):
    return pl.pallas_call(
        halo_kernel,
        out_shape=(
            jax.ShapeDtypeStruct((16, 8, 256), F32),
            jax.ShapeDtypeStruct((16, 8, 256), F32),
            jax.ShapeDtypeStruct((8, 256), jnp.int32),
            jax.ShapeDtypeStruct((8, 256), jnp.int32),
            jax.ShapeDtypeStruct((272, 128), F32),
            jax.ShapeDtypeStruct((272, 128), F32),
        ),
        in_specs=[ANY, VMEM],
        out_specs=(VMEM,) * 6,
        scratch_shapes=[
            pltpu.VMEM((16, 256, 256), F32),
            pltpu.VMEM((256, 128), F32),
            pltpu.SemaphoreType.DMA((4,)),
            pltpu.SemaphoreType.DMA((10,)),
            pltpu.SemaphoreType.DMA((10,)),
        ],
        compiler_params=pltpu.CompilerParams(
            collective_id=0, has_side_effects=True, vmem_limit_bytes=60 << 20
        ),
        name="halo",
    )(fields, mask)


def coarse_matrix():
    matrix = np.zeros((8, 128, 2, 8, 16), np.float32)
    for row in range(8):
        for column in range(128):
            matrix[row, column, column // 64, row, (column % 64) // 4] = 1 / 16
    return matrix.reshape(1024, 256).astype(ml_dtypes.bfloat16)


def ocean_kernel(
    rate, slot, fields, mask, top, bot, mtop, mbot, left, right, gather,
    out, chosen,
    now, later, final, wet, sl0, sl1, sr0, sr1, wl, wr, sums, wide, patches, in_sem, out_sem,
):
    loads = []
    for half in range(2):
        side = pl.ds(128 * half, 128)
        for j, (src, start, rows) in enumerate(((fields, 16, 256), (top, 8, 8), (bot, 272, 8))):
            dst = now.at[half, :, pl.ds(start, rows), :]
            loads.append(pltpu.make_async_copy(src.at[:, :, side], dst, in_sem.at[3 * half + j]))
    for load in loads:
        load.start()
    for half in range(2):
        side = pl.ds(128 * half, 128)
        wet[half, 8:16, :] = mtop[:, side].astype(F32)
        wet[half, 16:272, :] = mask[:, side].astype(F32)
        wet[half, 272:280, :] = mbot[:, side].astype(F32)
    for buf in (sl0, sr0, sl1, sr1):
        buf[0:8, :] = jnp.zeros((8, 128), F32)
        buf[280:288, :] = jnp.zeros((8, 128), F32)
    for buf in (now, later):
        buf[:, :, 0:8, :] = jnp.zeros((2, 16, 8, 128), F32)
        buf[:, :, 280:288, :] = jnp.zeros((2, 16, 8, 128), F32)
    for load in loads:
        load.wait()

    lane = lanes((136, 128))
    blocks = [(8 + 136 * b, pl.ds(8 + 136 * b, 136)) for b in range(2)]
    inner = (lane & 7) < 4
    for row, at in blocks:
        got = pl.ds(row - 8, 136)
        own = pack_edges(lambda i: (now[0, i, at, :], now[1, i, at, :]), lane)
        west, east = left[got, :], right[got, :]
        sl0[at, :] = jnp.where(inner, west, own)
        sr0[at, :] = jnp.where(inner, own, east)
        wet0, wet1 = wet[0, at, :], wet[1, at, :]
        low = jnp.where((lane >= 4) & (lane < 8), pltpu.roll(wet0, 4, 1), 0.0)
        low = jnp.where(lane == 2, pltpu.roll(west, 2, 1), low)
        low = jnp.where(lane == 3, pltpu.roll(west, 123, 1), low)
        high = jnp.where(lane < 4, pltpu.roll(wet1, 4, 1), 0.0)
        high = jnp.where(lane == 4, pltpu.roll(east, 125, 1), high)
        high = jnp.where(lane == 5, pltpu.roll(east, 118, 1), high)
        for shift in (8, 16, 32, 64):
            low = low + pltpu.roll(low, shift, 1)
            high = high + pltpu.roll(high, shift, 1)
        wl[at, :] = low
        wr[at, :] = high

    level = jnp.zeros((1, 128), F32)
    for k in range(8):
        level = jnp.where(lanes((1, 128)) >> 4 == k, rate[k], level)

    def advance_strips(*sides):
        for row, at in blocks:
            for src, dst, cells in sides:
                c = src[at, :]
                u = jnp.where(lane < 16, c, 0.0)
                v = jnp.where((lane >= 16) & (lane < 32), c, 0.0)
                for shift in (16, 32, 64):
                    u = u + pltpu.roll(u, shift, 1)
                    v = v + pltpu.roll(v, shift, 1)
                e, w = pltpu.roll(c, 127, 1), pltpu.roll(c, 1, 1)
                n, s = src[pl.ds(row - 1, 136), :], src[pl.ds(row + 1, 136), :]
                lap = (e + w) + (n + s) - 4.0 * c
                adv = u * (e - w) + v * (s - n)
                dst[at, :] = cells[at, :] * (c + level * lap - 0.05 * adv)

    def advance(src, dst, low, high, lead, blocks, shift):
        def body(k, _):
            diff = rate[k]
            for block in range(blocks):
                row = lead + 16 * block
                at = pl.ds(row, 16)
                lane = lanes((16, 128))
                strip_l, strip_r = low[at, :], high[at, :]
                for lev in range(2):
                    i = 2 * k + lev
                    x0, x1 = src[0, i, at, :], src[1, i, at, :]
                    into_l = pltpu.roll(strip_l, 125 - 8 * i, 1)
                    into_r = pltpu.roll(strip_r, 123 - 8 * i, 1)
                    r0, r1 = pltpu.roll(x0, 1, 1), pltpu.roll(x1, 1, 1)
                    l0, l1 = pltpu.roll(x0, 127, 1), pltpu.roll(x1, 127, 1)
                    w = (jnp.where(lane == 0, into_l, r0), jnp.where(lane == 0, r0, r1))
                    e = (jnp.where(lane == 127, l1, l0), jnp.where(lane == 127, into_r, l1))
                    for half in range(2):
                        c = (x0, x1)[half]
                        n = src[half, i, pl.ds(row - 1, 16), :]
                        s = src[half, i, pl.ds(row + 1, 16), :]
                        u, v = src[half, lev, at, :], src[half, 2 + lev, at, :]
                        lap = (e[half] + w[half]) + (n + s) - 4.0 * c
                        adv = u * (e[half] - w[half]) + v * (s - n)
                        new = wet[half, at, :] * (c + diff * lap - 0.05 * adv)
                        dst[half, i, pl.ds(row - shift, 16), :] = new
            return 0

        return body

    lax.fori_loop(0, 8, advance(now, later, sl0, sr0, 8, 17, 0), 0)
    advance_strips((sl0, sl1, wl), (sr0, sr1, wr))
    lax.fori_loop(0, 8, advance(later, now, sl1, sr1, 8, 17, 0), 0)
    advance_strips((sl1, sl0, wl), (sr1, sr0, wr))
    last = advance(now, final, sl0, sr0, 16, 16, 16)

    def every_fourth(half, i, j):
        return final[half, i, pl.ds(j, 64, stride=4), :]

    def send(k, half):
        cut = pl.ds(2 * k, 2)
        src, dst = final.at[half, cut], out.at[cut, :, pl.ds(128 * half, 128)]
        return pltpu.make_async_copy(src, dst, out_sem.at[k, half])

    def last_step(k, _):
        last(k, 0)
        for half in range(2):
            send(k, half).start()
        for lev in range(2):
            i = 2 * k + lev
            for half in range(2):
                total = every_fourth(half, i, 0)
                for j in range(1, 4):
                    total = total + every_fourth(half, i, j)
                for pr in range(4):
                    to = pl.multiple_of(((lev * 4 + pr) * 8 + k) * 16, 16)
                    sums[half, pl.ds(to, 16), :] = total[16 * pr : 16 * pr + 16]
        return 0

    sums[:, 1024:2048, :] = jnp.zeros((2, 1024, 128), F32)
    lax.fori_loop(0, 8, last_step, 0)

    for lev in range(2):
        for half in range(2):
            for which in range(3):
                total = None
                for j in range(4):
                    if which < 2:
                        term = every_fourth(half, 2 * which + lev, j)
                        term = term * every_fourth(half, 4 + 2 * which + lev, j)
                    else:
                        term = wet[half, pl.ds(16 + j, 64, stride=4), :]
                    total = term if total is None else total + term
                for pr in range(4):
                    to = 1024 + ((lev * 4 + pr) * 8 + which) * 16
                    sums[half, to : to + 16, :] = total[16 * pr : 16 * pr + 16]

    table = gather[...]
    for half in range(2):
        for rows in range(2):
            for y in range(8):
                x = sums[half, pl.ds(8 * rows + y, 128, stride=16), :]
                a = x.astype(BF16)
                x = x - a.astype(F32)
                b = x.astype(BF16)
                c = (x - b.astype(F32)).astype(BF16)
                side = pl.ds(128 * y, 128)
                wide[0:128, side] = a
                wide[128:256, side] = b
                wide[256:384, side] = c
            r = jnp.dot(wide[...], table, preferred_element_type=F32)
            r = r[0:128] + r[128:256] + r[256:384]
            means, products = r[0:64], r[64:128]
            for q in range(8):
                m = means[8 * q : 8 * q + 8]
                p = products[8 * q : 8 * q + 8]
                sub = lax.broadcasted_iota(jnp.int32, (8, 256), 0)
                p = p - jnp.where(sub < 2, m * pltpu.roll(m, 6, 0), 0.0)
                both = jnp.concatenate([m, p], axis=0).astype(BF16)
                for pc in range(2):
                    to = pl.ds(128 * rows, 128)
                    patches[4 * q + 2 * half + pc, :, to] = both[:, 128 * pc : 128 * pc + 128]

    for j in range(32):
        chosen[j] = patches[slot[j]]

    def finish(k, _):
        for half in range(2):
            send(k, half).wait()
        return 0

    lax.fori_loop(0, 8, finish, 0)


def run_ocean(rate, slot, fields, mask, halo, gather):
    return pl.pallas_call(
        ocean_kernel,
        out_shape=(
            jax.ShapeDtypeStruct((16, 256, 256), F32),
            jax.ShapeDtypeStruct((32, 16, 256), BF16),
        ),
        in_specs=[SMEM, SMEM, ANY, VMEM, ANY, ANY, VMEM, VMEM, VMEM, VMEM, VMEM],
        out_specs=(ANY, VMEM),
        scratch_shapes=[
            pltpu.VMEM((2, 16, 288, 128), F32),
            pltpu.VMEM((2, 16, 288, 128), F32),
            pltpu.VMEM((2, 16, 256, 128), F32),
            pltpu.VMEM((2, 288, 128), F32),
        ]
        + [pltpu.VMEM((288, 128), F32)] * 6
        + [
            pltpu.VMEM((2, 2048, 128), F32),
            pltpu.VMEM((384, 1024), BF16),
            pltpu.VMEM((32, 16, 256), BF16),
            pltpu.SemaphoreType.DMA((6,)),
            pltpu.SemaphoreType.DMA((8, 2)),
        ],
        compiler_params=pltpu.CompilerParams(vmem_limit_bytes=60 << 20),
        name="ocean",
    )(rate, slot, fields, mask, *halo, gather)


def swap_kernel(mine, got, own_sem, send, recv):
    my, mx = lax.axis_index("ty"), lax.axis_index("tx")
    barrier = pltpu.get_barrier_semaphore()
    for d in range(1, NTY):
        peer = lax.rem(my + d, NTY)
        pl.semaphore_signal(barrier, inc=1, device_id={"ty": peer, "tx": mx}, device_id_type=MESH)
    own = pltpu.make_async_copy(
        mine.at[pl.ds(4 * my, 4)], got.at[pl.ds(0, 4)], own_sem
    )
    own.start()
    pl.semaphore_wait(barrier, NTY - 1)
    copies = []
    for d in range(1, NTY):
        peer = lax.rem(my + d, NTY)
        copies.append(
            pltpu.make_async_remote_copy(
                src_ref=mine.at[pl.ds(4 * peer, 4)],
                dst_ref=got.at[pl.ds(4 * d, 4)],
                send_sem=send.at[d],
                recv_sem=recv.at[d],
                device_id={"ty": peer, "tx": mx},
                device_id_type=MESH,
            )
        )
        copies[-1].start()
    own.wait()
    for copy in copies:
        copy.wait()


def swap_patches(mine):
    return pl.pallas_call(
        swap_kernel,
        out_shape=jax.ShapeDtypeStruct((32, 16, 256), BF16),
        in_specs=[VMEM],
        out_specs=VMEM,
        scratch_shapes=[
            pltpu.SemaphoreType.DMA,
            pltpu.SemaphoreType.DMA((NTY,)),
            pltpu.SemaphoreType.DMA((NTY,)),
        ],
        compiler_params=pltpu.CompilerParams(
            collective_id=1, has_side_effects=True, vmem_limit_bytes=24 << 20
        ),
        name="swap",
    )(mine)


def greet(my, mx):
    barrier = pltpu.get_barrier_semaphore()
    for d in range(1, NTY):
        to = {"ty": lax.rem(my + d, NTY), "tx": mx}
        pl.semaphore_signal(barrier, inc=1, device_id=to, device_id_type=MESH)
    for d in range(1, NTY):
        to = {"ty": my, "tx": lax.rem(mx + 2 * d, NTX)}
        pl.semaphore_signal(barrier, inc=1, device_id=to, device_id_type=MESH)
    to = {"ty": my, "tx": mx + 1 - 2 * lax.rem(mx, 2)}
    pl.semaphore_signal(barrier, inc=1, device_id=to, device_id_type=MESH)


def add_up(my, mx, grads, got1, part, gotc, mine, got2, whole, sems):
    (s1, r1), (sc, rc), (s2, r2), (s3, r3), (s4, r4), (s5, r5) = sems
    core, place = lax.rem(mx, 2), mx // 2
    sibling = {"ty": my, "tx": mx + 1 - 2 * core}

    def copy(src, dst, send, recv, to):
        return pltpu.make_async_remote_copy(
            src_ref=src, dst_ref=dst, send_sem=send, recv_sem=recv, device_id=to, device_id_type=MESH
        )

    def rows(start, count):
        return pl.ds(pl.multiple_of(start, 8), count)

    def one(d):
        peer = lax.rem(my + d, NTY)
        src = grads.at[pl.ds(pl.multiple_of(CHUNK * peer, 16), CHUNK), :]
        return copy(src, got1.at[d], s1.at[d], r1.at[d], {"ty": peer, "tx": mx})

    for d in range(1, NTY):
        one(d).start()
    part[...] = grads[pl.ds(pl.multiple_of(CHUNK * my, 16), CHUNK), :].astype(F32)
    for d in range(1, NTY):
        one(d).wait_recv()
        part[...] += got1[d].astype(F32)

    pair = copy(part.at[rows(HALF * (1 - core), HALF), :], gotc, sc.at[0], rc.at[0], sibling)
    pair.start()
    pair.wait_recv()
    mine[...] = part[rows(HALF * core, HALF), :] + gotc[...]

    base = CHUNK * my + HALF * core

    def chip(index):
        return {"ty": my, "tx": 2 * index + core}

    def ahead(d):
        return lax.rem(place + d, NTY)

    def behind(d):
        return lax.rem(place + NTY - d, NTY)

    def two(d, piece):
        return copy(mine.at[rows(PIECE * piece, PIECE), :], got2.at[d], s2.at[d], r2.at[d], chip(ahead(d)))

    def three(d, owner, to):
        cut = whole.at[rows(base + PIECE * owner, PIECE), :]
        return copy(cut, cut, s3.at[d], r3.at[d], chip(to))

    for d in range(1, NTY):

        @pl.when(ahead(d) < OWNERS)
        def _(d=d):
            two(d, ahead(d)).start()

    @pl.when(place < OWNERS)
    def _():
        total = mine[rows(PIECE * place, PIECE), :]
        for d in range(1, NTY):
            two(d, 0).wait_recv()
            total = total + got2[d]
        whole[rows(base + PIECE * place, PIECE), :] = total
        for d in range(1, NTY):
            three(d, place, ahead(d)).start()

    for d in range(1, NTY):

        @pl.when(behind(d) < OWNERS)
        def _(d=d):
            three(d, behind(d), behind(d)).wait_recv()

    def four(d, source, peer):
        cut = whole.at[rows(CHUNK * source + HALF * core, HALF), :]
        return copy(cut, cut, s4.at[d], r4.at[d], {"ty": peer, "tx": mx})

    def five(d, half):
        source = lax.rem(my + NTY - d, NTY)
        cut = whole.at[rows(CHUNK * source + HALF * half, HALF), :]
        return copy(cut, cut, s5.at[d], r5.at[d], sibling)

    for d in range(1, NTY):
        four(d, my, lax.rem(my + d, NTY)).start()
    five(0, core).start()
    for d in range(1, NTY):
        source = lax.rem(my + NTY - d, NTY)
        four(d, source, source).wait_recv()
        five(d, core).start()
    for d in range(NTY):
        five(d, 1 - core).wait_recv()

    pair.wait_send()
    for d in range(NTY):
        five(d, core).wait_send()
    for d in range(1, NTY):
        one(d).wait_send()
        four(d, my, lax.rem(my + d, NTY)).wait_send()

        @pl.when(ahead(d) < OWNERS)
        def _(d=d):
            two(d, ahead(d)).wait_send()

        @pl.when(place < OWNERS)
        def _(d=d):
            three(d, place, ahead(d)).wait_send()


def contract(a, b, dim_a, dim_b):
    return lax.dot_general(
        a, b, (((dim_a,), (dim_b,)), ((), ())), preferred_element_type=F32
    )


def net_kernel(
    got, win, wmid, wout, misfit, first, mid, last,
    hs, ds, wback, wout8, amid, ain, aout, amis,
    grads, got1, part, gotc, mine, got2, whole, *sems,
):
    step = pl.program_id(0)
    my, mx = lax.axis_index("ty"), lax.axis_index("tx")
    size = GROUP * 256

    @pl.when(step == 0)
    def _():
        greet(my, mx)
        for t in range(9):
            wout8[8 * t : 8 * t + 8, :] = jnp.zeros((8, 128), F32)
            wout8[8 * t : 8 * t + 2, :] = wout[t].astype(F32)
        for ref in (hs, ds, amid, ain, aout, amis):
            ref[...] = jnp.zeros_like(ref)
        for t in range(9):
            at = pl.ds(128 * t, 128)
            wback[at, :] = wmid[at, :].astype(F32).T.astype(BF16)

    lane = lanes((8, size))
    col, row = lane & 15, (lane >> 4) & 15

    def inside(dy, dx):
        ok = None
        for value, change in ((row, dy), (col, dx)):
            if change:
                one = value >= 1 if change < 0 else value <= 14
                ok = one if ok is None else ok & one
        return ok

    def moved(a, dy, dx):
        off = 16 * dy + dx
        if off == 0:
            return a
        return jnp.where(inside(dy, dx), pltpu.roll(a, (-off) % size, 1), 0.0)

    side = lax.broadcasted_iota(jnp.int32, (size, 128), 0) & 15
    taps = wout8[...].astype(BF16)

    def spread(ref, a, sign):
        for j, dx in enumerate((-1, 0, 1)):
            go = sign * dx
            if go == 0:
                v = a
            elif go < 0:
                v = jnp.where(side == 0, 0.0, pltpu.roll(a, 1, 0))
            else:
                v = jnp.where(side == 15, 0.0, pltpu.roll(a, size - 1, 0))
            v = v.astype(BF16)
            for i, dy in enumerate((-1, 0, 1)):
                to = pl.ds(128 * (3 * i + j), 128)
                for p in range(GROUP):
                    b = 256 * p
                    if sign * dy == 0:
                        ref[b : b + 256, to] = v[b : b + 256]
                    elif sign * dy < 0:
                        ref[b + 16 : b + 256, to] = v[b : b + 240]
                    else:
                        ref[b : b + 240, to] = v[b + 16 : b + 256]

    def silu(z):
        s = 0.5 * jnp.tanh(0.5 * z) + 0.5
        h = z * s
        return h, s + h * (1.0 - s)

    def work(hs, ds, base):
        data = [got[base + p].astype(F32) for p in range(GROUP)]
        x = jnp.concatenate([d[0:8] for d in data], axis=1)
        lab = jnp.concatenate([d[8:16] for d in data], axis=1)
        xcat = jnp.concatenate([moved(x, dy, dx) for dy, dx in TAPS], axis=0).astype(BF16)
        z1 = contract(xcat, win[...], 0, 0)
        yield
        h1, slope1 = silu(z1)
        spread(hs, h1, 1)
        yield
        z2 = jnp.dot(hs[...], wmid[...], preferred_element_type=F32)
        yield
        h2, slope2 = silu(z2)
        h2 = h2.astype(BF16)
        parts = contract(taps, h2, 1, 1)
        yield
        y = jnp.zeros((8, size), F32)
        for t, (dy, dx) in enumerate(TAPS):
            y = y + moved(parts[8 * t : 8 * t + 8], dy, dx)
        sub = lax.broadcasted_iota(jnp.int32, (8, size), 0)
        diff = jnp.where(sub < 2, y - lab, 0.0)
        weighted = lab[2:3] * diff
        g = 2.0 * weighted
        gcat = jnp.concatenate([moved(g, -dy, -dx) for dy, dx in TAPS], axis=0).astype(BF16)
        dh2 = contract(gcat, taps, 0, 0).astype(BF16).astype(F32)
        yield
        dz2 = dh2 * slope2
        spread(ds, dz2, -1)
        yield
        dh1 = jnp.dot(ds[...], wback[...], preferred_element_type=F32).astype(BF16).astype(F32)
        yield
        dmid = contract(h1.astype(BF16), ds[...], 0, 0)
        yield
        dz1 = (dh1 * slope1).astype(BF16)
        dout = jnp.dot(gcat, h2, preferred_element_type=F32)
        din = jnp.dot(xcat, dz1, preferred_element_type=F32)
        yield weighted * diff, dmid, din, dout

    teams = [work(hs.at[i], ds.at[i], GROUP * i) for i in range(TEAMS)]
    results = []
    while len(results) < TEAMS:
        for team in teams:
            value = next(team)
            if value is not None:
                results.append(value)
    for ref, parts in zip((amis, amid, ain, aout), zip(*results)):
        ref[...] += functools.reduce(jnp.add, parts)

    @pl.when(step == pl.num_programs(0) - 1)
    def _():
        for t in range(9):
            at = pl.ds(128 * t, 128)
            grads[at, :] = amid[:, at].astype(BF16)
        both = jnp.concatenate(
            [ain[...]] + [aout[8 * t : 8 * t + 2, :] for t in range(9)] + [jnp.zeros((38, 128), F32)],
            axis=0,
        )
        grads[1152:1280, :] = both.astype(BF16)
        misfit[...] = jnp.full((1, 1), jnp.sum(amis[...]) / 8192, F32)
        pl.semaphore_wait(pltpu.get_barrier_semaphore(), 2 * NTY - 1)
        pairs = tuple(zip(sems[::2], sems[1::2]))
        add_up(my, mx, grads, got1, part, gotc, mine, got2, whole, pairs)

        def scale(start, rows):
            g = whole[start : start + rows, :]
            return lax.rsqrt(jnp.sum(g * g) / F32(rows * 128) + NORM_EPS)

        mid[...] = whole[0:1152, :] * scale(0, 1152)
        first[...] = whole[1152:1224, :] * scale(1152, 72)
        final = scale(1224, 18)
        for t in range(9):
            last[t] = whole[1224 + 2 * t : 1226 + 2 * t, :] * final


def run_net(got, win, wmid, wout):
    whole = lambda i: (0, 0)
    cube = lambda i: (0, 0, 0)
    dma = pltpu.SemaphoreType.DMA
    return pl.pallas_call(
        net_kernel,
        grid=(32 // (GROUP * TEAMS),),
        out_shape=(
            jax.ShapeDtypeStruct((1, 1), F32),
            jax.ShapeDtypeStruct((72, 128), F32),
            jax.ShapeDtypeStruct((1152, 128), F32),
            jax.ShapeDtypeStruct((9, 2, 128), F32),
        ),
        in_specs=[
            pl.BlockSpec((GROUP * TEAMS, 16, 256), lambda i: (i, 0, 0)),
            pl.BlockSpec((72, 128), whole),
            pl.BlockSpec((1152, 128), whole),
            pl.BlockSpec((9, 2, 128), cube),
        ],
        out_specs=(
            pl.BlockSpec((1, 1), whole),
            pl.BlockSpec((72, 128), whole),
            pl.BlockSpec((1152, 128), whole),
            pl.BlockSpec((9, 2, 128), cube),
        ),
        scratch_shapes=[
            pltpu.VMEM((TEAMS, GROUP * 256, 1152), BF16),
            pltpu.VMEM((TEAMS, GROUP * 256, 1152), BF16),
            pltpu.VMEM((1152, 128), BF16),
            pltpu.VMEM((72, 128), F32),
            pltpu.VMEM((128, 1152), F32),
            pltpu.VMEM((72, 128), F32),
            pltpu.VMEM((72, 128), F32),
            pltpu.VMEM((8, GROUP * 256), F32),
            pltpu.VMEM((ROWS, 128), BF16),
            pltpu.VMEM((NTY, CHUNK, 128), BF16),
            pltpu.VMEM((CHUNK, 128), F32),
            pltpu.VMEM((HALF, 128), F32),
            pltpu.VMEM((HALF, 128), F32),
            pltpu.VMEM((NTY, PIECE, 128), F32),
            pltpu.VMEM((ROWS, 128), F32),
        ]
        + [dma((NTY,)) for _ in range(12)],
        compiler_params=pltpu.CompilerParams(
            collective_id=2, has_side_effects=True, vmem_limit_bytes=48 << 20
        ),
        name="net",
    )(got, win, wmid, wout)


def per_device(fields, ocean_mask, diffusivity, patch_slot_assignment, conv_in, conv_mid, conv_out):
    state = fields.reshape(16, 256, 256)
    halo = exchange_halo(state, ocean_mask)
    gather = jnp.asarray(coarse_matrix())
    current, mine = run_ocean(
        diffusivity, patch_slot_assignment.reshape(32), state, ocean_mask, halo, gather
    )
    got = swap_patches(mine)
    win = conv_in.reshape(72, 128)
    wmid = conv_mid.reshape(1152, 128)
    wout = conv_out.reshape(9, 128, 2).transpose(0, 2, 1)
    member_loss, first, mid, last = run_net(got, win, wmid, wout)
    return (
        current.reshape(fields.shape),
        member_loss,
        first.reshape(conv_in.shape),
        mid.reshape(conv_mid.shape),
        last.transpose(0, 2, 1).reshape(conv_out.shape),
    )


def solution(mesh):
    placed = (P(None, None, "ty", "tx"), P("ty", "tx"), P(), P("ty", "tx", None), P(), P(), P())
    return jax.shard_map(
        per_device,
        mesh=mesh,
        in_specs=placed,
        out_specs=(P(None, None, "ty", "tx"), P("ty", "tx"), P(), P(), P()),
        check_vma=False,
    )
```

```python
import functools

import jax
import jax.numpy as jnp
import ml_dtypes
import numpy as np
from jax import lax
from jax.experimental import pallas as pl
from jax.experimental.pallas import tpu as pltpu
from jax.sharding import PartitionSpec as P

F32 = jnp.float32
BF16 = jnp.bfloat16
MESH = pl.DeviceIdType.MESH
NTY, NTX = 8, 16
ROWS = 1280
CHUNK = ROWS // NTY
PIECE = 16
HALF = CHUNK // 2
OWNERS = HALF // PIECE
GROUP = 4
TEAMS = 2
TAPS = [(i - 1, j - 1) for i in range(3) for j in range(3)]
NORM_EPS = 1e-6
ANY = pl.BlockSpec(memory_space=pl.ANY)
VMEM = pl.BlockSpec(memory_space=pltpu.VMEM)
SMEM = pl.BlockSpec(memory_space=pltpu.SMEM)


def lanes(shape):
    return lax.broadcasted_iota(jnp.int32, shape, len(shape) - 1)


def pack_edges(field, lane):
    packed = None
    for i in range(16):
        first, last = field(i)
        edge = pltpu.roll(jnp.where(lane >= 124, last, first), (8 * i + 4) % 128, 1)
        packed = edge if packed is None else jnp.where(lane >= 8 * i, edge, packed)
    return packed


def coarse_matrix():
    matrix = np.zeros((8, 128, 2, 8, 16), np.float32)
    for row in range(8):
        for column in range(128):
            matrix[row, column, column // 64, row, (column % 64) // 4] = 1 / 16
    return matrix.reshape(1024, 256).astype(ml_dtypes.bfloat16)


def halo_copies(my, mx, fields, mask, now, packed, left, right, mtop, mbot, send, recv):
    def present(a, b):
        ok = None
        for at, change, count in ((my, a, NTY), (mx, b, NTX)):
            if change:
                one = at > 0 if change < 0 else at < count - 1
                ok = one if ok is None else jnp.logical_and(ok, one)
        return ok

    rows = []
    for half in range(2):
        side = pl.ds(128 * half, 128)
        rows.append((fields.at[:, pl.ds(248, 8), side], now.at[half, :, pl.ds(8, 8), :], 1, 0))
        rows.append((fields.at[:, pl.ds(0, 8), side], now.at[half, :, pl.ds(272, 8), :], -1, 0))
    rows.append((mask.at[pl.ds(248, 8), :], mtop, 1, 0))
    rows.append((mask.at[pl.ds(0, 8), :], mbot, -1, 0))
    sides = [
        (packed.at[pl.ds(16, 256), :], left.at[pl.ds(8, 256), :], 0, 1),
        (packed.at[pl.ds(16, 256), :], right.at[pl.ds(8, 256), :], 0, -1),
        (packed.at[pl.ds(264, 8), :], left.at[pl.ds(0, 8), :], 1, 1),
        (packed.at[pl.ds(16, 8), :], left.at[pl.ds(264, 8), :], -1, 1),
        (packed.at[pl.ds(264, 8), :], right.at[pl.ds(0, 8), :], 1, -1),
        (packed.at[pl.ds(16, 8), :], right.at[pl.ds(264, 8), :], -1, -1),
    ]

    def copy(index):
        src, dst, a, b = (rows + sides)[index]
        return pltpu.make_async_remote_copy(
            src_ref=src,
            dst_ref=dst,
            send_sem=send.at[index],
            recv_sem=recv.at[index],
            device_id={"ty": my + a, "tx": mx + b},
            device_id_type=MESH,
        )

    def each(indices, act, arriving=False):
        for index in indices:
            a, b = (rows + sides)[index][2:]

            @pl.when(present(-a, -b) if arriving else present(a, b))
            def _(index=index):
                act(copy(index))

    return present, each, range(len(rows)), range(len(rows), len(rows) + len(sides))


def ocean_steps(rate, slot, packed, left, right, gather, out, chosen, now, later, final, wet, strips, sums, wide, patches, out_sem):
    sl0, sl1, sr0, sr1, wl, wr = strips
    lane = lanes((136, 128))
    blocks = [(8 + 136 * b, pl.ds(8 + 136 * b, 136)) for b in range(2)]
    inner = (lane & 7) < 4
    for row, at in blocks:
        got_rows = pl.ds(row - 8, 136)
        own = packed[at, :]
        west, east = left[got_rows, :], right[got_rows, :]
        sl0[at, :] = jnp.where(inner, west, own)
        sr0[at, :] = jnp.where(inner, own, east)
        wet0, wet1 = wet[0, at, :], wet[1, at, :]
        low = jnp.where((lane >= 4) & (lane < 8), pltpu.roll(wet0, 4, 1), 0.0)
        low = jnp.where(lane == 2, pltpu.roll(west, 2, 1), low)
        low = jnp.where(lane == 3, pltpu.roll(west, 123, 1), low)
        high = jnp.where(lane < 4, pltpu.roll(wet1, 4, 1), 0.0)
        high = jnp.where(lane == 4, pltpu.roll(east, 125, 1), high)
        high = jnp.where(lane == 5, pltpu.roll(east, 118, 1), high)
        for shift in (8, 16, 32, 64):
            low = low + pltpu.roll(low, shift, 1)
            high = high + pltpu.roll(high, shift, 1)
        wl[at, :] = low
        wr[at, :] = high

    level = jnp.zeros((1, 128), F32)
    for k in range(8):
        level = jnp.where(lanes((1, 128)) >> 4 == k, rate[k], level)

    def advance_strips(*sides):
        for row, at in blocks:
            for src, dst, cells in sides:
                c = src[at, :]
                u = jnp.where(lane < 16, c, 0.0)
                v = jnp.where((lane >= 16) & (lane < 32), c, 0.0)
                for shift in (16, 32, 64):
                    u = u + pltpu.roll(u, shift, 1)
                    v = v + pltpu.roll(v, shift, 1)
                e, w = pltpu.roll(c, 127, 1), pltpu.roll(c, 1, 1)
                n, s = src[pl.ds(row - 1, 136), :], src[pl.ds(row + 1, 136), :]
                lap = (e + w) + (n + s) - 4.0 * c
                adv = u * (e - w) + v * (s - n)
                dst[at, :] = cells[at, :] * (c + level * lap - 0.05 * adv)

    def advance(src, dst, low, high, lead, blocks, shift):
        def body(k, _):
            diff = rate[k]
            for block in range(blocks):
                row = lead + 16 * block
                at = pl.ds(row, 16)
                lane = lanes((16, 128))
                strip_l, strip_r = low[at, :], high[at, :]
                for lev in range(2):
                    i = 2 * k + lev
                    x0, x1 = src[0, i, at, :], src[1, i, at, :]
                    into_l = pltpu.roll(strip_l, 125 - 8 * i, 1)
                    into_r = pltpu.roll(strip_r, 123 - 8 * i, 1)
                    r0, r1 = pltpu.roll(x0, 1, 1), pltpu.roll(x1, 1, 1)
                    l0, l1 = pltpu.roll(x0, 127, 1), pltpu.roll(x1, 127, 1)
                    w = (jnp.where(lane == 0, into_l, r0), jnp.where(lane == 0, r0, r1))
                    e = (jnp.where(lane == 127, l1, l0), jnp.where(lane == 127, into_r, l1))
                    for half in range(2):
                        c = (x0, x1)[half]
                        n = src[half, i, pl.ds(row - 1, 16), :]
                        s = src[half, i, pl.ds(row + 1, 16), :]
                        u, v = src[half, lev, at, :], src[half, 2 + lev, at, :]
                        lap = (e[half] + w[half]) + (n + s) - 4.0 * c
                        adv = u * (e[half] - w[half]) + v * (s - n)
                        new = wet[half, at, :] * (c + diff * lap - 0.05 * adv)
                        dst[half, i, pl.ds(row - shift, 16), :] = new
            return 0

        return body

    lax.fori_loop(0, 8, advance(now, later, sl0, sr0, 8, 17, 0), 0)
    advance_strips((sl0, sl1, wl), (sr0, sr1, wr))
    lax.fori_loop(0, 8, advance(later, now, sl1, sr1, 8, 17, 0), 0)
    advance_strips((sl1, sl0, wl), (sr1, sr0, wr))
    last = advance(now, final, sl0, sr0, 16, 16, 16)

    def every_fourth(half, i, j):
        return final[half, i, pl.ds(j, 64, stride=4), :]

    def send(k, half):
        cut = pl.ds(2 * k, 2)
        src, dst = final.at[half, cut], out.at[cut, :, pl.ds(128 * half, 128)]
        return pltpu.make_async_copy(src, dst, out_sem.at[k, half])

    def last_step(k, _):
        last(k, 0)
        for half in range(2):
            send(k, half).start()
        for lev in range(2):
            i = 2 * k + lev
            for half in range(2):
                total = every_fourth(half, i, 0)
                for j in range(1, 4):
                    total = total + every_fourth(half, i, j)
                for pr in range(4):
                    to = pl.multiple_of(((lev * 4 + pr) * 8 + k) * 16, 16)
                    sums[half, pl.ds(to, 16), :] = total[16 * pr : 16 * pr + 16]
        return 0

    lax.fori_loop(0, 8, last_step, 0)

    for lev in range(2):
        for half in range(2):
            for which in range(3):
                total = None
                for j in range(4):
                    if which < 2:
                        term = every_fourth(half, 2 * which + lev, j)
                        term = term * every_fourth(half, 4 + 2 * which + lev, j)
                    else:
                        term = wet[half, pl.ds(16 + j, 64, stride=4), :]
                    total = term if total is None else total + term
                for pr in range(4):
                    to = 1024 + ((lev * 4 + pr) * 8 + which) * 16
                    sums[half, to : to + 16, :] = total[16 * pr : 16 * pr + 16]

    table = gather[...]
    for half in range(2):
        for rows in range(2):
            for y in range(8):
                x = sums[half, pl.ds(8 * rows + y, 128, stride=16), :]
                a = x.astype(BF16)
                x = x - a.astype(F32)
                b = x.astype(BF16)
                c = (x - b.astype(F32)).astype(BF16)
                side = pl.ds(128 * y, 128)
                wide[0:128, side] = a
                wide[128:256, side] = b
                wide[256:384, side] = c
            r = jnp.dot(wide[...], table, preferred_element_type=F32)
            r = r[0:128] + r[128:256] + r[256:384]
            means, products = r[0:64], r[64:128]
            for q in range(8):
                m = means[8 * q : 8 * q + 8]
                p = products[8 * q : 8 * q + 8]
                sub = lax.broadcasted_iota(jnp.int32, (8, 256), 0)
                p = p - jnp.where(sub < 2, m * pltpu.roll(m, 6, 0), 0.0)
                both = jnp.concatenate([m, p], axis=0).astype(BF16)
                for pc in range(2):
                    to = pl.ds(128 * rows, 128)
                    patches[4 * q + 2 * half + pc, :, to] = both[:, 128 * pc : 128 * pc + 128]

    for j in range(32):
        chosen[j] = patches[slot[j]]

    return send


def add_up(my, mx, grads, got1, part, gotc, mine, got2, whole, sems):
    (s1, r1), (sc, rc), (s2, r2), (s3, r3), (s4, r4), (s5, r5) = sems
    core, place = lax.rem(mx, 2), mx // 2
    sibling = {"ty": my, "tx": mx + 1 - 2 * core}

    def copy(src, dst, send, recv, to):
        return pltpu.make_async_remote_copy(
            src_ref=src, dst_ref=dst, send_sem=send, recv_sem=recv, device_id=to, device_id_type=MESH
        )

    def rows(start, count):
        return pl.ds(pl.multiple_of(start, 8), count)

    def one(d):
        peer = lax.rem(my + d, NTY)
        src = grads.at[pl.ds(pl.multiple_of(CHUNK * peer, 16), CHUNK), :]
        return copy(src, got1.at[d], s1.at[d], r1.at[d], {"ty": peer, "tx": mx})

    for d in range(1, NTY):
        one(d).start()
    part[...] = grads[pl.ds(pl.multiple_of(CHUNK * my, 16), CHUNK), :].astype(F32)
    for d in range(1, NTY):
        one(d).wait_recv()
        part[...] += got1[d].astype(F32)

    pair = copy(part.at[rows(HALF * (1 - core), HALF), :], gotc, sc.at[0], rc.at[0], sibling)
    pair.start()
    pair.wait_recv()
    mine[...] = part[rows(HALF * core, HALF), :] + gotc[...]

    base = CHUNK * my + HALF * core

    def chip(index):
        return {"ty": my, "tx": 2 * index + core}

    def ahead(d):
        return lax.rem(place + d, NTY)

    def behind(d):
        return lax.rem(place + NTY - d, NTY)

    def two(d, piece):
        return copy(mine.at[rows(PIECE * piece, PIECE), :], got2.at[d], s2.at[d], r2.at[d], chip(ahead(d)))

    def three(d, owner, to):
        cut = whole.at[rows(base + PIECE * owner, PIECE), :]
        return copy(cut, cut, s3.at[d], r3.at[d], chip(to))

    for d in range(1, NTY):

        @pl.when(ahead(d) < OWNERS)
        def _(d=d):
            two(d, ahead(d)).start()

    @pl.when(place < OWNERS)
    def _():
        total = mine[rows(PIECE * place, PIECE), :]
        for d in range(1, NTY):
            two(d, 0).wait_recv()
            total = total + got2[d]
        whole[rows(base + PIECE * place, PIECE), :] = total
        for d in range(1, NTY):
            three(d, place, ahead(d)).start()

    for d in range(1, NTY):

        @pl.when(behind(d) < OWNERS)
        def _(d=d):
            three(d, behind(d), behind(d)).wait_recv()

    def four(d, source, peer):
        cut = whole.at[rows(CHUNK * source + HALF * core, HALF), :]
        return copy(cut, cut, s4.at[d], r4.at[d], {"ty": peer, "tx": mx})

    def five(d, half):
        source = lax.rem(my + NTY - d, NTY)
        cut = whole.at[rows(CHUNK * source + HALF * half, HALF), :]
        return copy(cut, cut, s5.at[d], r5.at[d], sibling)

    for d in range(1, NTY):
        four(d, my, lax.rem(my + d, NTY)).start()
    five(0, core).start()
    for d in range(1, NTY):
        source = lax.rem(my + NTY - d, NTY)
        four(d, source, source).wait_recv()
        five(d, core).start()
    for d in range(NTY):
        five(d, 1 - core).wait_recv()

    pair.wait_send()
    for d in range(NTY):
        five(d, core).wait_send()
    for d in range(1, NTY):
        one(d).wait_send()
        four(d, my, lax.rem(my + d, NTY)).wait_send()

        @pl.when(ahead(d) < OWNERS)
        def _(d=d):
            two(d, ahead(d)).wait_send()

        @pl.when(place < OWNERS)
        def _(d=d):
            three(d, place, ahead(d)).wait_send()


def contract(a, b, dim_a, dim_b):
    return lax.dot_general(
        a, b, (((dim_a,), (dim_b,)), ((), ())), preferred_element_type=F32
    )


def net_step(step, got, win, wmid, hs, ds, wback, wout8, amid, ain, aout, amis):
    size = GROUP * 256
    lane = lanes((8, size))
    col, row = lane & 15, (lane >> 4) & 15

    def inside(dy, dx):
        ok = None
        for value, change in ((row, dy), (col, dx)):
            if change:
                one = value >= 1 if change < 0 else value <= 14
                ok = one if ok is None else ok & one
        return ok

    def moved(a, dy, dx):
        off = 16 * dy + dx
        if off == 0:
            return a
        return jnp.where(inside(dy, dx), pltpu.roll(a, (-off) % size, 1), 0.0)

    side = lax.broadcasted_iota(jnp.int32, (size, 128), 0) & 15
    taps = wout8[...].astype(BF16)

    def spread(ref, a, sign):
        for j, dx in enumerate((-1, 0, 1)):
            go = sign * dx
            if go == 0:
                v = a
            elif go < 0:
                v = jnp.where(side == 0, 0.0, pltpu.roll(a, 1, 0))
            else:
                v = jnp.where(side == 15, 0.0, pltpu.roll(a, size - 1, 0))
            v = v.astype(BF16)
            for i, dy in enumerate((-1, 0, 1)):
                to = pl.ds(128 * (3 * i + j), 128)
                for p in range(GROUP):
                    b = 256 * p
                    if sign * dy == 0:
                        ref[b : b + 256, to] = v[b : b + 256]
                    elif sign * dy < 0:
                        ref[b + 16 : b + 256, to] = v[b : b + 240]
                    else:
                        ref[b : b + 240, to] = v[b + 16 : b + 256]

    def silu(z):
        s = 0.5 * jnp.tanh(0.5 * z) + 0.5
        h = z * s
        return h, s + h * (1.0 - s)

    def work(hs, ds, base):
        data = [got[base + p].astype(F32) for p in range(GROUP)]
        x = jnp.concatenate([d[0:8] for d in data], axis=1)
        lab = jnp.concatenate([d[8:16] for d in data], axis=1)
        xcat = jnp.concatenate([moved(x, dy, dx) for dy, dx in TAPS], axis=0).astype(BF16)
        z1 = contract(xcat, win[...], 0, 0)
        yield
        h1, slope1 = silu(z1)
        spread(hs, h1, 1)
        yield
        z2 = jnp.dot(hs[...], wmid[...], preferred_element_type=F32)
        yield
        h2, slope2 = silu(z2)
        h2 = h2.astype(BF16)
        parts = contract(taps, h2, 1, 1)
        yield
        y = jnp.zeros((8, size), F32)
        for t, (dy, dx) in enumerate(TAPS):
            y = y + moved(parts[8 * t : 8 * t + 8], dy, dx)
        sub = lax.broadcasted_iota(jnp.int32, (8, size), 0)
        diff = jnp.where(sub < 2, y - lab, 0.0)
        weighted = lab[2:3] * diff
        g = 2.0 * weighted
        gcat = jnp.concatenate([moved(g, -dy, -dx) for dy, dx in TAPS], axis=0).astype(BF16)
        dh2 = contract(gcat, taps, 0, 0).astype(BF16).astype(F32)
        yield
        dz2 = dh2 * slope2
        spread(ds, dz2, -1)
        yield
        dh1 = jnp.dot(ds[...], wback[...], preferred_element_type=F32).astype(BF16).astype(F32)
        yield
        dmid = contract(h1.astype(BF16), ds[...], 0, 0)
        yield
        dz1 = (dh1 * slope1).astype(BF16)
        dout = jnp.dot(gcat, h2, preferred_element_type=F32)
        din = jnp.dot(xcat, dz1, preferred_element_type=F32)
        yield weighted * diff, dmid, din, dout

    teams = [work(hs.at[i], ds.at[i], TEAMS * GROUP * step + GROUP * i) for i in range(TEAMS)]
    results = []
    while len(results) < TEAMS:
        for team in teams:
            value = next(team)
            if value is not None:
                results.append(value)
    for ref, parts in zip((amis, amid, ain, aout), zip(*results)):
        ref[...] += functools.reduce(jnp.add, parts)


def whole_kernel(
    rate, slot, fields, mask, gather, win, wmid, wout,
    out, misfit, first, mid, last,
    now, later, final, wet, sl0, sl1, sr0, sr1, wl, wr, packed, left, right, mtop, mbot,
    sums, wide, patches, chosen, got,
    hs, ds, wback, wout8, amid, ain, aout, amis,
    grads, got1, part, gotc, mine, got2, whole,
    in_sem, out_sem, halo_send, halo_recv, swap_send, swap_recv, *sems,
):
    my, mx = lax.axis_index("ty"), lax.axis_index("tx")
    loads = []
    for half in range(2):
        src = fields.at[:, :, pl.ds(128 * half, 128)]
        loads.append(pltpu.make_async_copy(src, now.at[half, :, pl.ds(16, 256), :], in_sem.at[half]))
        loads[-1].start()

    barrier = pltpu.get_barrier_semaphore()
    present, each, rows, sides = halo_copies(
        my, mx, fields, mask, now, packed, left, right, mtop, mbot, halo_send, halo_recv
    )
    count = jnp.int32(2 * NTY - 1)
    for a in (-1, 0, 1):
        for b in (-1, 0, 1):
            if a or b:
                here = present(a, b)
                count = count + here.astype(jnp.int32)

                @pl.when(here)
                def _(a=a, b=b):
                    to = {"ty": my + a, "tx": mx + b}
                    pl.semaphore_signal(barrier, inc=1, device_id=to, device_id_type=MESH)

    others = [{"ty": lax.rem(my + d, NTY), "tx": mx} for d in range(1, NTY)]
    others += [{"ty": my, "tx": lax.rem(mx + 2 * d, NTX)} for d in range(1, NTY)]
    others += [{"ty": my, "tx": mx + 1 - 2 * lax.rem(mx, 2)}]
    for to in others:
        pl.semaphore_signal(barrier, inc=1, device_id=to, device_id_type=MESH)

    @pl.when(my == 0)
    def _():
        now[:, :, 8:16, :] = jnp.zeros((2, 16, 8, 128), F32)
        mtop[...] = jnp.zeros_like(mtop)
        left[0:8, :] = jnp.zeros((8, 128), F32)
        right[0:8, :] = jnp.zeros((8, 128), F32)

    @pl.when(my == NTY - 1)
    def _():
        now[:, :, 272:280, :] = jnp.zeros((2, 16, 8, 128), F32)
        mbot[...] = jnp.zeros_like(mbot)
        left[264:272, :] = jnp.zeros((8, 128), F32)
        right[264:272, :] = jnp.zeros((8, 128), F32)

    @pl.when(mx == 0)
    def _():
        left[...] = jnp.zeros_like(left)

    @pl.when(mx == NTX - 1)
    def _():
        right[...] = jnp.zeros_like(right)

    for load in loads:
        load.wait()
    for block in range(2):
        lane = lanes((128, 128))
        at, to = pl.ds(128 * block, 128), pl.ds(16 + 128 * block, 128)
        edges = pack_edges(lambda i: (now[0, i, to, :], now[1, i, to, :]), lane)
        wet0 = mask[at, 0:128].astype(F32)
        wet1 = mask[at, 128:256].astype(F32)
        edges = jnp.where(lane == 0, pltpu.roll(wet1, 2, 1), edges)
        edges = jnp.where(lane == 8, pltpu.roll(wet1, 9, 1), edges)
        edges = jnp.where(lane == 7, pltpu.roll(wet0, 7, 1), edges)
        edges = jnp.where(lane == 15, pltpu.roll(wet0, 14, 1), edges)
        packed[to, :] = edges

    pl.semaphore_wait(barrier, count)
    start = lambda copy: copy.start()
    each(rows, start)
    each(sides, start)

    for half in range(2):
        wet[half, 16:272, :] = mask[:, 128 * half : 128 * half + 128].astype(F32)
        for buf in (now, later):
            buf[half, :, 0:8, :] = jnp.zeros((16, 8, 128), F32)
            buf[half, :, 280:288, :] = jnp.zeros((16, 8, 128), F32)
    for buf in (sl0, sr0, sl1, sr1):
        buf[0:8, :] = jnp.zeros((8, 128), F32)
        buf[280:288, :] = jnp.zeros((8, 128), F32)
    sums[:, 1024:2048, :] = jnp.zeros((2, 1024, 128), F32)
    for ref in (hs, ds, amid, ain, aout, amis):
        ref[...] = jnp.zeros_like(ref)
    for t in range(9):
        at = pl.ds(128 * t, 128)
        wback[at, :] = wmid[at, :].astype(F32).T.astype(BF16)
        wout8[8 * t : 8 * t + 8, :] = jnp.zeros((8, 128), F32)
        wout8[8 * t : 8 * t + 2, :] = wout[t].astype(F32)

    arrived = lambda copy: copy.wait_recv()
    each(rows, arrived, arriving=True)
    each(sides, arrived, arriving=True)
    for half in range(2):
        side = pl.ds(128 * half, 128)
        wet[half, 8:16, :] = mtop[:, side].astype(F32)
        wet[half, 272:280, :] = mbot[:, side].astype(F32)
    for at in (pl.ds(8, 8), pl.ds(272, 8)):
        packed[at, :] = pack_edges(lambda i: (now[0, i, at, :], now[1, i, at, :]), lanes((8, 128)))

    strips = (sl0, sl1, sr0, sr1, wl, wr)
    leaving = ocean_steps(
        rate, slot, packed, left, right, gather, out, chosen, now, later, final, wet, strips, sums, wide, patches, out_sem
    )

    def swap(d):
        peer = lax.rem(my + d, NTY)
        return pltpu.make_async_remote_copy(
            src_ref=chosen.at[pl.ds(4 * peer, 4)],
            dst_ref=got.at[pl.ds(4 * d, 4)],
            send_sem=swap_send.at[d],
            recv_sem=swap_recv.at[d],
            device_id={"ty": peer, "tx": mx},
            device_id_type=MESH,
        )

    for d in range(1, NTY):
        swap(d).start()
    for j in range(4):
        got[j] = chosen[4 * my + j]
    for d in range(1, NTY):
        swap(d).wait_recv()

    def step(index, _):
        net_step(index, got, win, wmid, hs, ds, wback, wout8, amid, ain, aout, amis)
        return 0

    lax.fori_loop(0, 32 // (GROUP * TEAMS), step, 0)
    for t in range(9):
        at = pl.ds(128 * t, 128)
        grads[at, :] = amid[:, at].astype(BF16)
    both = jnp.concatenate(
        [ain[...]] + [aout[8 * t : 8 * t + 2, :] for t in range(9)] + [jnp.zeros((38, 128), F32)],
        axis=0,
    )
    grads[1152:1280, :] = both.astype(BF16)
    misfit[...] = jnp.full((1, 1), jnp.sum(amis[...]) / 8192, F32)
    pairs = tuple(zip(sems[::2], sems[1::2]))
    add_up(my, mx, grads, got1, part, gotc, mine, got2, whole, pairs)

    def scale(start, rows):
        g = whole[start : start + rows, :]
        return lax.rsqrt(jnp.sum(g * g) / F32(rows * 128) + NORM_EPS)

    mid[...] = whole[0:1152, :] * scale(0, 1152)
    first[...] = whole[1152:1224, :] * scale(1152, 72)
    size = scale(1224, 18)
    for t in range(9):
        last[t] = whole[1224 + 2 * t : 1226 + 2 * t, :] * size

    sent = lambda copy: copy.wait_send()
    each(rows, sent)
    each(sides, sent)
    for d in range(1, NTY):
        swap(d).wait_send()
    for k in range(8):
        for half in range(2):
            leaving(k, half).wait()


def run(rate, slot, fields, mask, gather, win, wmid, wout):
    dma = pltpu.SemaphoreType.DMA
    f32 = lambda *shape: pltpu.VMEM(shape, F32)
    bf16 = lambda *shape: pltpu.VMEM(shape, BF16)
    return pl.pallas_call(
        whole_kernel,
        out_shape=(
            jax.ShapeDtypeStruct((16, 256, 256), F32),
            jax.ShapeDtypeStruct((1, 1), F32),
            jax.ShapeDtypeStruct((72, 128), F32),
            jax.ShapeDtypeStruct((1152, 128), F32),
            jax.ShapeDtypeStruct((9, 2, 128), F32),
        ),
        in_specs=[SMEM, SMEM, ANY, VMEM, VMEM, VMEM, VMEM, VMEM],
        out_specs=(ANY, VMEM, VMEM, VMEM, VMEM),
        scratch_shapes=[
            f32(2, 16, 288, 128),
            f32(2, 16, 288, 128),
            f32(2, 16, 256, 128),
            f32(2, 288, 128),
        ]
        + [f32(288, 128)] * 7
        + [
            f32(272, 128),
            f32(272, 128),
            pltpu.VMEM((8, 256), jnp.int32),
            pltpu.VMEM((8, 256), jnp.int32),
            f32(2, 2048, 128),
            bf16(384, 1024),
            bf16(32, 16, 256),
            bf16(32, 16, 256),
            bf16(32, 16, 256),
            bf16(TEAMS, GROUP * 256, 1152),
            bf16(TEAMS, GROUP * 256, 1152),
            bf16(1152, 128),
            f32(72, 128),
            f32(128, 1152),
            f32(72, 128),
            f32(72, 128),
            f32(8, GROUP * 256),
            bf16(ROWS, 128),
            bf16(NTY, CHUNK, 128),
            f32(CHUNK, 128),
            f32(HALF, 128),
            f32(HALF, 128),
            f32(NTY, PIECE, 128),
            f32(ROWS, 128),
            dma((2,)),
            dma((8, 2)),
            dma((12,)),
            dma((12,)),
        ]
        + [dma((NTY,)) for _ in range(14)],
        compiler_params=pltpu.CompilerParams(
            collective_id=0, has_side_effects=True, vmem_limit_bytes=60 << 20
        ),
        name="whole",
    )(rate, slot, fields, mask, gather, win, wmid, wout)


def per_device(fields, ocean_mask, diffusivity, patch_slot_assignment, conv_in, conv_mid, conv_out):
    current, member_loss, first, mid, last = run(
        diffusivity,
        patch_slot_assignment.reshape(32),
        fields.reshape(16, 256, 256),
        ocean_mask,
        jnp.asarray(coarse_matrix()),
        conv_in.reshape(72, 128),
        conv_mid.reshape(1152, 128),
        conv_out.reshape(9, 128, 2).transpose(0, 2, 1),
    )
    return (
        current.reshape(fields.shape),
        member_loss,
        first.reshape(conv_in.shape),
        mid.reshape(conv_mid.shape),
        last.transpose(0, 2, 1).reshape(conv_out.shape),
    )


def solution(mesh):
    placed = (P(None, None, "ty", "tx"), P("ty", "tx"), P(), P("ty", "tx", None), P(), P(), P())
    return jax.shard_map(
        per_device,
        mesh=mesh,
        in_specs=placed,
        out_specs=(P(None, None, "ty", "tx"), P("ty", "tx"), P(), P(), P()),
        check_vma=False,
    )
```

```python
import functools

import jax
import jax.numpy as jnp
import ml_dtypes
import numpy as np
from jax import lax
from jax.experimental import pallas as pl
from jax.experimental.pallas import tpu as pltpu
from jax.sharding import PartitionSpec as P

F32 = jnp.float32
BF16 = jnp.bfloat16
MESH = pl.DeviceIdType.MESH
NTY, NTX = 8, 16
ROWS = 1280
CHUNK = ROWS // NTY
PIECE = 16
HALF = CHUNK // 2
OWNERS = HALF // PIECE
GROUP = 4
TEAMS = 2
TAPS = [(i - 1, j - 1) for i in range(3) for j in range(3)]
NORM_EPS = 1e-6
ANY = pl.BlockSpec(memory_space=pl.ANY)
VMEM = pl.BlockSpec(memory_space=pltpu.VMEM)
SMEM = pl.BlockSpec(memory_space=pltpu.SMEM)


def lanes(shape):
    return lax.broadcasted_iota(jnp.int32, shape, len(shape) - 1)


def pack_edges(field, lane):
    packed = None
    for i in range(16):
        first, last = field(i)
        edge = pltpu.roll(jnp.where(lane >= 124, last, first), (8 * i + 4) % 128, 1)
        packed = edge if packed is None else jnp.where(lane >= 8 * i, edge, packed)
    return packed


def coarse_matrix():
    matrix = np.zeros((8, 128, 2, 8, 16), np.float32)
    for row in range(8):
        for column in range(128):
            matrix[row, column, column // 64, row, (column % 64) // 4] = 1 / 16
    return matrix.reshape(1024, 256).astype(ml_dtypes.bfloat16)


def halo_copies(my, mx, fields, mask, now, packed, left, right, mtop, mbot, send, recv):
    def present(a, b):
        ok = None
        for at, change, count in ((my, a, NTY), (mx, b, NTX)):
            if change:
                one = at > 0 if change < 0 else at < count - 1
                ok = one if ok is None else jnp.logical_and(ok, one)
        return ok

    rows = []
    for half in range(2):
        side = pl.ds(128 * half, 128)
        rows.append((fields.at[:, pl.ds(248, 8), side], now.at[half, :, pl.ds(8, 8), :], 1, 0))
        rows.append((fields.at[:, pl.ds(0, 8), side], now.at[half, :, pl.ds(272, 8), :], -1, 0))
    rows.append((mask.at[pl.ds(248, 8), :], mtop, 1, 0))
    rows.append((mask.at[pl.ds(0, 8), :], mbot, -1, 0))
    sides = [
        (packed.at[pl.ds(16, 256), :], left.at[pl.ds(8, 256), :], 0, 1),
        (packed.at[pl.ds(16, 256), :], right.at[pl.ds(8, 256), :], 0, -1),
        (packed.at[pl.ds(264, 8), :], left.at[pl.ds(0, 8), :], 1, 1),
        (packed.at[pl.ds(16, 8), :], left.at[pl.ds(264, 8), :], -1, 1),
        (packed.at[pl.ds(264, 8), :], right.at[pl.ds(0, 8), :], 1, -1),
        (packed.at[pl.ds(16, 8), :], right.at[pl.ds(264, 8), :], -1, -1),
    ]

    def copy(index):
        src, dst, a, b = (rows + sides)[index]
        return pltpu.make_async_remote_copy(
            src_ref=src,
            dst_ref=dst,
            send_sem=send.at[index],
            recv_sem=recv.at[index],
            device_id={"ty": my + a, "tx": mx + b},
            device_id_type=MESH,
        )

    def each(indices, act, arriving=False):
        for index in indices:
            a, b = (rows + sides)[index][2:]

            @pl.when(present(-a, -b) if arriving else present(a, b))
            def _(index=index):
                act(copy(index))

    return present, each, range(len(rows)), range(len(rows), len(rows) + len(sides))


def advance(rate, wet, uv, src, dst, low, high, starts, shift):
    def body(k, _):
        diff = rate[k]
        keep = 1.0 - 4.0 * diff
        for row in starts:
            at = pl.ds(row, 16)
            lane = lanes((16, 128))
            for lev in range(2):
                i = 2 * k + lev
                x0, x1 = src[0, i, at, :], src[1, i, at, :]
                r0, r1 = pltpu.roll(x0, 1, 1), pltpu.roll(x1, 1, 1)
                l0, l1 = pltpu.roll(x0, 127, 1), pltpu.roll(x1, 127, 1)
                into_l, into_r = r0, l1
                if low is not None:
                    into_l = jnp.where(lane == 0, pltpu.roll(low[at, :], 125 - 8 * i, 1), r0)
                    into_r = jnp.where(lane == 127, pltpu.roll(high[at, :], 123 - 8 * i, 1), l1)
                w = (into_l, jnp.where(lane == 0, r0, r1))
                e = (jnp.where(lane == 127, l1, l0), into_r)
                for half in range(2):
                    c = (x0, x1)[half]
                    n = src[half, i, pl.ds(row - 1, 16), :]
                    s = src[half, i, pl.ds(row + 1, 16), :]
                    u, v = uv[half, lev, at, :], uv[half, 2 + lev, at, :]
                    near = (e[half] + w[half]) + (n + s)
                    adv = u * (e[half] - w[half]) + v * (s - n)
                    new = wet[half, at, :] * (c * keep + diff * near - adv)
                    dst[half, i, pl.ds(row - shift, 16), :] = new
        return 0

    return body


def velocities(uv, src, start, rows):
    at = pl.ds(start, rows)
    for half in range(2):
        uv[half, :, at, :] = 0.05 * src[half, 0:4, at, :]


def ocean_steps(rate, slot, packed, left, right, gather, out, chosen, now, later, final, wet, uv, strips, sums, wide, patches, out_sem):
    sl0, sl1, sr0, sr1, wl, wr = strips
    lane = lanes((136, 128))
    blocks = [(8 + 136 * b, pl.ds(8 + 136 * b, 136)) for b in range(2)]
    inner = (lane & 7) < 4
    for row, at in blocks:
        got_rows = pl.ds(row - 8, 136)
        own = packed[at, :]
        west, east = left[got_rows, :], right[got_rows, :]
        sl0[at, :] = jnp.where(inner, west, own)
        sr0[at, :] = jnp.where(inner, own, east)
        wet0, wet1 = wet[0, at, :], wet[1, at, :]
        low = jnp.where((lane >= 4) & (lane < 8), pltpu.roll(wet0, 4, 1), 0.0)
        low = jnp.where(lane == 2, pltpu.roll(west, 2, 1), low)
        low = jnp.where(lane == 3, pltpu.roll(west, 123, 1), low)
        high = jnp.where(lane < 4, pltpu.roll(wet1, 4, 1), 0.0)
        high = jnp.where(lane == 4, pltpu.roll(east, 125, 1), high)
        high = jnp.where(lane == 5, pltpu.roll(east, 118, 1), high)
        for shift in (8, 16, 32, 64):
            low = low + pltpu.roll(low, shift, 1)
            high = high + pltpu.roll(high, shift, 1)
        wl[at, :] = low
        wr[at, :] = high

    level = jnp.zeros((1, 128), F32)
    for k in range(8):
        level = jnp.where(lanes((1, 128)) >> 4 == k, rate[k], level)

    def advance_strips(*sides):
        for row, at in blocks:
            for src, dst, cells in sides:
                c = src[at, :]
                u = jnp.where(lane < 16, c, 0.0)
                v = jnp.where((lane >= 16) & (lane < 32), c, 0.0)
                for shift in (16, 32, 64):
                    u = u + pltpu.roll(u, shift, 1)
                    v = v + pltpu.roll(v, shift, 1)
                e, w = pltpu.roll(c, 127, 1), pltpu.roll(c, 1, 1)
                n, s = src[pl.ds(row - 1, 136), :], src[pl.ds(row + 1, 136), :]
                lap = (e + w) + (n + s) - 4.0 * c
                adv = u * (e - w) + v * (s - n)
                dst[at, :] = cells[at, :] * (c + level * lap - 0.05 * adv)

    velocities(uv, now, 8, 16)
    velocities(uv, now, 264, 16)
    lax.fori_loop(0, 8, advance(rate, wet, uv, now, later, sl0, sr0, (8, 264), 0), 0)
    advance_strips((sl0, sl1, wl), (sr0, sr1, wr))
    line = lanes((80, 128))

    def mend(k, _):
        for i in (2 * k, 2 * k + 1):
            for block in range(3):
                at = pl.ds(24 + 80 * block, 80)
                for half, strip, edge in ((0, sl1, 0), (1, sr1, 127)):
                    outer = pltpu.roll(strip[at, :], 124 - 8 * i, 1)
                    later[half, i, at, :] = jnp.where(line == edge, outer, later[half, i, at, :])
        return 0

    lax.fori_loop(0, 8, mend, 0)
    velocities(uv, later, 8, 272)
    every = tuple(range(8, 280, 16))
    lax.fori_loop(0, 8, advance(rate, wet, uv, later, now, sl1, sr1, every, 0), 0)
    advance_strips((sl1, sl0, wl), (sr1, sr0, wr))
    velocities(uv, now, 16, 256)
    last = advance(rate, wet, uv, now, final, sl0, sr0, tuple(range(16, 272, 16)), 16)

    def every_fourth(half, i, j):
        return final[half, i, pl.ds(j, 64, stride=4), :]

    def send(k, half):
        cut = pl.ds(2 * k, 2)
        src, dst = final.at[half, cut], out.at[cut, :, pl.ds(128 * half, 128)]
        return pltpu.make_async_copy(src, dst, out_sem.at[k, half])

    def last_step(k, _):
        last(k, 0)
        for half in range(2):
            send(k, half).start()
        for lev in range(2):
            i = 2 * k + lev
            for half in range(2):
                total = every_fourth(half, i, 0)
                for j in range(1, 4):
                    total = total + every_fourth(half, i, j)
                for pr in range(4):
                    to = pl.multiple_of(((lev * 4 + pr) * 8 + k) * 16, 16)
                    sums[half, pl.ds(to, 16), :] = total[16 * pr : 16 * pr + 16]
        return 0

    lax.fori_loop(0, 8, last_step, 0)

    for lev in range(2):
        for half in range(2):
            for which in range(3):
                total = None
                for j in range(4):
                    if which < 2:
                        term = every_fourth(half, 2 * which + lev, j)
                        term = term * every_fourth(half, 4 + 2 * which + lev, j)
                    else:
                        term = wet[half, pl.ds(16 + j, 64, stride=4), :]
                    total = term if total is None else total + term
                for pr in range(4):
                    to = 1024 + ((lev * 4 + pr) * 8 + which) * 16
                    sums[half, to : to + 16, :] = total[16 * pr : 16 * pr + 16]

    table = gather[...]
    for half in range(2):
        for rows in range(2):
            for y in range(8):
                x = sums[half, pl.ds(8 * rows + y, 128, stride=16), :]
                a = x.astype(BF16)
                x = x - a.astype(F32)
                b = x.astype(BF16)
                c = (x - b.astype(F32)).astype(BF16)
                side = pl.ds(128 * y, 128)
                wide[0:128, side] = a
                wide[128:256, side] = b
                wide[256:384, side] = c
            r = jnp.dot(wide[...], table, preferred_element_type=F32)
            r = r[0:128] + r[128:256] + r[256:384]
            means, products = r[0:64], r[64:128]
            for q in range(8):
                m = means[8 * q : 8 * q + 8]
                p = products[8 * q : 8 * q + 8]
                sub = lax.broadcasted_iota(jnp.int32, (8, 256), 0)
                p = p - jnp.where(sub < 2, m * pltpu.roll(m, 6, 0), 0.0)
                both = jnp.concatenate([m, p], axis=0).astype(BF16)
                for pc in range(2):
                    to = pl.ds(128 * rows, 128)
                    patches[4 * q + 2 * half + pc, :, to] = both[:, 128 * pc : 128 * pc + 128]

    for j in range(32):
        chosen[j] = patches[slot[j]]

    return send


def add_up(my, mx, grads, got1, part, got2, whole, sems):
    (s1, r1), (s2, r2), (s3, r3), (s4, r4), (s5, r5) = sems
    core, place = lax.rem(mx, 2), mx // 2
    sibling = {"ty": my, "tx": mx + 1 - 2 * core}

    def copy(src, dst, send, recv, to):
        return pltpu.make_async_remote_copy(
            src_ref=src, dst_ref=dst, send_sem=send, recv_sem=recv, device_id=to, device_id_type=MESH
        )

    def rows(start, count):
        return pl.ds(pl.multiple_of(start, 8), count)

    def one(d):
        peer = lax.rem(my + d, NTY)
        src = grads.at[pl.ds(pl.multiple_of(CHUNK * peer, 16), CHUNK), :]
        return copy(src, got1.at[d], s1.at[d], r1.at[d], {"ty": peer, "tx": mx})

    for d in range(1, NTY):
        one(d).start()
    part[...] = grads[pl.ds(pl.multiple_of(CHUNK * my, 16), CHUNK), :].astype(F32)
    for d in range(1, NTY):
        one(d).wait_recv()
        part[...] += got1[d].astype(F32)

    base = CHUNK * my + HALF * core

    def chip(index):
        return {"ty": my, "tx": 2 * index + core}

    def ahead(d):
        return lax.rem(place + d, NTY)

    def behind(d):
        return lax.rem(place + NTY - d, NTY)

    def two(d, start):
        to = {"ty": my, "tx": lax.rem(mx + d, NTX)}
        return copy(part.at[rows(start, PIECE), :], got2.at[d], s2.at[d], r2.at[d], to)

    def piece_of(device):
        return HALF * lax.rem(device, 2) + PIECE * (device // 2)

    def three(d, owner, to):
        cut = whole.at[rows(base + PIECE * owner, PIECE), :]
        return copy(cut, cut, s3.at[d], r3.at[d], chip(to))

    for d in range(1, NTX):
        peer = lax.rem(mx + d, NTX)

        @pl.when(peer // 2 < OWNERS)
        def _(d=d, peer=peer):
            two(d, piece_of(peer)).start()

    @pl.when(place < OWNERS)
    def _():
        total = part[rows(piece_of(mx), PIECE), :]
        for d in range(1, NTX):
            two(d, 0).wait_recv()
            total = total + got2[d]
        whole[rows(base + PIECE * place, PIECE), :] = total
        for d in range(1, NTY):
            three(d, place, ahead(d)).start()

    for d in range(1, NTY):

        @pl.when(behind(d) < OWNERS)
        def _(d=d):
            three(d, behind(d), behind(d)).wait_recv()

    def four(d, source, peer):
        cut = whole.at[rows(CHUNK * source + HALF * core, HALF), :]
        return copy(cut, cut, s4.at[d], r4.at[d], {"ty": peer, "tx": mx})

    def five(d, half):
        source = lax.rem(my + NTY - d, NTY)
        cut = whole.at[rows(CHUNK * source + HALF * half, HALF), :]
        return copy(cut, cut, s5.at[d], r5.at[d], sibling)

    for d in range(1, NTY):
        four(d, my, lax.rem(my + d, NTY)).start()
    five(0, core).start()
    for d in range(1, NTY):
        source = lax.rem(my + NTY - d, NTY)
        four(d, source, source).wait_recv()
        five(d, core).start()
    for d in range(NTY):
        five(d, 1 - core).wait_recv()

    for d in range(NTY):
        five(d, core).wait_send()
    for d in range(1, NTX):
        peer = lax.rem(mx + d, NTX)

        @pl.when(peer // 2 < OWNERS)
        def _(d=d, peer=peer):
            two(d, piece_of(peer)).wait_send()

    for d in range(1, NTY):
        one(d).wait_send()
        four(d, my, lax.rem(my + d, NTY)).wait_send()

        @pl.when(place < OWNERS)
        def _(d=d):
            three(d, place, ahead(d)).wait_send()


def contract(a, b, dim_a, dim_b):
    return lax.dot_general(
        a, b, (((dim_a,), (dim_b,)), ((), ())), preferred_element_type=F32
    )


def net_step(step, got, win, wmid, hs, ds, wback, wout8, amid, ain, aout, amis):
    size = GROUP * 256
    lane = lanes((8, size))
    col, row = lane & 15, (lane >> 4) & 15

    def inside(dy, dx):
        ok = None
        for value, change in ((row, dy), (col, dx)):
            if change:
                one = value >= 1 if change < 0 else value <= 14
                ok = one if ok is None else ok & one
        return ok

    def moved(a, dy, dx):
        off = 16 * dy + dx
        if off == 0:
            return a
        return jnp.where(inside(dy, dx), pltpu.roll(a, (-off) % size, 1), 0.0)

    side = lax.broadcasted_iota(jnp.int32, (size, 128), 0) & 15
    taps = wout8[...].astype(BF16)

    def spread(ref, a, sign):
        for j, dx in enumerate((-1, 0, 1)):
            go = sign * dx
            if go == 0:
                v = a
            elif go < 0:
                v = jnp.where(side == 0, 0.0, pltpu.roll(a, 1, 0))
            else:
                v = jnp.where(side == 15, 0.0, pltpu.roll(a, size - 1, 0))
            v = v.astype(BF16)
            for i, dy in enumerate((-1, 0, 1)):
                to = pl.ds(128 * (3 * i + j), 128)
                for p in range(GROUP):
                    b = 256 * p
                    if sign * dy == 0:
                        ref[b : b + 256, to] = v[b : b + 256]
                    elif sign * dy < 0:
                        ref[b + 16 : b + 256, to] = v[b : b + 240]
                    else:
                        ref[b : b + 240, to] = v[b + 16 : b + 256]

    def silu(z):
        s = 0.5 * jnp.tanh(0.5 * z) + 0.5
        h = z * s
        return h, s + h * (1.0 - s)

    def work(hs, ds, base):
        data = [got[base + p].astype(F32) for p in range(GROUP)]
        x = jnp.concatenate([d[0:8] for d in data], axis=1)
        lab = jnp.concatenate([d[8:16] for d in data], axis=1)
        xcat = jnp.concatenate([moved(x, dy, dx) for dy, dx in TAPS], axis=0).astype(BF16)
        z1 = contract(xcat, win[...], 0, 0)
        yield
        h1, slope1 = silu(z1)
        spread(hs, h1, 1)
        yield
        z2 = jnp.dot(hs[...], wmid[...], preferred_element_type=F32)
        yield
        h2, slope2 = silu(z2)
        h2 = h2.astype(BF16)
        parts = contract(taps, h2, 1, 1)
        yield
        y = jnp.zeros((8, size), F32)
        for t, (dy, dx) in enumerate(TAPS):
            y = y + moved(parts[8 * t : 8 * t + 8], dy, dx)
        sub = lax.broadcasted_iota(jnp.int32, (8, size), 0)
        diff = jnp.where(sub < 2, y - lab, 0.0)
        weighted = lab[2:3] * diff
        g = 2.0 * weighted
        gcat = jnp.concatenate([moved(g, -dy, -dx) for dy, dx in TAPS], axis=0).astype(BF16)
        dh2 = contract(gcat, taps, 0, 0).astype(BF16).astype(F32)
        yield
        dz2 = dh2 * slope2
        spread(ds, dz2, -1)
        yield
        dh1 = jnp.dot(ds[...], wback[...], preferred_element_type=F32).astype(BF16).astype(F32)
        yield
        dmid = contract(h1.astype(BF16), ds[...], 0, 0)
        yield
        dz1 = (dh1 * slope1).astype(BF16)
        dout = jnp.dot(gcat, h2, preferred_element_type=F32)
        din = jnp.dot(xcat, dz1, preferred_element_type=F32)
        yield weighted * diff, dmid, din, dout

    teams = [work(hs.at[i], ds.at[i], TEAMS * GROUP * step + GROUP * i) for i in range(TEAMS)]
    results = []
    while len(results) < TEAMS:
        for team in teams:
            value = next(team)
            if value is not None:
                results.append(value)
    for ref, parts in zip((amis, amid, ain, aout), zip(*results)):
        ref[...] += functools.reduce(jnp.add, parts)


def whole_kernel(
    rate, slot, fields, mask, gather, win, wmid, wout,
    out, misfit, first, mid, last,
    now, later, final, wet, uv, sl0, sl1, sr0, sr1, wl, wr, packed, left, right, mtop, mbot,
    sums, wide, patches, chosen, got,
    hs, ds, wback, wout8, amid, ain, aout, amis,
    grads, got1, part, got2, whole,
    in_sem, out_sem, halo_send, halo_recv, swap_send, swap_recv, *sems,
):
    my, mx = lax.axis_index("ty"), lax.axis_index("tx")
    loads = []
    for half in range(2):
        src = fields.at[:, :, pl.ds(128 * half, 128)]
        loads.append(pltpu.make_async_copy(src, now.at[half, :, pl.ds(16, 256), :], in_sem.at[half]))
        loads[-1].start()

    barrier = pltpu.get_barrier_semaphore()
    present, each, rows, sides = halo_copies(
        my, mx, fields, mask, now, packed, left, right, mtop, mbot, halo_send, halo_recv
    )
    count = jnp.int32(NTY + NTX - 2)
    for a in (-1, 0, 1):
        for b in (-1, 0, 1):
            if a or b:
                here = present(a, b)
                count = count + here.astype(jnp.int32)

                @pl.when(here)
                def _(a=a, b=b):
                    to = {"ty": my + a, "tx": mx + b}
                    pl.semaphore_signal(barrier, inc=1, device_id=to, device_id_type=MESH)

    others = [{"ty": lax.rem(my + d, NTY), "tx": mx} for d in range(1, NTY)]
    others += [{"ty": my, "tx": lax.rem(mx + d, NTX)} for d in range(1, NTX)]
    for to in others:
        pl.semaphore_signal(barrier, inc=1, device_id=to, device_id_type=MESH)

    @pl.when(my == 0)
    def _():
        now[:, :, 8:16, :] = jnp.zeros((2, 16, 8, 128), F32)
        mtop[...] = jnp.zeros_like(mtop)
        left[0:8, :] = jnp.zeros((8, 128), F32)
        right[0:8, :] = jnp.zeros((8, 128), F32)

    @pl.when(my == NTY - 1)
    def _():
        now[:, :, 272:280, :] = jnp.zeros((2, 16, 8, 128), F32)
        mbot[...] = jnp.zeros_like(mbot)
        left[264:272, :] = jnp.zeros((8, 128), F32)
        right[264:272, :] = jnp.zeros((8, 128), F32)

    @pl.when(mx == 0)
    def _():
        left[...] = jnp.zeros_like(left)

    @pl.when(mx == NTX - 1)
    def _():
        right[...] = jnp.zeros_like(right)

    for load in loads:
        load.wait()
    for block in range(2):
        lane = lanes((128, 128))
        at, to = pl.ds(128 * block, 128), pl.ds(16 + 128 * block, 128)
        edges = pack_edges(lambda i: (now[0, i, to, :], now[1, i, to, :]), lane)
        wet0 = mask[at, 0:128].astype(F32)
        wet1 = mask[at, 128:256].astype(F32)
        edges = jnp.where(lane == 0, pltpu.roll(wet1, 2, 1), edges)
        edges = jnp.where(lane == 8, pltpu.roll(wet1, 9, 1), edges)
        edges = jnp.where(lane == 7, pltpu.roll(wet0, 7, 1), edges)
        edges = jnp.where(lane == 15, pltpu.roll(wet0, 14, 1), edges)
        packed[to, :] = edges

    pl.semaphore_wait(barrier, count)
    start = lambda copy: copy.start()
    each(rows, start)
    each(sides, start)

    for half in range(2):
        wet[half, 16:272, :] = mask[:, 128 * half : 128 * half + 128].astype(F32)
        for buf in (now, later):
            buf[half, :, 0:8, :] = jnp.zeros((16, 8, 128), F32)
            buf[half, :, 280:288, :] = jnp.zeros((16, 8, 128), F32)
    for buf in (sl0, sr0, sl1, sr1):
        buf[0:8, :] = jnp.zeros((8, 128), F32)
        buf[280:288, :] = jnp.zeros((8, 128), F32)
    sums[:, 1024:2048, :] = jnp.zeros((2, 1024, 128), F32)
    for ref in (hs, ds, amid, ain, aout, amis):
        ref[...] = jnp.zeros_like(ref)
    for t in range(9):
        at = pl.ds(128 * t, 128)
        wback[at, :] = wmid[at, :].astype(F32).T.astype(BF16)
        wout8[8 * t : 8 * t + 8, :] = jnp.zeros((8, 128), F32)
        wout8[8 * t : 8 * t + 2, :] = wout[t].astype(F32)

    velocities(uv, now, 24, 240)
    inner = tuple(range(24, 264, 16))
    lax.fori_loop(0, 8, advance(rate, wet, uv, now, later, None, None, inner, 0), 0)

    arrived = lambda copy: copy.wait_recv()
    each(rows, arrived, arriving=True)
    each(sides, arrived, arriving=True)
    for half in range(2):
        side = pl.ds(128 * half, 128)
        wet[half, 8:16, :] = mtop[:, side].astype(F32)
        wet[half, 272:280, :] = mbot[:, side].astype(F32)
    for at in (pl.ds(8, 8), pl.ds(272, 8)):
        packed[at, :] = pack_edges(lambda i: (now[0, i, at, :], now[1, i, at, :]), lanes((8, 128)))

    strips = (sl0, sl1, sr0, sr1, wl, wr)
    leaving = ocean_steps(
        rate, slot, packed, left, right, gather, out, chosen, now, later, final, wet, uv, strips, sums, wide, patches, out_sem
    )

    def swap(d):
        peer = lax.rem(my + d, NTY)
        return pltpu.make_async_remote_copy(
            src_ref=chosen.at[pl.ds(4 * peer, 4)],
            dst_ref=got.at[pl.ds(4 * d, 4)],
            send_sem=swap_send.at[d],
            recv_sem=swap_recv.at[d],
            device_id={"ty": peer, "tx": mx},
            device_id_type=MESH,
        )

    for d in range(1, NTY):
        swap(d).start()
    for j in range(4):
        got[j] = chosen[4 * my + j]

    def step(index, _):
        for i in range(NTY // TEAMS):

            @pl.when(index == i)
            def _(i=i):
                for d in range(max(1, TEAMS * i), TEAMS * (i + 1)):
                    swap(d).wait_recv()

        net_step(index, got, win, wmid, hs, ds, wback, wout8, amid, ain, aout, amis)
        return 0

    lax.fori_loop(0, 32 // (GROUP * TEAMS), step, 0)
    for t in range(9):
        at = pl.ds(128 * t, 128)
        grads[at, :] = amid[:, at].astype(BF16)
    both = jnp.concatenate(
        [ain[...]] + [aout[8 * t : 8 * t + 2, :] for t in range(9)] + [jnp.zeros((38, 128), F32)],
        axis=0,
    )
    grads[1152:1280, :] = both.astype(BF16)
    misfit[...] = jnp.full((1, 1), jnp.sum(amis[...]) / 8192, F32)
    pairs = tuple(zip(sems[::2], sems[1::2]))
    add_up(my, mx, grads, got1, part, got2, whole, pairs)

    def scale(start, rows):
        g = whole[start : start + rows, :]
        return lax.rsqrt(jnp.sum(g * g) / F32(rows * 128) + NORM_EPS)

    mid[...] = whole[0:1152, :] * scale(0, 1152)
    first[...] = whole[1152:1224, :] * scale(1152, 72)
    size = scale(1224, 18)
    for t in range(9):
        last[t] = whole[1224 + 2 * t : 1226 + 2 * t, :] * size

    sent = lambda copy: copy.wait_send()
    each(rows, sent)
    each(sides, sent)
    for d in range(1, NTY):
        swap(d).wait_send()
    for k in range(8):
        for half in range(2):
            leaving(k, half).wait()


def run(rate, slot, fields, mask, gather, win, wmid, wout):
    dma = pltpu.SemaphoreType.DMA
    f32 = lambda *shape: pltpu.VMEM(shape, F32)
    bf16 = lambda *shape: pltpu.VMEM(shape, BF16)
    return pl.pallas_call(
        whole_kernel,
        out_shape=(
            jax.ShapeDtypeStruct((16, 256, 256), F32),
            jax.ShapeDtypeStruct((1, 1), F32),
            jax.ShapeDtypeStruct((72, 128), F32),
            jax.ShapeDtypeStruct((1152, 128), F32),
            jax.ShapeDtypeStruct((9, 2, 128), F32),
        ),
        in_specs=[SMEM, SMEM, ANY, VMEM, VMEM, VMEM, VMEM, VMEM],
        out_specs=(ANY, VMEM, VMEM, VMEM, VMEM),
        scratch_shapes=[
            f32(2, 16, 288, 128),
            f32(2, 16, 288, 128),
            f32(2, 16, 256, 128),
            f32(2, 288, 128),
            f32(2, 4, 288, 128),
        ]
        + [f32(288, 128)] * 7
        + [
            f32(272, 128),
            f32(272, 128),
            pltpu.VMEM((8, 256), jnp.int32),
            pltpu.VMEM((8, 256), jnp.int32),
            f32(2, 2048, 128),
            bf16(384, 1024),
            bf16(32, 16, 256),
            bf16(32, 16, 256),
            bf16(32, 16, 256),
            bf16(TEAMS, GROUP * 256, 1152),
            bf16(TEAMS, GROUP * 256, 1152),
            bf16(1152, 128),
            f32(72, 128),
            f32(128, 1152),
            f32(72, 128),
            f32(72, 128),
            f32(8, GROUP * 256),
            bf16(ROWS, 128),
            bf16(NTY, CHUNK, 128),
            f32(CHUNK, 128),
            f32(NTX, PIECE, 128),
            f32(ROWS, 128),
            dma((2,)),
            dma((8, 2)),
            dma((12,)),
            dma((12,)),
        ]
        + [dma((n,)) for n in (NTY, NTY, NTY, NTY, NTX, NTX) + (NTY,) * 6],
        compiler_params=pltpu.CompilerParams(
            collective_id=0, has_side_effects=True, vmem_limit_bytes=60 << 20
        ),
        name="whole",
    )(rate, slot, fields, mask, gather, win, wmid, wout)


def per_device(fields, ocean_mask, diffusivity, patch_slot_assignment, conv_in, conv_mid, conv_out):
    current, member_loss, first, mid, last = run(
        diffusivity,
        patch_slot_assignment.reshape(32),
        fields.reshape(16, 256, 256),
        ocean_mask,
        jnp.asarray(coarse_matrix()),
        conv_in.reshape(72, 128),
        conv_mid.reshape(1152, 128),
        conv_out.reshape(9, 128, 2).transpose(0, 2, 1),
    )
    return (
        current.reshape(fields.shape),
        member_loss,
        first.reshape(conv_in.shape),
        mid.reshape(conv_mid.shape),
        last.transpose(0, 2, 1).reshape(conv_out.shape),
    )


def solution(mesh):
    placed = (P(None, None, "ty", "tx"), P("ty", "tx"), P(), P("ty", "tx", None), P(), P(), P())
    return jax.shard_map(
        per_device,
        mesh=mesh,
        in_specs=placed,
        out_specs=(P(None, None, "ty", "tx"), P("ty", "tx"), P(), P(), P()),
        check_vma=False,
    )
```

```python
import functools

import jax
import jax.numpy as jnp
import ml_dtypes
import numpy as np
from jax import lax
from jax.experimental import pallas as pl
from jax.experimental.pallas import tpu as pltpu
from jax.sharding import PartitionSpec as P

F32 = jnp.float32
BF16 = jnp.bfloat16
MESH = pl.DeviceIdType.MESH
NTY, NTX = 8, 16
ROWS = 1280
CHUNK = ROWS // NTY
PIECE = 16
HALF = CHUNK // 2
OWNERS = HALF // PIECE
GROUP = 4
TEAMS = 2
TAPS = [(i - 1, j - 1) for i in range(3) for j in range(3)]
NORM_EPS = 1e-6
ANY = pl.BlockSpec(memory_space=pl.ANY)
VMEM = pl.BlockSpec(memory_space=pltpu.VMEM)
SMEM = pl.BlockSpec(memory_space=pltpu.SMEM)


def lanes(shape):
    return lax.broadcasted_iota(jnp.int32, shape, len(shape) - 1)


def pack_edges(field, lane):
    packed = None
    for i in range(16):
        first, last = field(i)
        edge = pltpu.roll(jnp.where(lane >= 124, last, first), (8 * i + 4) % 128, 1)
        packed = edge if packed is None else jnp.where(lane >= 8 * i, edge, packed)
    return packed


def coarse_matrix():
    matrix = np.zeros((8, 128, 2, 8, 16), np.float32)
    for row in range(8):
        for column in range(128):
            matrix[row, column, column // 64, row, (column % 64) // 4] = 1 / 16
    return matrix.reshape(1024, 256).astype(ml_dtypes.bfloat16)


def halo_copies(my, mx, fields, mask, now, packed, left, right, mtop, mbot, send, recv):
    def present(a, b):
        ok = None
        for at, change, count in ((my, a, NTY), (mx, b, NTX)):
            if change:
                one = at > 0 if change < 0 else at < count - 1
                ok = one if ok is None else jnp.logical_and(ok, one)
        return ok

    rows = []
    for half in range(2):
        side = pl.ds(128 * half, 128)
        rows.append((fields.at[:, pl.ds(248, 8), side], now.at[half, :, pl.ds(8, 8), :], 1, 0))
        rows.append((fields.at[:, pl.ds(0, 8), side], now.at[half, :, pl.ds(272, 8), :], -1, 0))
    rows.append((mask.at[pl.ds(248, 8), :], mtop, 1, 0))
    rows.append((mask.at[pl.ds(0, 8), :], mbot, -1, 0))
    sides = [
        (packed.at[pl.ds(16, 256), :], left.at[pl.ds(8, 256), :], 0, 1),
        (packed.at[pl.ds(16, 256), :], right.at[pl.ds(8, 256), :], 0, -1),
        (packed.at[pl.ds(264, 8), :], left.at[pl.ds(0, 8), :], 1, 1),
        (packed.at[pl.ds(16, 8), :], left.at[pl.ds(264, 8), :], -1, 1),
        (packed.at[pl.ds(264, 8), :], right.at[pl.ds(0, 8), :], 1, -1),
        (packed.at[pl.ds(16, 8), :], right.at[pl.ds(264, 8), :], -1, -1),
    ]

    def copy(index):
        src, dst, a, b = (rows + sides)[index]
        return pltpu.make_async_remote_copy(
            src_ref=src,
            dst_ref=dst,
            send_sem=send.at[index],
            recv_sem=recv.at[index],
            device_id={"ty": my + a, "tx": mx + b},
            device_id_type=MESH,
        )

    def each(indices, act, arriving=False):
        for index in indices:
            a, b = (rows + sides)[index][2:]

            @pl.when(present(-a, -b) if arriving else present(a, b))
            def _(index=index):
                act(copy(index))

    return present, each, range(len(rows)), range(len(rows), len(rows) + len(sides))


def advance(rate, wet, uv, src, dst, low, high, starts, shift):
    def body(k, _):
        diff = rate[k]
        keep = 1.0 - 4.0 * diff
        for row in starts:
            at = pl.ds(row, 16)
            lane = lanes((16, 128))
            for lev in range(2):
                i = 2 * k + lev
                x0, x1 = src[0, i, at, :], src[1, i, at, :]
                r0, r1 = pltpu.roll(x0, 1, 1), pltpu.roll(x1, 1, 1)
                l0, l1 = pltpu.roll(x0, 127, 1), pltpu.roll(x1, 127, 1)
                into_l, into_r = r0, l1
                if low is not None:
                    into_l = jnp.where(lane == 0, pltpu.roll(low[at, :], 125 - 8 * i, 1), r0)
                    into_r = jnp.where(lane == 127, pltpu.roll(high[at, :], 123 - 8 * i, 1), l1)
                w = (into_l, jnp.where(lane == 0, r0, r1))
                e = (jnp.where(lane == 127, l1, l0), into_r)
                for half in range(2):
                    c = (x0, x1)[half]
                    n = src[half, i, pl.ds(row - 1, 16), :]
                    s = src[half, i, pl.ds(row + 1, 16), :]
                    u, v = uv[half, lev, at, :], uv[half, 2 + lev, at, :]
                    near = (e[half] + w[half]) + (n + s)
                    adv = u * (e[half] - w[half]) + v * (s - n)
                    new = wet[half, at, :] * (c * keep + diff * near - adv)
                    dst[half, i, pl.ds(row - shift, 16), :] = new
        return 0

    return body


def velocities(uv, src, start, rows):
    at = pl.ds(start, rows)
    for half in range(2):
        uv[half, :, at, :] = 0.05 * src[half, 0:4, at, :]


def ocean_steps(rate, slot, packed, left, right, gather, out, chosen, now, later, final, wet, uv, strips, sums, wide, patches, out_sem):
    sl0, sl1, sr0, sr1, wl, wr = strips
    lane = lanes((136, 128))
    blocks = [(8 + 136 * b, pl.ds(8 + 136 * b, 136)) for b in range(2)]
    inner = (lane & 7) < 4
    for row, at in blocks:
        got_rows = pl.ds(row - 8, 136)
        own = packed[at, :]
        west, east = left[got_rows, :], right[got_rows, :]
        sl0[at, :] = jnp.where(inner, west, own)
        sr0[at, :] = jnp.where(inner, own, east)
        wet0, wet1 = wet[0, at, :], wet[1, at, :]
        low = jnp.where((lane >= 4) & (lane < 8), pltpu.roll(wet0, 4, 1), 0.0)
        low = jnp.where(lane == 2, pltpu.roll(west, 2, 1), low)
        low = jnp.where(lane == 3, pltpu.roll(west, 123, 1), low)
        high = jnp.where(lane < 4, pltpu.roll(wet1, 4, 1), 0.0)
        high = jnp.where(lane == 4, pltpu.roll(east, 125, 1), high)
        high = jnp.where(lane == 5, pltpu.roll(east, 118, 1), high)
        for shift in (8, 16, 32, 64):
            low = low + pltpu.roll(low, shift, 1)
            high = high + pltpu.roll(high, shift, 1)
        wl[at, :] = low
        wr[at, :] = high

    level = jnp.zeros((1, 128), F32)
    for k in range(8):
        level = jnp.where(lanes((1, 128)) >> 4 == k, rate[k], level)

    def advance_strips(*sides):
        for row, at in blocks:
            for src, dst, cells in sides:
                c = src[at, :]
                u = jnp.where(lane < 16, c, 0.0)
                v = jnp.where((lane >= 16) & (lane < 32), c, 0.0)
                for shift in (16, 32, 64):
                    u = u + pltpu.roll(u, shift, 1)
                    v = v + pltpu.roll(v, shift, 1)
                e, w = pltpu.roll(c, 127, 1), pltpu.roll(c, 1, 1)
                n, s = src[pl.ds(row - 1, 136), :], src[pl.ds(row + 1, 136), :]
                lap = (e + w) + (n + s) - 4.0 * c
                adv = u * (e - w) + v * (s - n)
                dst[at, :] = cells[at, :] * (c + level * lap - 0.05 * adv)

    velocities(uv, now, 8, 16)
    velocities(uv, now, 264, 16)
    lax.fori_loop(0, 8, advance(rate, wet, uv, now, later, sl0, sr0, (8, 264), 0), 0)
    advance_strips((sl0, sl1, wl), (sr0, sr1, wr))
    line = lanes((80, 128))

    def mend(k, _):
        for i in (2 * k, 2 * k + 1):
            for block in range(3):
                at = pl.ds(24 + 80 * block, 80)
                for half, strip, edge in ((0, sl1, 0), (1, sr1, 127)):
                    outer = pltpu.roll(strip[at, :], 124 - 8 * i, 1)
                    later[half, i, at, :] = jnp.where(line == edge, outer, later[half, i, at, :])
        return 0

    lax.fori_loop(0, 8, mend, 0)
    velocities(uv, later, 8, 272)
    every = tuple(range(8, 280, 16))
    lax.fori_loop(0, 8, advance(rate, wet, uv, later, now, sl1, sr1, every, 0), 0)
    advance_strips((sl1, sl0, wl), (sr1, sr0, wr))
    velocities(uv, now, 16, 256)
    last = advance(rate, wet, uv, now, final, sl0, sr0, tuple(range(16, 272, 16)), 16)

    def every_fourth(half, i, j):
        return final[half, i, pl.ds(j, 64, stride=4), :]

    def send(k, half):
        cut = pl.ds(2 * k, 2)
        src, dst = final.at[half, cut], out.at[cut, :, pl.ds(128 * half, 128)]
        return pltpu.make_async_copy(src, dst, out_sem.at[k, half])

    def last_step(k, _):
        last(k, 0)
        for half in range(2):
            send(k, half).start()
        for lev in range(2):
            i = 2 * k + lev
            for half in range(2):
                total = every_fourth(half, i, 0)
                for j in range(1, 4):
                    total = total + every_fourth(half, i, j)
                for pr in range(4):
                    to = pl.multiple_of(((lev * 4 + pr) * 8 + k) * 16, 16)
                    sums[half, pl.ds(to, 16), :] = total[16 * pr : 16 * pr + 16]
        return 0

    lax.fori_loop(0, 8, last_step, 0)

    for lev in range(2):
        for half in range(2):
            for which in range(3):
                total = None
                for j in range(4):
                    if which < 2:
                        term = every_fourth(half, 2 * which + lev, j)
                        term = term * every_fourth(half, 4 + 2 * which + lev, j)
                    else:
                        term = wet[half, pl.ds(16 + j, 64, stride=4), :]
                    total = term if total is None else total + term
                for pr in range(4):
                    to = 1024 + ((lev * 4 + pr) * 8 + which) * 16
                    sums[half, to : to + 16, :] = total[16 * pr : 16 * pr + 16]

    table = gather[...]
    for half in range(2):
        for rows in range(2):
            for y in range(8):
                x = sums[half, pl.ds(8 * rows + y, 128, stride=16), :]
                a = x.astype(BF16)
                x = x - a.astype(F32)
                b = x.astype(BF16)
                c = (x - b.astype(F32)).astype(BF16)
                side = pl.ds(128 * y, 128)
                wide[0:128, side] = a
                wide[128:256, side] = b
                wide[256:384, side] = c
            r = jnp.dot(wide[...], table, preferred_element_type=F32)
            r = r[0:128] + r[128:256] + r[256:384]
            means, products = r[0:64], r[64:128]
            for q in range(8):
                m = means[8 * q : 8 * q + 8]
                p = products[8 * q : 8 * q + 8]
                sub = lax.broadcasted_iota(jnp.int32, (8, 256), 0)
                p = p - jnp.where(sub < 2, m * pltpu.roll(m, 6, 0), 0.0)
                both = jnp.concatenate([m, p], axis=0).astype(BF16)
                for pc in range(2):
                    to = pl.ds(128 * rows, 128)
                    patches[4 * q + 2 * half + pc, :, to] = both[:, 128 * pc : 128 * pc + 128]

    for j in range(32):
        chosen[j] = patches[slot[j]]

    return send


def add_up(my, mx, grads, got1, part, got2, whole, sems):
    (s1, r1), (s2, r2), (s3, r3), (s4, r4), (s5, r5) = sems
    core, place = lax.rem(mx, 2), mx // 2
    sibling = {"ty": my, "tx": mx + 1 - 2 * core}

    def copy(src, dst, send, recv, to):
        return pltpu.make_async_remote_copy(
            src_ref=src, dst_ref=dst, send_sem=send, recv_sem=recv, device_id=to, device_id_type=MESH
        )

    def rows(start, count):
        return pl.ds(pl.multiple_of(start, 8), count)

    def one(d):
        peer = lax.rem(my + d, NTY)
        src = grads.at[pl.ds(pl.multiple_of(CHUNK * peer, 16), CHUNK), :]
        return copy(src, got1.at[d], s1.at[d], r1.at[d], {"ty": peer, "tx": mx})

    for d in range(1, NTY):
        one(d).start()
    part[...] = grads[pl.ds(pl.multiple_of(CHUNK * my, 16), CHUNK), :].astype(F32)
    for d in range(1, NTY):
        one(d).wait_recv()
        part[...] += got1[d].astype(F32)

    base = CHUNK * my + HALF * core

    def chip(index):
        return {"ty": my, "tx": 2 * index + core}

    def ahead(d):
        return lax.rem(place + d, NTY)

    def behind(d):
        return lax.rem(place + NTY - d, NTY)

    def two(d, start):
        to = {"ty": my, "tx": lax.rem(mx + d, NTX)}
        return copy(part.at[rows(start, PIECE), :], got2.at[d], s2.at[d], r2.at[d], to)

    def piece_of(device):
        return HALF * lax.rem(device, 2) + PIECE * (device // 2)

    def three(d, owner, to):
        cut = whole.at[rows(base + PIECE * owner, PIECE), :]
        return copy(cut, cut, s3.at[d], r3.at[d], chip(to))

    for d in range(1, NTX):
        peer = lax.rem(mx + d, NTX)

        @pl.when(peer // 2 < OWNERS)
        def _(d=d, peer=peer):
            two(d, piece_of(peer)).start()

    @pl.when(place < OWNERS)
    def _():
        total = part[rows(piece_of(mx), PIECE), :]
        for d in range(1, NTX):
            two(d, 0).wait_recv()
            total = total + got2[d]
        whole[rows(base + PIECE * place, PIECE), :] = total
        for d in range(1, NTY):
            three(d, place, ahead(d)).start()

    for d in range(1, NTY):

        @pl.when(behind(d) < OWNERS)
        def _(d=d):
            three(d, behind(d), behind(d)).wait_recv()

    def four(d, source, peer):
        cut = whole.at[rows(CHUNK * source + HALF * core, HALF), :]
        return copy(cut, cut, s4.at[d], r4.at[d], {"ty": peer, "tx": mx})

    def five(d, half):
        source = lax.rem(my + NTY - d, NTY)
        cut = whole.at[rows(CHUNK * source + HALF * half, HALF), :]
        return copy(cut, cut, s5.at[d], r5.at[d], sibling)

    for d in range(1, NTY):
        four(d, my, lax.rem(my + d, NTY)).start()
    five(0, core).start()
    for d in range(1, NTY):
        source = lax.rem(my + NTY - d, NTY)
        four(d, source, source).wait_recv()
        five(d, core).start()
    for d in range(NTY):
        five(d, 1 - core).wait_recv()

    for d in range(NTY):
        five(d, core).wait_send()
    for d in range(1, NTX):
        peer = lax.rem(mx + d, NTX)

        @pl.when(peer // 2 < OWNERS)
        def _(d=d, peer=peer):
            two(d, piece_of(peer)).wait_send()

    for d in range(1, NTY):
        one(d).wait_send()
        four(d, my, lax.rem(my + d, NTY)).wait_send()

        @pl.when(place < OWNERS)
        def _(d=d):
            three(d, place, ahead(d)).wait_send()


def contract(a, b, dim_a, dim_b):
    return lax.dot_general(
        a, b, (((dim_a,), (dim_b,)), ((), ())), preferred_element_type=F32
    )


def net_step(first, group, got, win, wmid, hs, ds, wback, wout8, amid, ain, aout, amis):
    size = group * 256
    lane = lanes((8, size))
    col, row = lane & 15, (lane >> 4) & 15

    def inside(dy, dx):
        ok = None
        for value, change in ((row, dy), (col, dx)):
            if change:
                one = value >= 1 if change < 0 else value <= 14
                ok = one if ok is None else ok & one
        return ok

    def moved(a, dy, dx):
        off = 16 * dy + dx
        if off == 0:
            return a
        return jnp.where(inside(dy, dx), pltpu.roll(a, (-off) % size, 1), 0.0)

    side = lax.broadcasted_iota(jnp.int32, (size, 128), 0) & 15
    taps = wout8[...].astype(BF16)

    def spread(ref, a, sign):
        for j, dx in enumerate((-1, 0, 1)):
            go = sign * dx
            if go == 0:
                v = a
            elif go < 0:
                v = jnp.where(side == 0, 0.0, pltpu.roll(a, 1, 0))
            else:
                v = jnp.where(side == 15, 0.0, pltpu.roll(a, size - 1, 0))
            v = v.astype(BF16)
            for i, dy in enumerate((-1, 0, 1)):
                to = pl.ds(128 * (3 * i + j), 128)
                for p in range(group):
                    b = 256 * p
                    if sign * dy == 0:
                        ref[b : b + 256, to] = v[b : b + 256]
                    elif sign * dy < 0:
                        ref[b + 16 : b + 256, to] = v[b : b + 240]
                    else:
                        ref[b : b + 240, to] = v[b + 16 : b + 256]

    def silu(z):
        s = 0.5 * jnp.tanh(0.5 * z) + 0.5
        h = z * s
        return h, s + h * (1.0 - s)

    def work(hs, ds, base):
        data = [got[base + p].astype(F32) for p in range(group)]
        x = jnp.concatenate([d[0:8] for d in data], axis=1)
        lab = jnp.concatenate([d[8:16] for d in data], axis=1)
        xcat = jnp.concatenate([moved(x, dy, dx) for dy, dx in TAPS], axis=0).astype(BF16)
        z1 = contract(xcat, win[...], 0, 0)
        yield
        h1, slope1 = silu(z1)
        spread(hs, h1, 1)
        yield
        z2 = jnp.dot(hs[...], wmid[...], preferred_element_type=F32)
        yield
        h2, slope2 = silu(z2)
        h2 = h2.astype(BF16)
        parts = contract(taps, h2, 1, 1)
        yield
        y = jnp.zeros((8, size), F32)
        for t, (dy, dx) in enumerate(TAPS):
            y = y + moved(parts[8 * t : 8 * t + 8], dy, dx)
        sub = lax.broadcasted_iota(jnp.int32, (8, size), 0)
        diff = jnp.where(sub < 2, y - lab, 0.0)
        weighted = lab[2:3] * diff
        g = 2.0 * weighted
        gcat = jnp.concatenate([moved(g, -dy, -dx) for dy, dx in TAPS], axis=0).astype(BF16)
        dh2 = contract(gcat, taps, 0, 0).astype(BF16).astype(F32)
        yield
        dz2 = dh2 * slope2
        spread(ds, dz2, -1)
        yield
        dh1 = jnp.dot(ds[...], wback[...], preferred_element_type=F32).astype(BF16).astype(F32)
        yield
        dmid = contract(h1.astype(BF16), ds[...], 0, 0)
        yield
        dz1 = (dh1 * slope1).astype(BF16)
        dout = jnp.dot(gcat, h2, preferred_element_type=F32)
        din = jnp.dot(xcat, dz1, preferred_element_type=F32)
        yield weighted * diff, dmid, din, dout

    cut = pl.ds(0, size)
    teams = [work(hs.at[i, cut], ds.at[i, cut], first + group * i) for i in range(TEAMS)]
    results = []
    while len(results) < TEAMS:
        for team in teams:
            value = next(team)
            if value is not None:
                results.append(value)
    for ref, parts in zip((amis.at[:, cut], amid, ain, aout), zip(*results)):
        ref[...] += functools.reduce(jnp.add, parts)


def whole_kernel(
    rate, slot, fields, mask, gather, win, wmid, wout,
    out, misfit, first, mid, last,
    now, later, final, wet, uv, sl0, sl1, sr0, sr1, wl, wr, packed, left, right, mtop, mbot,
    sums, wide, patches, chosen, got,
    hs, ds, wback, wout8, amid, ain, aout, amis,
    grads, got1, part, got2, whole,
    in_sem, out_sem, halo_send, halo_recv, swap_send, swap_recv, *sems,
):
    my, mx = lax.axis_index("ty"), lax.axis_index("tx")
    loads = []
    for half in range(2):
        src = fields.at[:, :, pl.ds(128 * half, 128)]
        loads.append(pltpu.make_async_copy(src, now.at[half, :, pl.ds(16, 256), :], in_sem.at[half]))
        loads[-1].start()

    barrier = pltpu.get_barrier_semaphore()
    present, each, rows, sides = halo_copies(
        my, mx, fields, mask, now, packed, left, right, mtop, mbot, halo_send, halo_recv
    )
    count = jnp.int32(NTY + NTX - 2)
    for a in (-1, 0, 1):
        for b in (-1, 0, 1):
            if a or b:
                here = present(a, b)
                count = count + here.astype(jnp.int32)

                @pl.when(here)
                def _(a=a, b=b):
                    to = {"ty": my + a, "tx": mx + b}
                    pl.semaphore_signal(barrier, inc=1, device_id=to, device_id_type=MESH)

    others = [{"ty": lax.rem(my + d, NTY), "tx": mx} for d in range(1, NTY)]
    others += [{"ty": my, "tx": lax.rem(mx + d, NTX)} for d in range(1, NTX)]
    for to in others:
        pl.semaphore_signal(barrier, inc=1, device_id=to, device_id_type=MESH)

    @pl.when(my == 0)
    def _():
        now[:, :, 8:16, :] = jnp.zeros((2, 16, 8, 128), F32)
        mtop[...] = jnp.zeros_like(mtop)
        left[0:8, :] = jnp.zeros((8, 128), F32)
        right[0:8, :] = jnp.zeros((8, 128), F32)

    @pl.when(my == NTY - 1)
    def _():
        now[:, :, 272:280, :] = jnp.zeros((2, 16, 8, 128), F32)
        mbot[...] = jnp.zeros_like(mbot)
        left[264:272, :] = jnp.zeros((8, 128), F32)
        right[264:272, :] = jnp.zeros((8, 128), F32)

    @pl.when(mx == 0)
    def _():
        left[...] = jnp.zeros_like(left)

    @pl.when(mx == NTX - 1)
    def _():
        right[...] = jnp.zeros_like(right)

    for load in loads:
        load.wait()
    for block in range(2):
        lane = lanes((128, 128))
        at, to = pl.ds(128 * block, 128), pl.ds(16 + 128 * block, 128)
        edges = pack_edges(lambda i: (now[0, i, to, :], now[1, i, to, :]), lane)
        wet0 = mask[at, 0:128].astype(F32)
        wet1 = mask[at, 128:256].astype(F32)
        edges = jnp.where(lane == 0, pltpu.roll(wet1, 2, 1), edges)
        edges = jnp.where(lane == 8, pltpu.roll(wet1, 9, 1), edges)
        edges = jnp.where(lane == 7, pltpu.roll(wet0, 7, 1), edges)
        edges = jnp.where(lane == 15, pltpu.roll(wet0, 14, 1), edges)
        packed[to, :] = edges

    pl.semaphore_wait(barrier, count)
    start = lambda copy: copy.start()
    each(rows, start)
    each(sides, start)

    for half in range(2):
        wet[half, 16:272, :] = mask[:, 128 * half : 128 * half + 128].astype(F32)
        for buf in (now, later):
            buf[half, :, 0:8, :] = jnp.zeros((16, 8, 128), F32)
            buf[half, :, 280:288, :] = jnp.zeros((16, 8, 128), F32)
    for buf in (sl0, sr0, sl1, sr1):
        buf[0:8, :] = jnp.zeros((8, 128), F32)
        buf[280:288, :] = jnp.zeros((8, 128), F32)
    sums[:, 1024:2048, :] = jnp.zeros((2, 1024, 128), F32)
    for ref in (hs, ds, amid, ain, aout, amis):
        ref[...] = jnp.zeros_like(ref)
    for t in range(9):
        at = pl.ds(128 * t, 128)
        wback[at, :] = wmid[at, :].astype(F32).T.astype(BF16)
        wout8[8 * t : 8 * t + 8, :] = jnp.zeros((8, 128), F32)
        wout8[8 * t : 8 * t + 2, :] = wout[t].astype(F32)

    velocities(uv, now, 24, 240)
    inner = tuple(range(24, 264, 16))
    lax.fori_loop(0, 8, advance(rate, wet, uv, now, later, None, None, inner, 0), 0)

    arrived = lambda copy: copy.wait_recv()
    each(rows, arrived, arriving=True)
    each(sides, arrived, arriving=True)
    for half in range(2):
        side = pl.ds(128 * half, 128)
        wet[half, 8:16, :] = mtop[:, side].astype(F32)
        wet[half, 272:280, :] = mbot[:, side].astype(F32)
    for at in (pl.ds(8, 8), pl.ds(272, 8)):
        packed[at, :] = pack_edges(lambda i: (now[0, i, at, :], now[1, i, at, :]), lanes((8, 128)))

    strips = (sl0, sl1, sr0, sr1, wl, wr)
    leaving = ocean_steps(
        rate, slot, packed, left, right, gather, out, chosen, now, later, final, wet, uv, strips, sums, wide, patches, out_sem
    )

    def swap(d):
        peer = lax.rem(my + d, NTY)
        return pltpu.make_async_remote_copy(
            src_ref=chosen.at[pl.ds(4 * peer, 4)],
            dst_ref=got.at[pl.ds(4 * d, 4)],
            send_sem=swap_send.at[d],
            recv_sem=swap_recv.at[d],
            device_id={"ty": peer, "tx": mx},
            device_id_type=MESH,
        )

    for d in range(1, NTY):
        swap(d).start()
    for j in range(4):
        got[j] = chosen[4 * my + j]

    def net(first, group):
        net_step(first, group, got, win, wmid, hs, ds, wback, wout8, amid, ain, aout, amis)

    def step(index, _):
        for i in range(1, 5):

            @pl.when(index == i)
            def _(i=i):
                for d in range(2 * i - 1, min(2 * i + 1, NTY)):
                    swap(d).wait_recv()

        ends = jnp.logical_or(index == 0, index == 4)

        @pl.when(ends)
        def _():
            net(7 * index, GROUP // 2)

        @pl.when(jnp.logical_not(ends))
        def _():
            net(8 * index - 4, GROUP)

        return 0

    lax.fori_loop(0, 5, step, 0)
    for t in range(9):
        at = pl.ds(128 * t, 128)
        grads[at, :] = amid[:, at].astype(BF16)
    both = jnp.concatenate(
        [ain[...]] + [aout[8 * t : 8 * t + 2, :] for t in range(9)] + [jnp.zeros((38, 128), F32)],
        axis=0,
    )
    grads[1152:1280, :] = both.astype(BF16)
    misfit[...] = jnp.full((1, 1), jnp.sum(amis[...]) / 8192, F32)
    pairs = tuple(zip(sems[::2], sems[1::2]))
    add_up(my, mx, grads, got1, part, got2, whole, pairs)

    def scale(start, rows):
        g = whole[start : start + rows, :]
        return lax.rsqrt(jnp.sum(g * g) / F32(rows * 128) + NORM_EPS)

    mid[...] = whole[0:1152, :] * scale(0, 1152)
    first[...] = whole[1152:1224, :] * scale(1152, 72)
    size = scale(1224, 18)
    for t in range(9):
        last[t] = whole[1224 + 2 * t : 1226 + 2 * t, :] * size

    sent = lambda copy: copy.wait_send()
    each(rows, sent)
    each(sides, sent)
    for d in range(1, NTY):
        swap(d).wait_send()
    for k in range(8):
        for half in range(2):
            leaving(k, half).wait()


def run(rate, slot, fields, mask, gather, win, wmid, wout):
    dma = pltpu.SemaphoreType.DMA
    f32 = lambda *shape: pltpu.VMEM(shape, F32)
    bf16 = lambda *shape: pltpu.VMEM(shape, BF16)
    return pl.pallas_call(
        whole_kernel,
        out_shape=(
            jax.ShapeDtypeStruct((16, 256, 256), F32),
            jax.ShapeDtypeStruct((1, 1), F32),
            jax.ShapeDtypeStruct((72, 128), F32),
            jax.ShapeDtypeStruct((1152, 128), F32),
            jax.ShapeDtypeStruct((9, 2, 128), F32),
        ),
        in_specs=[SMEM, SMEM, ANY, VMEM, VMEM, VMEM, VMEM, VMEM],
        out_specs=(ANY, VMEM, VMEM, VMEM, VMEM),
        scratch_shapes=[
            f32(2, 16, 288, 128),
            f32(2, 16, 288, 128),
            f32(2, 16, 256, 128),
            f32(2, 288, 128),
            f32(2, 4, 288, 128),
        ]
        + [f32(288, 128)] * 7
        + [
            f32(272, 128),
            f32(272, 128),
            pltpu.VMEM((8, 256), jnp.int32),
            pltpu.VMEM((8, 256), jnp.int32),
            f32(2, 2048, 128),
            bf16(384, 1024),
            bf16(32, 16, 256),
            bf16(32, 16, 256),
            bf16(32, 16, 256),
            bf16(TEAMS, GROUP * 256, 1152),
            bf16(TEAMS, GROUP * 256, 1152),
            bf16(1152, 128),
            f32(72, 128),
            f32(128, 1152),
            f32(72, 128),
            f32(72, 128),
            f32(8, GROUP * 256),
            bf16(ROWS, 128),
            bf16(NTY, CHUNK, 128),
            f32(CHUNK, 128),
            f32(NTX, PIECE, 128),
            f32(ROWS, 128),
            dma((2,)),
            dma((8, 2)),
            dma((12,)),
            dma((12,)),
        ]
        + [dma((n,)) for n in (NTY, NTY, NTY, NTY, NTX, NTX) + (NTY,) * 6],
        compiler_params=pltpu.CompilerParams(
            collective_id=0, has_side_effects=True, vmem_limit_bytes=60 << 20
        ),
        name="whole",
    )(rate, slot, fields, mask, gather, win, wmid, wout)


def per_device(fields, ocean_mask, diffusivity, patch_slot_assignment, conv_in, conv_mid, conv_out):
    current, member_loss, first, mid, last = run(
        diffusivity,
        patch_slot_assignment.reshape(32),
        fields.reshape(16, 256, 256),
        ocean_mask,
        jnp.asarray(coarse_matrix()),
        conv_in.reshape(72, 128),
        conv_mid.reshape(1152, 128),
        conv_out.reshape(9, 128, 2).transpose(0, 2, 1),
    )
    return (
        current.reshape(fields.shape),
        member_loss,
        first.reshape(conv_in.shape),
        mid.reshape(conv_mid.shape),
        last.transpose(0, 2, 1).reshape(conv_out.shape),
    )


def solution(mesh):
    placed = (P(None, None, "ty", "tx"), P("ty", "tx"), P(), P("ty", "tx", None), P(), P(), P())
    return jax.shard_map(
        per_device,
        mesh=mesh,
        in_specs=placed,
        out_specs=(P(None, None, "ty", "tx"), P("ty", "tx"), P(), P(), P()),
        check_vma=False,
    )
```

```python
import functools

import jax
import jax.numpy as jnp
import ml_dtypes
import numpy as np
from jax import lax
from jax.experimental import pallas as pl
from jax.experimental.pallas import tpu as pltpu
from jax.sharding import PartitionSpec as P

F32 = jnp.float32
BF16 = jnp.bfloat16
MESH = pl.DeviceIdType.MESH
NTY, NTX = 8, 16
ROWS = 1280
CHUNK = ROWS // NTY
PIECE = 16
HALF = CHUNK // 2
OWNERS = HALF // PIECE
GROUP = 4
TEAMS = 2
TAPS = [(i - 1, j - 1) for i in range(3) for j in range(3)]
NORM_EPS = 1e-6
ANY = pl.BlockSpec(memory_space=pl.ANY)
VMEM = pl.BlockSpec(memory_space=pltpu.VMEM)
SMEM = pl.BlockSpec(memory_space=pltpu.SMEM)


def lanes(shape):
    return lax.broadcasted_iota(jnp.int32, shape, len(shape) - 1)


def pack_edges(field, lane):
    packed = None
    for i in range(16):
        first, last = field(i)
        edge = pltpu.roll(jnp.where(lane >= 124, last, first), (8 * i + 4) % 128, 1)
        packed = edge if packed is None else jnp.where(lane >= 8 * i, edge, packed)
    return packed


def coarse_matrix():
    matrix = np.zeros((8, 128, 2, 8, 16), np.float32)
    for row in range(8):
        for column in range(128):
            matrix[row, column, column // 64, row, (column % 64) // 4] = 1 / 16
    return matrix.reshape(1024, 256).astype(ml_dtypes.bfloat16)


def halo_copies(my, mx, fields, mask, now, packed, left, right, mtop, mbot, send, recv):
    def present(a, b):
        ok = None
        for at, change, count in ((my, a, NTY), (mx, b, NTX)):
            if change:
                one = at > 0 if change < 0 else at < count - 1
                ok = one if ok is None else jnp.logical_and(ok, one)
        return ok

    rows = []
    for half in range(2):
        side = pl.ds(128 * half, 128)
        rows.append((fields.at[:, pl.ds(248, 8), side], now.at[half, :, pl.ds(8, 8), :], 1, 0))
        rows.append((fields.at[:, pl.ds(0, 8), side], now.at[half, :, pl.ds(272, 8), :], -1, 0))
    rows.append((mask.at[pl.ds(248, 8), :], mtop, 1, 0))
    rows.append((mask.at[pl.ds(0, 8), :], mbot, -1, 0))
    sides = [
        (packed.at[pl.ds(16, 256), :], left.at[pl.ds(8, 256), :], 0, 1),
        (packed.at[pl.ds(16, 256), :], right.at[pl.ds(8, 256), :], 0, -1),
        (packed.at[pl.ds(264, 8), :], left.at[pl.ds(0, 8), :], 1, 1),
        (packed.at[pl.ds(16, 8), :], left.at[pl.ds(264, 8), :], -1, 1),
        (packed.at[pl.ds(264, 8), :], right.at[pl.ds(0, 8), :], 1, -1),
        (packed.at[pl.ds(16, 8), :], right.at[pl.ds(264, 8), :], -1, -1),
    ]

    def copy(index):
        src, dst, a, b = (rows + sides)[index]
        return pltpu.make_async_remote_copy(
            src_ref=src,
            dst_ref=dst,
            send_sem=send.at[index],
            recv_sem=recv.at[index],
            device_id={"ty": my + a, "tx": mx + b},
            device_id_type=MESH,
        )

    def each(indices, act, arriving=False):
        for index in indices:
            a, b = (rows + sides)[index][2:]

            @pl.when(present(-a, -b) if arriving else present(a, b))
            def _(index=index):
                act(copy(index))

    return present, each, range(len(rows)), range(len(rows), len(rows) + len(sides))


def advance(rate, wet, uv, src, dst, low, high, starts, shift):
    def body(k, _):
        diff = rate[k]
        keep = 1.0 - 4.0 * diff
        for row in starts:
            at = pl.ds(row, 16)
            lane = lanes((16, 128))
            for lev in range(2):
                i = 2 * k + lev
                x0, x1 = src[0, i, at, :], src[1, i, at, :]
                r0, r1 = pltpu.roll(x0, 1, 1), pltpu.roll(x1, 1, 1)
                l0, l1 = pltpu.roll(x0, 127, 1), pltpu.roll(x1, 127, 1)
                into_l, into_r = r0, l1
                if low is not None:
                    into_l = jnp.where(lane == 0, pltpu.roll(low[at, :], 125 - 8 * i, 1), r0)
                    into_r = jnp.where(lane == 127, pltpu.roll(high[at, :], 123 - 8 * i, 1), l1)
                w = (into_l, jnp.where(lane == 0, r0, r1))
                e = (jnp.where(lane == 127, l1, l0), into_r)
                for half in range(2):
                    c = (x0, x1)[half]
                    n = src[half, i, pl.ds(row - 1, 16), :]
                    s = src[half, i, pl.ds(row + 1, 16), :]
                    u, v = uv[half, lev, at, :], uv[half, 2 + lev, at, :]
                    near = (e[half] + w[half]) + (n + s)
                    adv = u * (e[half] - w[half]) + v * (s - n)
                    new = wet[half, at, :] * (c * keep + diff * near - adv)
                    dst[half, i, pl.ds(row - shift, 16), :] = new
        return 0

    return body


def velocities(uv, src, start, rows):
    at = pl.ds(start, rows)
    for half in range(2):
        uv[half, :, at, :] = 0.05 * src[half, 0:4, at, :]


def ocean_steps(rate, slot, packed, left, right, gather, out, chosen, now, later, final, wet, uv, strips, sums, wide, patches, out_sem):
    sl0, sl1, sr0, sr1, wl, wr = strips
    lane = lanes((136, 128))
    blocks = [(8 + 136 * b, pl.ds(8 + 136 * b, 136)) for b in range(2)]
    inner = (lane & 7) < 4
    for row, at in blocks:
        got_rows = pl.ds(row - 8, 136)
        own = packed[at, :]
        west, east = left[got_rows, :], right[got_rows, :]
        sl0[at, :] = jnp.where(inner, west, own)
        sr0[at, :] = jnp.where(inner, own, east)
        wet0, wet1 = wet[0, at, :], wet[1, at, :]
        low = jnp.where((lane >= 4) & (lane < 8), pltpu.roll(wet0, 4, 1), 0.0)
        low = jnp.where(lane == 2, pltpu.roll(west, 2, 1), low)
        low = jnp.where(lane == 3, pltpu.roll(west, 123, 1), low)
        high = jnp.where(lane < 4, pltpu.roll(wet1, 4, 1), 0.0)
        high = jnp.where(lane == 4, pltpu.roll(east, 125, 1), high)
        high = jnp.where(lane == 5, pltpu.roll(east, 118, 1), high)
        for shift in (8, 16, 32, 64):
            low = low + pltpu.roll(low, shift, 1)
            high = high + pltpu.roll(high, shift, 1)
        wl[at, :] = low
        wr[at, :] = high

    level = jnp.zeros((1, 128), F32)
    for k in range(8):
        level = jnp.where(lanes((1, 128)) >> 4 == k, rate[k], level)

    def advance_strips(*sides):
        for row, at in blocks:
            for src, dst, cells in sides:
                c = src[at, :]
                u = jnp.where(lane < 16, c, 0.0)
                v = jnp.where((lane >= 16) & (lane < 32), c, 0.0)
                for shift in (16, 32, 64):
                    u = u + pltpu.roll(u, shift, 1)
                    v = v + pltpu.roll(v, shift, 1)
                e, w = pltpu.roll(c, 127, 1), pltpu.roll(c, 1, 1)
                n, s = src[pl.ds(row - 1, 136), :], src[pl.ds(row + 1, 136), :]
                lap = (e + w) + (n + s) - 4.0 * c
                adv = u * (e - w) + v * (s - n)
                dst[at, :] = cells[at, :] * (c + level * lap - 0.05 * adv)

    velocities(uv, now, 8, 16)
    velocities(uv, now, 264, 16)
    lax.fori_loop(0, 8, advance(rate, wet, uv, now, later, sl0, sr0, (8, 264), 0), 0)
    advance_strips((sl0, sl1, wl), (sr0, sr1, wr))
    line = lanes((80, 128))

    def mend(k, _):
        for i in (2 * k, 2 * k + 1):
            for block in range(3):
                at = pl.ds(24 + 80 * block, 80)
                for half, strip, edge in ((0, sl1, 0), (1, sr1, 127)):
                    outer = pltpu.roll(strip[at, :], 124 - 8 * i, 1)
                    later[half, i, at, :] = jnp.where(line == edge, outer, later[half, i, at, :])
        return 0

    lax.fori_loop(0, 8, mend, 0)
    velocities(uv, later, 8, 272)
    every = tuple(range(8, 280, 16))
    lax.fori_loop(0, 8, advance(rate, wet, uv, later, now, sl1, sr1, every, 0), 0)
    advance_strips((sl1, sl0, wl), (sr1, sr0, wr))
    velocities(uv, now, 16, 256)
    last = advance(rate, wet, uv, now, final, sl0, sr0, tuple(range(16, 272, 16)), 16)

    def every_fourth(half, i, j):
        return final[half, i, pl.ds(j, 64, stride=4), :]

    def send(k, half):
        cut = pl.ds(2 * k, 2)
        src, dst = final.at[half, cut], out.at[cut, :, pl.ds(128 * half, 128)]
        return pltpu.make_async_copy(src, dst, out_sem.at[k, half])

    def last_step(k, _):
        last(k, 0)
        for half in range(2):
            send(k, half).start()
        for lev in range(2):
            i = 2 * k + lev
            for half in range(2):
                total = every_fourth(half, i, 0)
                for j in range(1, 4):
                    total = total + every_fourth(half, i, j)
                for pr in range(4):
                    to = pl.multiple_of(((lev * 4 + pr) * 8 + k) * 16, 16)
                    sums[half, pl.ds(to, 16), :] = total[16 * pr : 16 * pr + 16]
        return 0

    lax.fori_loop(0, 8, last_step, 0)

    for lev in range(2):
        for half in range(2):
            for which in range(3):
                total = None
                for j in range(4):
                    if which < 2:
                        term = every_fourth(half, 2 * which + lev, j)
                        term = term * every_fourth(half, 4 + 2 * which + lev, j)
                    else:
                        term = wet[half, pl.ds(16 + j, 64, stride=4), :]
                    total = term if total is None else total + term
                for pr in range(4):
                    to = 1024 + ((lev * 4 + pr) * 8 + which) * 16
                    sums[half, to : to + 16, :] = total[16 * pr : 16 * pr + 16]

    table = gather[...]
    for half in range(2):
        for rows in range(2):
            for y in range(8):
                x = sums[half, pl.ds(8 * rows + y, 128, stride=16), :]
                a = x.astype(BF16)
                x = x - a.astype(F32)
                b = x.astype(BF16)
                c = (x - b.astype(F32)).astype(BF16)
                side = pl.ds(128 * y, 128)
                wide[0:128, side] = a
                wide[128:256, side] = b
                wide[256:384, side] = c
            r = jnp.dot(wide[...], table, preferred_element_type=F32)
            r = r[0:128] + r[128:256] + r[256:384]
            means, products = r[0:64], r[64:128]
            for q in range(8):
                m = means[8 * q : 8 * q + 8]
                p = products[8 * q : 8 * q + 8]
                sub = lax.broadcasted_iota(jnp.int32, (8, 256), 0)
                p = p - jnp.where(sub < 2, m * pltpu.roll(m, 6, 0), 0.0)
                both = jnp.concatenate([m, p], axis=0).astype(BF16)
                for pc in range(2):
                    to = pl.ds(128 * rows, 128)
                    patches[4 * q + 2 * half + pc, :, to] = both[:, 128 * pc : 128 * pc + 128]

    for j in range(32):
        chosen[j] = patches[slot[j]]

    return send


def add_up(my, mx, grads, got1, part, got2, whole, sems):
    (s1, r1), (s2, r2), (s3, r3), (s4, r4), (s5, r5) = sems
    core, place = lax.rem(mx, 2), mx // 2
    sibling = {"ty": my, "tx": mx + 1 - 2 * core}

    def copy(src, dst, send, recv, to):
        return pltpu.make_async_remote_copy(
            src_ref=src, dst_ref=dst, send_sem=send, recv_sem=recv, device_id=to, device_id_type=MESH
        )

    def rows(start, count):
        return pl.ds(pl.multiple_of(start, 8), count)

    def one(d):
        peer = lax.rem(my + d, NTY)
        src = grads.at[pl.ds(pl.multiple_of(CHUNK * peer, 16), CHUNK), :]
        return copy(src, got1.at[d], s1.at[d], r1.at[d], {"ty": peer, "tx": mx})

    for d in range(1, NTY):
        one(d).start()
    part[...] = grads[pl.ds(pl.multiple_of(CHUNK * my, 16), CHUNK), :].astype(F32)
    for d in range(1, NTY):
        one(d).wait_recv()
        part[...] += got1[d].astype(F32)

    base = CHUNK * my + HALF * core

    def chip(index):
        return {"ty": my, "tx": 2 * index + core}

    def ahead(d):
        return lax.rem(place + d, NTY)

    def behind(d):
        return lax.rem(place + NTY - d, NTY)

    def two(d, start):
        to = {"ty": my, "tx": lax.rem(mx + d, NTX)}
        return copy(part.at[rows(start, PIECE), :], got2.at[d], s2.at[d], r2.at[d], to)

    def piece_of(device):
        return HALF * lax.rem(device, 2) + PIECE * (device // 2)

    def three(d, owner, to):
        cut = whole.at[rows(base + PIECE * owner, PIECE), :]
        return copy(cut, cut, s3.at[d], r3.at[d], chip(to))

    for d in range(1, NTX):
        peer = lax.rem(mx + d, NTX)

        @pl.when(peer // 2 < OWNERS)
        def _(d=d, peer=peer):
            two(d, piece_of(peer)).start()

    @pl.when(place < OWNERS)
    def _():
        total = part[rows(piece_of(mx), PIECE), :]
        for d in range(1, NTX):
            two(d, 0).wait_recv()
            total = total + got2[d]
        whole[rows(base + PIECE * place, PIECE), :] = total
        for d in range(1, NTY):
            three(d, place, ahead(d)).start()

    for d in range(1, NTY):

        @pl.when(behind(d) < OWNERS)
        def _(d=d):
            three(d, behind(d), behind(d)).wait_recv()

    def four(d, source, peer):
        cut = whole.at[rows(CHUNK * source + HALF * core, HALF), :]
        return copy(cut, cut, s4.at[d], r4.at[d], {"ty": peer, "tx": mx})

    def five(d, half):
        source = lax.rem(my + NTY - d, NTY)
        cut = whole.at[rows(CHUNK * source + HALF * half, HALF), :]
        return copy(cut, cut, s5.at[d], r5.at[d], sibling)

    for d in range(1, NTY):
        four(d, my, lax.rem(my + d, NTY)).start()
    five(0, core).start()
    for d in range(1, NTY):
        source = lax.rem(my + NTY - d, NTY)
        four(d, source, source).wait_recv()
        five(d, core).start()
    for d in range(NTY):
        five(d, 1 - core).wait_recv()

    for d in range(NTY):
        five(d, core).wait_send()
    for d in range(1, NTX):
        peer = lax.rem(mx + d, NTX)

        @pl.when(peer // 2 < OWNERS)
        def _(d=d, peer=peer):
            two(d, piece_of(peer)).wait_send()

    for d in range(1, NTY):
        one(d).wait_send()
        four(d, my, lax.rem(my + d, NTY)).wait_send()

        @pl.when(place < OWNERS)
        def _(d=d):
            three(d, place, ahead(d)).wait_send()


def contract(a, b, dim_a, dim_b):
    return lax.dot_general(
        a, b, (((dim_a,), (dim_b,)), ((), ())), preferred_element_type=F32
    )


def net_step(first, group, got, win, wmid, hs, ds, wback, wout8, amid, ain, aout, amis):
    size = group * 256
    lane = lanes((8, size))
    col, row = lane & 15, (lane >> 4) & 15

    def inside(dy, dx):
        ok = None
        for value, change in ((row, dy), (col, dx)):
            if change:
                one = value >= 1 if change < 0 else value <= 14
                ok = one if ok is None else ok & one
        return ok

    def moved(a, dy, dx):
        off = 16 * dy + dx
        if off == 0:
            return a
        return jnp.where(inside(dy, dx), pltpu.roll(a, (-off) % size, 1), 0.0)

    side = lax.broadcasted_iota(jnp.int32, (size, 128), 0) & 15
    taps = wout8[...].astype(BF16)

    def spread(ref, a, sign):
        for j, dx in enumerate((-1, 0, 1)):
            go = sign * dx
            if go == 0:
                v = a
            elif go < 0:
                v = jnp.where(side == 0, 0.0, pltpu.roll(a, 1, 0))
            else:
                v = jnp.where(side == 15, 0.0, pltpu.roll(a, size - 1, 0))
            v = v.astype(BF16)
            for i, dy in enumerate((-1, 0, 1)):
                to = pl.ds(128 * (3 * i + j), 128)
                for p in range(group):
                    b = 256 * p
                    if sign * dy == 0:
                        ref[b : b + 256, to] = v[b : b + 256]
                    elif sign * dy < 0:
                        ref[b + 16 : b + 256, to] = v[b : b + 240]
                    else:
                        ref[b : b + 240, to] = v[b + 16 : b + 256]

    def silu(z):
        s = 0.5 * jnp.tanh(0.5 * z) + 0.5
        h = z * s
        return h, s + h * (1.0 - s)

    def work(hs, ds, base):
        data = [got[base + p].astype(F32) for p in range(group)]
        x = jnp.concatenate([d[0:8] for d in data], axis=1)
        lab = jnp.concatenate([d[8:16] for d in data], axis=1)
        xcat = jnp.concatenate([moved(x, dy, dx) for dy, dx in TAPS], axis=0).astype(BF16)
        z1 = contract(xcat, win[...], 0, 0)
        yield
        h1, slope1 = silu(z1)
        spread(hs, h1, 1)
        yield
        z2 = jnp.dot(hs[...], wmid[...], preferred_element_type=F32)
        yield
        h2, slope2 = silu(z2)
        h2 = h2.astype(BF16)
        parts = contract(taps, h2, 1, 1)
        yield
        y = jnp.zeros((8, size), F32)
        for t, (dy, dx) in enumerate(TAPS):
            y = y + moved(parts[8 * t : 8 * t + 8], dy, dx)
        sub = lax.broadcasted_iota(jnp.int32, (8, size), 0)
        diff = jnp.where(sub < 2, y - lab, 0.0)
        weighted = lab[2:3] * diff
        g = 2.0 * weighted
        gcat = jnp.concatenate([moved(g, -dy, -dx) for dy, dx in TAPS], axis=0).astype(BF16)
        dh2 = contract(gcat, taps, 0, 0).astype(BF16).astype(F32)
        yield
        dz2 = dh2 * slope2
        spread(ds, dz2, -1)
        yield
        dh1 = jnp.dot(ds[...], wback[...], preferred_element_type=F32).astype(BF16).astype(F32)
        yield
        dmid = contract(h1.astype(BF16), ds[...], 0, 0)
        yield
        dz1 = (dh1 * slope1).astype(BF16)
        dout = jnp.dot(gcat, h2, preferred_element_type=F32)
        din = jnp.dot(xcat, dz1, preferred_element_type=F32)
        yield weighted * diff, dmid, din, dout

    cut = pl.ds(0, size)
    teams = [work(hs.at[i, cut], ds.at[i, cut], first + group * i) for i in range(TEAMS)]
    results = []
    while len(results) < TEAMS:
        for team in teams:
            value = next(team)
            if value is not None:
                results.append(value)
    for ref, parts in zip((amis.at[:, cut], amid, ain, aout), zip(*results)):
        ref[...] += functools.reduce(jnp.add, parts)


def whole_kernel(
    rate, slot, fields, mask, gather, win, wmid, wout,
    out, misfit, first, mid, last,
    now, later, final, wet, uv, sl0, sl1, sr0, sr1, wl, wr, packed, left, right, mtop, mbot,
    sums, wide, patches, chosen, got,
    hs, ds, wback, wout8, amid, ain, aout, amis,
    grads, got1, part, got2, whole,
    in_sem, out_sem, halo_send, halo_recv, swap_send, swap_recv, *sems,
):
    my, mx = lax.axis_index("ty"), lax.axis_index("tx")
    loads = []
    for half in range(2):
        src = fields.at[:, :, pl.ds(128 * half, 128)]
        loads.append(pltpu.make_async_copy(src, now.at[half, :, pl.ds(16, 256), :], in_sem.at[half]))
        loads[-1].start()

    barrier = pltpu.get_barrier_semaphore()
    present, each, rows, sides = halo_copies(
        my, mx, fields, mask, now, packed, left, right, mtop, mbot, halo_send, halo_recv
    )
    count = jnp.int32(NTY + NTX - 2)
    for a in (-1, 0, 1):
        for b in (-1, 0, 1):
            if a or b:
                here = present(a, b)
                count = count + here.astype(jnp.int32)

                @pl.when(here)
                def _(a=a, b=b):
                    to = {"ty": my + a, "tx": mx + b}
                    pl.semaphore_signal(barrier, inc=1, device_id=to, device_id_type=MESH)

    others = [{"ty": lax.rem(my + d, NTY), "tx": mx} for d in range(1, NTY)]
    others += [{"ty": my, "tx": lax.rem(mx + d, NTX)} for d in range(1, NTX)]
    for to in others:
        pl.semaphore_signal(barrier, inc=1, device_id=to, device_id_type=MESH)

    @pl.when(my == 0)
    def _():
        now[:, :, 8:16, :] = jnp.zeros((2, 16, 8, 128), F32)
        mtop[...] = jnp.zeros_like(mtop)
        left[0:8, :] = jnp.zeros((8, 128), F32)
        right[0:8, :] = jnp.zeros((8, 128), F32)

    @pl.when(my == NTY - 1)
    def _():
        now[:, :, 272:280, :] = jnp.zeros((2, 16, 8, 128), F32)
        mbot[...] = jnp.zeros_like(mbot)
        left[264:272, :] = jnp.zeros((8, 128), F32)
        right[264:272, :] = jnp.zeros((8, 128), F32)

    @pl.when(mx == 0)
    def _():
        left[...] = jnp.zeros_like(left)

    @pl.when(mx == NTX - 1)
    def _():
        right[...] = jnp.zeros_like(right)

    for half in range(2):
        for buf in (now, later):
            buf[half, :, 0:8, :] = jnp.zeros((16, 8, 128), F32)
            buf[half, :, 280:288, :] = jnp.zeros((16, 8, 128), F32)
    for buf in (sl0, sr0, sl1, sr1):
        buf[0:8, :] = jnp.zeros((8, 128), F32)
        buf[280:288, :] = jnp.zeros((8, 128), F32)
    sums[:, 1024:2048, :] = jnp.zeros((2, 1024, 128), F32)
    for ref in (hs, ds, amid, ain, aout, amis):
        ref[...] = jnp.zeros_like(ref)
    for load in loads:
        load.wait()
    for block in range(2):
        lane = lanes((128, 128))
        at, to = pl.ds(128 * block, 128), pl.ds(16 + 128 * block, 128)
        edges = pack_edges(lambda i: (now[0, i, to, :], now[1, i, to, :]), lane)
        wet0 = mask[at, 0:128].astype(F32)
        wet1 = mask[at, 128:256].astype(F32)
        edges = jnp.where(lane == 0, pltpu.roll(wet1, 2, 1), edges)
        edges = jnp.where(lane == 8, pltpu.roll(wet1, 9, 1), edges)
        edges = jnp.where(lane == 7, pltpu.roll(wet0, 7, 1), edges)
        edges = jnp.where(lane == 15, pltpu.roll(wet0, 14, 1), edges)
        packed[to, :] = edges

    pl.semaphore_wait(barrier, count)
    start = lambda copy: copy.start()
    each(rows, start)
    each(sides, start)

    for half in range(2):
        wet[half, 16:272, :] = mask[:, 128 * half : 128 * half + 128].astype(F32)
    for t in range(9):
        at = pl.ds(128 * t, 128)
        wback[at, :] = wmid[at, :].astype(F32).T.astype(BF16)
        wout8[8 * t : 8 * t + 8, :] = jnp.zeros((8, 128), F32)
        wout8[8 * t : 8 * t + 2, :] = wout[t].astype(F32)

    velocities(uv, now, 24, 240)
    inner = tuple(range(24, 264, 16))
    lax.fori_loop(0, 8, advance(rate, wet, uv, now, later, None, None, inner, 0), 0)

    arrived = lambda copy: copy.wait_recv()
    each(rows, arrived, arriving=True)
    each(sides, arrived, arriving=True)
    for half in range(2):
        side = pl.ds(128 * half, 128)
        wet[half, 8:16, :] = mtop[:, side].astype(F32)
        wet[half, 272:280, :] = mbot[:, side].astype(F32)
    for at in (pl.ds(8, 8), pl.ds(272, 8)):
        packed[at, :] = pack_edges(lambda i: (now[0, i, at, :], now[1, i, at, :]), lanes((8, 128)))

    strips = (sl0, sl1, sr0, sr1, wl, wr)
    leaving = ocean_steps(
        rate, slot, packed, left, right, gather, out, chosen, now, later, final, wet, uv, strips, sums, wide, patches, out_sem
    )

    def swap(d):
        peer = lax.rem(my + d, NTY)
        return pltpu.make_async_remote_copy(
            src_ref=chosen.at[pl.ds(4 * peer, 4)],
            dst_ref=got.at[pl.ds(4 * d, 4)],
            send_sem=swap_send.at[d],
            recv_sem=swap_recv.at[d],
            device_id={"ty": peer, "tx": mx},
            device_id_type=MESH,
        )

    for d in range(1, NTY):
        swap(d).start()
    for j in range(4):
        got[j] = chosen[4 * my + j]

    def net(first, group):
        net_step(first, group, got, win, wmid, hs, ds, wback, wout8, amid, ain, aout, amis)

    def step(index, _):
        for i in range(1, 5):

            @pl.when(index == i)
            def _(i=i):
                for d in range(2 * i - 1, min(2 * i + 1, NTY)):
                    swap(d).wait_recv()

        ends = jnp.logical_or(index == 0, index == 4)

        @pl.when(ends)
        def _():
            net(7 * index, GROUP // 2)

        @pl.when(jnp.logical_not(ends))
        def _():
            net(8 * index - 4, GROUP)

        return 0

    lax.fori_loop(0, 5, step, 0)
    for t in range(9):
        at = pl.ds(128 * t, 128)
        grads[at, :] = amid[:, at].astype(BF16)
    both = jnp.concatenate(
        [ain[...]] + [aout[8 * t : 8 * t + 2, :] for t in range(9)] + [jnp.zeros((38, 128), F32)],
        axis=0,
    )
    grads[1152:1280, :] = both.astype(BF16)
    misfit[...] = jnp.full((1, 1), jnp.sum(amis[...]) / 8192, F32)
    pairs = tuple(zip(sems[::2], sems[1::2]))
    add_up(my, mx, grads, got1, part, got2, whole, pairs)

    def scale(start, rows):
        g = whole[start : start + rows, :]
        return lax.rsqrt(jnp.sum(g * g) / F32(rows * 128) + NORM_EPS)

    mid[...] = whole[0:1152, :] * scale(0, 1152)
    first[...] = whole[1152:1224, :] * scale(1152, 72)
    size = scale(1224, 18)
    for t in range(9):
        last[t] = whole[1224 + 2 * t : 1226 + 2 * t, :] * size

    sent = lambda copy: copy.wait_send()
    each(rows, sent)
    each(sides, sent)
    for d in range(1, NTY):
        swap(d).wait_send()
    for k in range(8):
        for half in range(2):
            leaving(k, half).wait()


def run(rate, slot, fields, mask, gather, win, wmid, wout):
    dma = pltpu.SemaphoreType.DMA
    f32 = lambda *shape: pltpu.VMEM(shape, F32)
    bf16 = lambda *shape: pltpu.VMEM(shape, BF16)
    return pl.pallas_call(
        whole_kernel,
        out_shape=(
            jax.ShapeDtypeStruct((16, 256, 256), F32),
            jax.ShapeDtypeStruct((1, 1), F32),
            jax.ShapeDtypeStruct((72, 128), F32),
            jax.ShapeDtypeStruct((1152, 128), F32),
            jax.ShapeDtypeStruct((9, 2, 128), F32),
        ),
        in_specs=[SMEM, SMEM, ANY, VMEM, VMEM, VMEM, VMEM, VMEM],
        out_specs=(ANY, VMEM, VMEM, VMEM, VMEM),
        scratch_shapes=[
            f32(2, 16, 288, 128),
            f32(2, 16, 288, 128),
            f32(2, 16, 256, 128),
            f32(2, 288, 128),
            f32(2, 4, 288, 128),
        ]
        + [f32(288, 128)] * 7
        + [
            f32(272, 128),
            f32(272, 128),
            pltpu.VMEM((8, 256), jnp.int32),
            pltpu.VMEM((8, 256), jnp.int32),
            f32(2, 2048, 128),
            bf16(384, 1024),
            bf16(32, 16, 256),
            bf16(32, 16, 256),
            bf16(32, 16, 256),
            bf16(TEAMS, GROUP * 256, 1152),
            bf16(TEAMS, GROUP * 256, 1152),
            bf16(1152, 128),
            f32(72, 128),
            f32(128, 1152),
            f32(72, 128),
            f32(72, 128),
            f32(8, GROUP * 256),
            bf16(ROWS, 128),
            bf16(NTY, CHUNK, 128),
            f32(CHUNK, 128),
            f32(NTX, PIECE, 128),
            f32(ROWS, 128),
            dma((2,)),
            dma((8, 2)),
            dma((12,)),
            dma((12,)),
        ]
        + [dma((n,)) for n in (NTY, NTY, NTY, NTY, NTX, NTX) + (NTY,) * 6],
        compiler_params=pltpu.CompilerParams(
            collective_id=0, has_side_effects=True, vmem_limit_bytes=60 << 20
        ),
        name="whole",
    )(rate, slot, fields, mask, gather, win, wmid, wout)


def per_device(fields, ocean_mask, diffusivity, patch_slot_assignment, conv_in, conv_mid, conv_out):
    current, member_loss, first, mid, last = run(
        diffusivity,
        patch_slot_assignment.reshape(32),
        fields.reshape(16, 256, 256),
        ocean_mask,
        jnp.asarray(coarse_matrix()),
        conv_in.reshape(72, 128),
        conv_mid.reshape(1152, 128),
        conv_out.reshape(9, 128, 2).transpose(0, 2, 1),
    )
    return (
        current.reshape(fields.shape),
        member_loss,
        first.reshape(conv_in.shape),
        mid.reshape(conv_mid.shape),
        last.transpose(0, 2, 1).reshape(conv_out.shape),
    )


def solution(mesh):
    placed = (P(None, None, "ty", "tx"), P("ty", "tx"), P(), P("ty", "tx", None), P(), P(), P())
    return jax.shard_map(
        per_device,
        mesh=mesh,
        in_specs=placed,
        out_specs=(P(None, None, "ty", "tx"), P("ty", "tx"), P(), P(), P()),
        check_vma=False,
    )
```
